32 devices in a mesh: row: 2 (over x), col: 16 (over z, y, core).
Axes of the slice: x: 2, y: 2, z: 4, core: 2. Of those that a mesh axis runs over, the one named last changes fastest.
Arguments:
- latent: bfloat16 [4, 32, 2048], P(None, 'row', 'col'), may hold values from -6 to 6
- cotangent: bfloat16 [4, 32, 2048], P(None, 'row', 'col'), may hold values from -6 to 6
- item_ids: int32 [16, 1024], P('row', 'col'), may hold values from 0 to 257, as said below
- positions: int32 [2, 16, 1024], P(None, 'row', 'col'), may hold values from 0 to 22, as said below
- gap_mask: int32 [16, 1024], P('row', 'col'), may hold values from 0 to 1, as said below
- timesteps: int32 [258], replicated, may hold values from 0 to 999
- labels: int32 [258], replicated, may hold values from 0 to 1000
- patch_weight: bfloat16 [16, 384], replicated, may hold values from -1.5 to 1.5
- patch_bias: bfloat16 [384], replicated, may hold values from -3 to 3
- time_weight: bfloat16 [256, 384], replicated, may hold values from -0.5 to 0.5
- time_bias: bfloat16 [384], replicated, may hold values from -3 to 3
- clock_weight: bfloat16 [384, 384], replicated, may hold values from -0.4375 to 0.4375
- clock_bias: bfloat16 [384], replicated, may hold values from -3 to 3
- class_table: bfloat16 [1001, 384], replicated, may hold values from -6 to 6
- modulation_weight: bfloat16 [384, 2304], replicated, may hold values from -0.3125 to 0.3125
- modulation_bias: bfloat16 [2304], replicated, may hold values from -3 to 3
- attention_weight: bfloat16 [384, 1152], replicated, may hold values from -0.3125 to 0.3125
- query_bias: bfloat16 [384], replicated, may hold values from -1.75 to 1.75
- value_bias: bfloat16 [384], replicated, may hold values from -1.75 to 1.75
- output_weight: bfloat16 [384, 384], replicated, may hold values from -1.25 to 1.25
- output_bias: bfloat16 [384], replicated, may hold values from -1.75 to 1.75
- hidden_weight: bfloat16 [384, 1536], replicated, may hold values from -0.3125 to 0.3125
- hidden_bias: bfloat16 [1536], replicated, may hold values from -1.75 to 1.75
- return_weight: bfloat16 [1536, 384], replicated, may hold values from -0.3125 to 0.3125
- return_bias: bfloat16 [384], replicated, may hold values from -1.75 to 1.75
- final_modulation: bfloat16 [384, 768], replicated, may hold values from -0.3125 to 0.3125
- final_offsets: bfloat16 [768], replicated, may hold values from -3 to 3
- readout_weight: bfloat16 [384, 16], replicated, may hold values from -0.3125 to 0.3125
- readout_bias: bfloat16 [16], replicated, may hold values from -1.75 to 1.75
Outputs:
- velocity: bfloat16 [4, 32, 2048], P(None, 'row', 'col')
- latent_grad: float32 [4, 32, 2048], P(None, 'row', 'col')
- patch_weight_grad: float32 [16, 384], replicated
- patch_bias_grad: float32 [384], replicated
- time_weight_grad: float32 [256, 384], replicated
- time_bias_grad: float32 [384], replicated
- clock_weight_grad: float32 [384, 384], replicated
- clock_bias_grad: float32 [384], replicated
- class_table_grad: float32 [1001, 384], replicated
- modulation_weight_grad: float32 [384, 2304], replicated
- modulation_bias_grad: float32 [2304], replicated
- attention_weight_grad: float32 [384, 1152], replicated
- query_bias_grad: float32 [384], replicated
- value_bias_grad: float32 [384], replicated
- output_weight_grad: float32 [384, 384], replicated
- output_bias_grad: float32 [384], replicated
- hidden_weight_grad: float32 [384, 1536], replicated
- hidden_bias_grad: float32 [1536], replicated
- return_weight_grad: float32 [1536, 384], replicated
- return_bias_grad: float32 [384], replicated
- final_modulation_grad: float32 [384, 768], replicated
- final_offsets_grad: float32 [768], replicated
- readout_weight_grad: float32 [384, 16], replicated
- readout_bias_grad: float32 [16], replicated
The draws below stay inside these ranges and needn't reach their ends.
Inputs may be any that keep to these rules, and one draw needn't show every extreme that they name: `item_ids`: the patch columns fall into strips of 8 to 16 consecutive columns (the rightmost may be cut by the canvas). Strips are numbered by consecutive integers from left to right, the rightmost strip having number 129 - 1; strip s is one item with id 2 s, or is cut once at a row into id 2 s above and 2 s + 1 below. The rightmost strip is always cut; at least one strip is not cut. positions[0] is the patch's row within its item and positions[1] its column within its strip, each plus an offset of 0 to 7 drawn per strip. `gap_mask`: gaps are the last 0 to 3 columns of a strip; the first column of a strip is never a gap.
All inputs are finite; a program needn't handle non-finite values.
Results may differ from the reference program's by a relative error of at most 0.023.
Values may be sent and summed in bfloat16 or wider, within the bound.
No kernel may reach another device: no remote copies, remote signals or barrier semaphores. Data moves between devices by JAX's collectives and lax.ppermute only.
A program may use at most 320 MiB of HBM per device.

```python
import math
import jax
import jax.numpy as jnp
from jax import lax

D = 384
HEADS = 6
MLP = 1536
FREQ = 256
NCLASS = 1001
CH = 4
PC = 64
STRIP_LO = 8
STRIP_HI = 16
HDIM = 64
HP = 16
WP = 1024
LH = 32
LW = 2048
NSTRIP = 129
ITEMS = 258
N_COL = 16


def canvas_layout(key):
    keys = jax.random.split(key, 7)
    forced = jax.random.randint(keys[1], (), 0, WP // STRIP_HI - 1)
    strip_index = jnp.arange(NSTRIP, dtype=jnp.int32)
    is_forced = (strip_index == forced).astype(jnp.int32)
    widths = jax.random.randint(keys[0], (NSTRIP,), STRIP_LO, STRIP_HI + 1)
    widths = jnp.where(is_forced == 1, STRIP_HI, widths)
    ends = jnp.cumsum(widths)
    starts = ends - widths
    columns = jnp.arange(WP, dtype=jnp.int32)
    strip = jnp.sum((starts[None, 1:] <= columns[:, None]).astype(jnp.int32), axis=1)
    last_strip = strip[WP - 1]
    split_flag = jax.random.randint(keys[2], (NSTRIP,), 0, 2) * (1 - is_forced)
    split_flag = jnp.where(strip_index == last_strip, 1, split_flag)
    cut_row = jax.random.randint(keys[3], (NSTRIP,), HP // 4, 3 * HP // 4 + 1)
    gap_width = jax.random.randint(keys[4], (NSTRIP,), 0, STRIP_LO // 2)
    offset_row = jnp.where(is_forced == 1, 7, jax.random.randint(keys[5], (NSTRIP,), 0, 8))
    offset_col = jnp.where(is_forced == 1, 7, jax.random.randint(keys[6], (NSTRIP,), 0, 8))
    rows = jnp.arange(HP, dtype=jnp.int32)[:, None]
    lower = ((rows >= cut_row[strip][None, :]) & (split_flag[strip][None, :] == 1)).astype(jnp.int32)
    number = strip + (NSTRIP - 1 - last_strip)
    item_ids = 2 * number[None, :] + lower
    inside = columns - starts[strip]
    real = (inside < widths[strip] - gap_width[strip]).astype(jnp.int32)
    gap_mask = jnp.broadcast_to(real[None, :], (HP, WP))
    top_row = lower * cut_row[strip][None, :]
    place_row = rows - top_row + offset_row[strip][None, :]
    place_col = jnp.broadcast_to((inside + offset_col[strip])[None, :], (HP, WP))
    positions = jnp.stack([place_row, place_col])
    return (item_ids.astype(jnp.int32), positions.astype(jnp.int32), gap_mask.astype(jnp.int32))


def draw_item_ids(key, part):
    return canvas_layout(key)[0]


def draw_positions(key, part):
    return canvas_layout(key)[1]


def draw_gap_mask(key, part):
    return canvas_layout(key)[2]


def plant(values, key, least, high):
    spot = [jax.random.randint(jax.random.fold_in(key, axis), (), 0, length) for axis, length in enumerate(values.shape)]
    main_axis = values.shape.index(max(values.shape))
    next_to = spot[:main_axis] + [(spot[main_axis] + 1) % values.shape[main_axis]] + spot[main_axis + 1:]
    return values.at[tuple(spot)].set(least).at[tuple(next_to)].set(high)


def steps_of(own_key, shape, cuts, least, high):
    loudness = 1.0
    for dim, shards_of in cuts:
        steps = jax.random.uniform(jax.random.fold_in(jax.random.fold_in(own_key, 6), dim), (shards_of,), jnp.float32, least / len(cuts), high / len(cuts))
        loudness = loudness * jnp.repeat(jnp.exp(steps), shape[dim] // shards_of).reshape((-1,) + (1,) * (len(shape) - 1 - dim))
    return loudness


def centred(stream_key, shape, scale, bound, cuts=(), kind=jnp.bfloat16):
    loudness = steps_of(stream_key, shape, cuts, -0.22, 0.18) if cuts else 1.0
    drawn = jax.random.normal(stream_key, shape, jnp.float32) * scale * loudness
    return jnp.minimum(jnp.maximum(drawn, -bound), bound).astype(kind)


def setup_inputs(seed: int = 0) -> dict:
    arg_keys = jax.random.split(jax.random.key(seed), 30)
    latent = centred(arg_keys[0], (CH, LH, LW), 1.0, 6.0, ((1, 2), (2, 16)))
    cotangent = centred(arg_keys[1], (CH, LH, LW), 1.0, 6.0, ((1, 2), (2, 16)))
    item_ids = draw_item_ids(jax.random.fold_in(arg_keys[29], 71), 0)
    positions = draw_positions(jax.random.fold_in(arg_keys[29], 71), 0)
    gap_mask = draw_gap_mask(jax.random.fold_in(arg_keys[29], 71), 0)
    timesteps = plant(jax.random.randint(arg_keys[5], (ITEMS,), 0, 1000), jax.random.fold_in(arg_keys[5], 1), 0, 999).astype(jnp.int32)
    labels = plant(jax.random.randint(arg_keys[6], (ITEMS,), 0, NCLASS), jax.random.fold_in(arg_keys[6], 1), 0, NCLASS - 1).astype(jnp.int32)
    patch_weight = centred(arg_keys[7], (4 * CH, D), (4 * CH) ** -0.5, 1.5)
    patch_bias = centred(arg_keys[8], (D,), 0.5, 3.0)
    time_weight = centred(arg_keys[9], (FREQ, D), (FREQ // 2) ** -0.5, 0.5)
    time_bias = centred(arg_keys[10], (D,), 0.5, 3.0)
    clock_weight = centred(arg_keys[11], (D, D), (D // 2) ** -0.5, 0.4375)
    clock_bias = centred(arg_keys[12], (D,), 0.5, 3.0)
    class_table = centred(arg_keys[13], (NCLASS, D), 1.0, 6.0)
    modulation_weight = centred(arg_keys[14], (D, 6 * D), D ** -0.5, 0.3125)
    modulation_bias = centred(arg_keys[15], (6 * D,), 0.5, 3.0)
    attention_weight = centred(arg_keys[16], (D, 3 * D), D ** -0.5, 0.3125)
    query_bias = centred(arg_keys[17], (D,), 0.3, 1.75)
    value_bias = centred(arg_keys[18], (D,), 0.3, 1.75)
    output_weight = centred(arg_keys[19], (D, D), (D // 16) ** -0.5, 1.25)
    output_bias = centred(arg_keys[20], (D,), 0.3, 1.75)
    hidden_weight = centred(arg_keys[21], (D, MLP), D ** -0.5, 0.3125)
    hidden_bias = centred(arg_keys[22], (MLP,), 0.3, 1.75)
    return_weight = centred(arg_keys[23], (MLP, D), (MLP // 4) ** -0.5, 0.3125)
    return_bias = centred(arg_keys[24], (D,), 0.3, 1.75)
    final_modulation = centred(arg_keys[25], (D, 2 * D), D ** -0.5, 0.3125)
    final_offsets = centred(arg_keys[26], (2 * D,), 0.5, 3.0)
    readout_weight = centred(arg_keys[27], (D, 4 * CH), D ** -0.5, 0.3125)
    readout_bias = centred(arg_keys[28], (4 * CH,), 0.3, 1.75)
    return dict(latent=latent, cotangent=cotangent, item_ids=item_ids, positions=positions, gap_mask=gap_mask, timesteps=timesteps, labels=labels, patch_weight=patch_weight, patch_bias=patch_bias, time_weight=time_weight, time_bias=time_bias, clock_weight=clock_weight, clock_bias=clock_bias, class_table=class_table, modulation_weight=modulation_weight, modulation_bias=modulation_bias, attention_weight=attention_weight, query_bias=query_bias, value_bias=value_bias, output_weight=output_weight, output_bias=output_bias, hidden_weight=hidden_weight, hidden_bias=hidden_bias, return_weight=return_weight, return_bias=return_bias, final_modulation=final_modulation, final_offsets=final_offsets, readout_weight=readout_weight, readout_bias=readout_bias)


@jax.custom_vjp
def low(v):
    return lax.optimization_barrier(v.astype(jnp.bfloat16)).astype(jnp.float32)

@jax.custom_vjp
def low_back(v):
    return v

def low_keep(v):
    return (low(v), None)

def low_pass(kept, grad):
    return (grad,)

def back_keep(v):
    return (v, None)

def back_low(kept, grad):
    return (low(grad),)
low.defvjp(low_keep, low_pass)
low_back.defvjp(back_keep, back_low)

def matmul_high(operand, weights):
    return jnp.dot(operand, weights, precision=lax.Precision.HIGHEST)

def layer_norm(values):
    center = values - lax.optimization_barrier(jnp.mean(values, axis=-1, keepdims=True))
    spread = lax.optimization_barrier(jnp.mean(center * center, axis=-1, keepdims=True))
    return center * lax.rsqrt(spread + 1e-06)

def time_features(step_values, feature_count):
    half_count = feature_count // 2
    frequencies = jnp.exp(-math.log(10000.0) * jnp.arange(half_count, dtype=jnp.float32) / half_count)
    angles = step_values.astype(jnp.float32)[..., None] * frequencies
    return jnp.concatenate([jnp.cos(angles), jnp.sin(angles)], axis=-1)

def place_features(row_place, col_place, model_width):
    quarter = model_width // 4
    omegas = jnp.exp(-math.log(10000.0) * jnp.arange(quarter, dtype=jnp.float32) / quarter)
    pieces = []
    for coordinate in (row_place, col_place):
        angles = coordinate.astype(jnp.float32)[..., None] * omegas
        pieces.append(jnp.sin(angles))
        pieces.append(jnp.cos(angles))
    return jnp.concatenate(pieces, axis=-1)

def attention(projected, item_ids, gap_mask):
    query_tags = item_ids + 1
    key_tags = jnp.where(gap_mask == 1, item_ids + 1, 0)
    window = PC + 2 * STRIP_HI
    key_side = jnp.pad(projected[:, :, D:], ((0, 0), (STRIP_HI, STRIP_HI), (0, 0)))
    tag_side = jnp.pad(key_tags, ((0, 0), (STRIP_HI, STRIP_HI)))
    score_scale = 1.0 / math.sqrt(HDIM)

    def one_tile(tile_index):
        start_col = (tile_index * PC).astype(jnp.int32)
        queries = lax.dynamic_slice_in_dim(projected[:, :, :D], start_col, PC, 1).reshape(HP * PC, D)
        keyvals = lax.dynamic_slice_in_dim(key_side, start_col, window, 1).reshape(HP * window, 2 * D)
        tags_query = lax.dynamic_slice_in_dim(query_tags, start_col, PC, 1).reshape(HP * PC)
        tags_key = lax.dynamic_slice_in_dim(tag_side, start_col, window, 1).reshape(HP * window)
        allowed = tags_query[:, None] == tags_key[None, :]
        results = []
        for head_index in range(HEADS):
            head_start = head_index * HDIM
            query_head = queries[:, head_start:head_start + HDIM]
            key_head = keyvals[:, head_start:head_start + HDIM]
            value_head = keyvals[:, D + head_start:D + head_start + HDIM]
            scores = low_back(matmul_high(query_head, key_head.T)) * score_scale
            scores = jnp.where(allowed, scores, -1e+30)
            row_max = lax.optimization_barrier(jnp.max(scores, axis=-1, keepdims=True))
            exponent = jnp.exp(scores - row_max)
            probabilities = exponent / lax.optimization_barrier(jnp.sum(exponent, axis=-1, keepdims=True))
            results.append(matmul_high(low(probabilities), value_head))
        return jnp.concatenate(results, axis=-1)
    tile_out = lax.map(jax.checkpoint(one_tile), jnp.arange(N_COL, dtype=jnp.int32))
    return tile_out.reshape(N_COL, HP, PC, D).transpose(1, 0, 2, 3).reshape(HP, WP, D)

def reference(latent, cotangent, item_ids, positions, gap_mask, timesteps, labels, patch_weight, patch_bias, time_weight, time_bias, clock_weight, clock_bias, class_table, modulation_weight, modulation_bias, attention_weight, query_bias, value_bias, output_weight, output_bias, hidden_weight, hidden_bias, return_weight, return_bias, final_modulation, final_offsets, readout_weight, readout_bias):
    weight_list = [w_item.astype(jnp.float32) for w_item in (patch_weight, patch_bias, time_weight, time_bias, clock_weight, clock_bias, class_table, modulation_weight, modulation_bias, attention_weight, query_bias, value_bias, output_weight, output_bias, hidden_weight, hidden_bias, return_weight, return_bias, final_modulation, final_offsets, readout_weight, readout_bias)]
    mask_float = gap_mask.astype(jnp.float32)[..., None]
    place = place_features(positions[0], positions[1], D)

    def forward(latent_f, p_weight, p_bias, t_weight, t_bias, c_weight, c_bias, table, m_weight, m_bias, a_weight, q_bias, v_bias, o_weight, o_bias, h_weight, h_bias, r_weight, r_bias, f_weight, f_bias, out_weight, out_bias):
        extended = jnp.pad(latent_f, ((0, 0), (0, 1), (0, 1)))[:, 1:, 1:]
        patches = extended.reshape(CH, HP, 2, WP, 2).transpose(1, 3, 2, 4, 0).reshape(HP, WP, 4 * CH)
        time_feat = low(time_features(timesteps, FREQ))
        time_pre = matmul_high(time_feat, t_weight) + t_bias
        time_hidden = low(jax.nn.silu(time_pre))
        condition = matmul_high(time_hidden, c_weight) + c_bias + table[labels]
        cond_act = low(jax.nn.silu(condition))
        modulation = matmul_high(cond_act, m_weight) + m_bias
        closing = matmul_high(cond_act, f_weight) + f_bias
        shift_a, scale_a, gate_a, shift_m, scale_m, gate_m = jnp.split(modulation[item_ids], 6, axis=-1)
        shift_f, scale_f = jnp.split(closing[item_ids], 2, axis=-1)
        residual_in = matmul_high(patches, p_weight) + p_bias + place
        attn_in = low(layer_norm(residual_in) * (1.0 + scale_a) + shift_a)
        qkv_bias = jnp.concatenate([q_bias, jnp.zeros_like(q_bias), v_bias])
        qkv = low(low_back(matmul_high(attn_in, a_weight) + qkv_bias))
        attended = low(low_back(attention(qkv, item_ids, gap_mask)))
        branch_a = low_back(matmul_high(attended, o_weight) + o_bias)
        residual_mid = residual_in + gate_a * branch_a
        mlp_in = low(layer_norm(residual_mid) * (1.0 + scale_m) + shift_m)
        hidden_pre = low_back(matmul_high(mlp_in, h_weight) + h_bias)
        hidden_act = low(jax.nn.gelu(hidden_pre, approximate=True))
        branch_m = low_back(matmul_high(hidden_act, r_weight) + r_bias)
        residual_out = residual_mid + gate_m * branch_m
        readout_in = low(layer_norm(residual_out) * (1.0 + scale_f) + shift_f)
        token_velocity = low_back(matmul_high(readout_in, out_weight) + out_bias) * mask_float
        grid = token_velocity.reshape(HP, WP, 2, 2, CH).transpose(4, 0, 2, 1, 3).reshape(CH, 2 * HP, 2 * WP)
        return jnp.pad(grid, ((0, 0), (1, 0), (1, 0)))[:, :2 * HP, :2 * WP]
    velocity_f, pull_back = jax.vjp(forward, latent.astype(jnp.float32), *weight_list)
    grads = pull_back(cotangent.astype(jnp.float32))
    return (velocity_f.astype(jnp.bfloat16), grads[0], grads[1], grads[2], grads[3], grads[4], grads[5], grads[6], grads[7], grads[8], grads[9], grads[10], grads[11], grads[12], grads[13], grads[14], grads[15], grads[16], grads[17], grads[18], grads[19], grads[20], grads[21], grads[22])
```

```python
import functools
import math

import jax
import jax.numpy as jnp
from jax import lax
from jax.experimental import pallas as pl
from jax.experimental.pallas import tpu as pltpu
from jax.sharding import PartitionSpec as P

HEADS = 6
HALO = 16
LEAST = 8
BLOCK = 256
LEFT = 16
RIGHT = 32
POSITIONS = 128
F32 = jnp.float32
BF16 = jnp.bfloat16
VMEM_BYTES = 60 * 1024 * 1024


def iota(shape, dim):
    return lax.broadcasted_iota(jnp.int32, shape, dim)


def mm(a, b):
    return jnp.dot(a, b, preferred_element_type=F32)


def mm_t(a, b):
    return lax.dot_general(a, b, (((1,), (1,)), ((), ())), preferred_element_type=F32)


def t_mm(a, b):
    return lax.dot_general(a, b, (((0,), (0,)), ((), ())), preferred_element_type=F32)


def low(v):
    return v.astype(BF16)


def one(cond):
    return jnp.where(cond, 1.0, 0.0).astype(BF16)


def sigmoid(v):
    return 1.0 / (1.0 + jnp.exp(-v))


def layer_norm(v):
    center = v - jnp.mean(v, axis=-1, keepdims=True)
    inverse = lax.rsqrt(jnp.mean(center * center, axis=-1, keepdims=True) + 1e-06)
    return center * inverse, inverse


def norm_back(normed, inverse, grad):
    mean_grad = jnp.mean(grad, axis=-1, keepdims=True)
    mean_cross = jnp.mean(grad * normed, axis=-1, keepdims=True)
    return inverse * (grad - mean_grad - normed * mean_cross)


def call(body, outs, ins, scratch=()):
    spec = pl.BlockSpec(memory_space=pltpu.VMEM)
    return pl.pallas_call(
        body,
        out_shape=[jax.ShapeDtypeStruct(shape, dtype) for shape, dtype in outs],
        in_specs=[spec] * len(ins),
        out_specs=[spec] * len(outs),
        scratch_shapes=[pltpu.VMEM(shape, dtype) for shape, dtype in scratch],
        compiler_params=pltpu.CompilerParams(vmem_limit_bytes=VMEM_BYTES),
    )(*ins)


def lane_fold(rows):
    lane = iota((rows, 128), 1)
    feature = 8 * (1 - (lane & 1)) + 4 * (1 - (lane >> 6)) + ((lane >> 4) & 3)
    return one(iota((rows, 128), 0) == feature)


def tile_kernel(lat_ref, cot_ref, ids_ref, pos_ref, gap_ref, tile_ref, first_ref, last_ref):
    cols = ids_ref.shape[1]
    pieces = []
    for ref in (lat_ref, cot_ref):
        flat = ref[...].reshape(64, 2 * cols)
        for side in (0, 1):
            pick = one(iota((cols, 2 * cols), 1) == 2 * iota((cols, 2 * cols), 0) + side)
            pieces.append(mm_t(pick, flat))
    tag = ids_ref[...] + 1
    meta = jnp.concatenate(
        [tag >> 8, tag & 255, pos_ref[0], pos_ref[1], gap_ref[...], jnp.zeros((88, cols), jnp.int32)], axis=0
    ).astype(F32)
    pieces.append(mm_t(one(iota((cols, cols), 0) == iota((cols, cols), 1)), low(meta)))
    tile = low(jnp.concatenate(pieces, axis=1))
    tile_ref[...] = tile
    first_ref[...] = tile[:RIGHT]
    last_ref[...] = tile[cols - LEFT :]


def item_kernel(tl_ref, tw_ref, cw_ref, ct_ref, bias_ref, feat_ref, pre_ref, cond_ref, act_ref, table_ref):
    items = tl_ref.shape[1]
    half = tw_ref.shape[0] // 2
    steps = tl_ref[0:1, :].astype(F32)
    freq = jnp.exp(iota((half, 1), 0).astype(F32) * (-math.log(10000.0) / half))
    angle = freq * steps
    feat_ref[0:half, :] = low(jnp.cos(angle))
    feat_ref[half:, :] = low(jnp.sin(angle))
    pre = t_mm(feat_ref[...], tw_ref[...]) + bias_ref[1:2, :]
    pre_ref[...] = pre
    hidden = low(pre * sigmoid(pre))
    classes = ct_ref.shape[0]
    pick = one(iota((classes, items), 0) == tl_ref[1:2, :])
    cond = mm(hidden, cw_ref[...]) + bias_ref[2:3, :] + t_mm(pick, ct_ref[...])
    cond_ref[...] = cond
    act_ref[...] = low(cond * sigmoid(cond))
    width = table_ref.shape[1]
    quarter = width // 4
    shape = (2 * POSITIONS, width)
    lane = iota(shape, 1)
    row = iota(shape, 0)
    second = lane >= 2 * quarter
    within = jnp.where(second, lane - 2 * quarter, lane)
    cosine = within >= quarter
    index = jnp.where(cosine, within - quarter, within)
    omega = jnp.exp(index.astype(F32) * (-math.log(10000.0) / quarter))
    angle = (row & (POSITIONS - 1)).astype(F32) * omega
    value = jnp.where(cosine, jnp.cos(angle), jnp.sin(angle))
    value = jnp.where(jnp.where(second, 1, 0) == jnp.where(row >= POSITIONS, 1, 0), value, 0.0)
    high = low(value)
    table_ref[0 : 2 * POSITIONS, :] = high
    table_ref[2 * POSITIONS :, :] = low(value - high.astype(F32))


def row_mask(q, i, shape):
    return ((q * 16 + (iota(shape, 1) & 15) - 1) >> 1) == i


def main_kernel(dims, *refs):
    n_rows, hp, cw, tokens, ni, half_rows = dims
    own_ref, left_ref = refs[0:2]
    tiles = refs[2 : 1 + n_rows]
    rights = refs[1 + n_rows : 1 + 2 * n_rows]
    (act_ref, table_ref, bias_ref, pw_ref, mw_ref, fw_ref, aw_ref, ow_ref, hw_ref, rw_ref, low_ref,
     q_ref, k_ref, v_ref, da_ref, rows_ref, aux_ref, res_ref, mid_ref, in_ref, x_ref, mem_ref, ms_ref, vel_ref,
     dmod_ref, keep_ref, send_ref,
     es, ct_s, at_s, mlp_s, ha_s, dh_s, dbm_s, dba_s, ri_s, gd_s, dacc, small, g_s) = refs[1 + 2 * n_rows :]
    width = res_ref.shape[1]
    pairs = width // 128
    r = lax.axis_index("row")
    core = lax.axis_index("col") & 1
    shift = int(math.log2(hp))

    es[...] = jnp.zeros_like(es)
    es[r, LEFT : LEFT + 64, :] = own_ref[...]
    es[r, 0:LEFT, :] = left_ref[...]
    for k in range(1, n_rows):
        es[lax.rem(r - k + n_rows, n_rows), LEFT : LEFT + 64, :] = tiles[k - 1][...]
    for k in range(n_rows):
        es[lax.rem(r - k + n_rows, n_rows), LEFT + 64 :, :] = rights[k][...]
    meta = es[r, :, 256:384].astype(F32)
    lane = iota(meta.shape, 1)
    weighted = meta * jnp.where(lane == 0, 256.0, jnp.where(lane == 8, 1.0, 0.0))
    line = iota(meta.shape, 0)
    start = LEFT + r * cw
    tag_prev = jnp.sum(jnp.where(line == start - 1, weighted, 0.0)).astype(jnp.int32)
    tag_last = jnp.sum(jnp.where(line == start + cw - 1, weighted, 0.0)).astype(jnp.int32)
    tag_first = jnp.sum(jnp.where(line == start, weighted, 0.0)).astype(jnp.int32)
    strip_prev = jnp.where(tag_prev == 0, ((tag_first - 1) >> 1) - 1, (tag_prev - 1) >> 1)
    strip_last = (tag_last - 1) >> 1
    base = 2 * (strip_prev + 1)

    pick = one(iota((16, act_ref.shape[0]), 1) == base + iota((16, act_ref.shape[0]), 0))
    own_act = low(mm(pick, act_ref[...]))
    ms_ref[48:, :] = jnp.zeros_like(ms_ref[48:, :])
    for b in range(8):
        cols = slice(b * width, (b + 1) * width)
        if b < 6:
            value = mm(own_act, mw_ref[:, cols]) + bias_ref[3 + b : 4 + b, :]
        else:
            value = mm(own_act, fw_ref[:, (b - 6) * width : (b - 5) * width]) + bias_ref[11 + b : 12 + b, :]
        p0 = low(value)
        rest = value - p0.astype(F32)
        p1 = low(rest)
        ms_ref[0:16, cols] = p0
        ms_ref[16:32, cols] = p1
        ms_ref[32:48, cols] = low(rest - p1.astype(F32))

    def mod(mem, b, n=1):
        return mm(mem, ms_ref[:, b * width : (b + n) * width])

    fold = lane_fold(16)
    embed = low(t_mm(fold, pw_ref[...]))
    unread = low(mm(low_ref[...], fold))
    b_lanes = iota((BLOCK, 128), 1)
    is_b1 = b_lanes >= 64
    half_lanes = (one(b_lanes < 64), one(is_b1))

    def first(tb, carry):
        t0 = pl.multiple_of(tb * BLOCK, BLOCK)
        rows = pl.ds(t0, BLOCK)
        token = t0 + iota((BLOCK, 1), 0)
        j = token >> shift
        i = token & (hp - 1)
        spot = iota((BLOCK, LEFT + 64 + RIGHT), 1)
        rep0 = one(spot == start + j)
        rep1 = one(spot == start + j + 1)
        x = jnp.zeros((BLOCK, 128), F32)
        c = jnp.zeros((BLOCK, 128), F32)
        m = jnp.zeros((BLOCK, 128), F32)
        for q in range(n_rows):
            here = mm(rep0, es[q])
            beside = mm(rep1, es[q, :, 0:256])
            mask = row_mask(q, i, (BLOCK, 128))
            x = x + jnp.where(mask, jnp.where(is_b1, here[:, 0:128], beside[:, 0:128]), 0.0)
            c = c + jnp.where(mask, jnp.where(is_b1, here[:, 128:256], beside[:, 128:256]), 0.0)
            m = m + jnp.where((q * 8 + (b_lanes & 7)) == i, here[:, 256:384], 0.0)
        x = low(x)
        m = low(m)
        x_ref[rows, :] = x
        ml = iota((128, 128), 0)
        mc = iota((128, 128), 1)
        kind = ml >> 3
        gather = jnp.where(
            (mc == 0) & (kind == 0), 256.0,
            jnp.where(((mc == 0) & (kind == 1)) | ((mc >= 1) & (mc <= 3) & (kind == mc + 1)), 1.0, 0.0),
        ).astype(BF16)
        cols = mm(m, gather)
        rl = iota((8, 128), 1) >> 3
        rr = iota((8, 128), 0)
        row_pick = jnp.where((rr == 6) & (rl == 0), 256.0, jnp.where((rr == 6) & (rl == 1), 1.0, 0.0)).astype(BF16)
        rows_ref[:, rows] = mm_t(row_pick, m) + jnp.where(iota((8, BLOCK), 0) == 7, base.astype(F32), 0.0)
        tag = cols[:, 0:1]
        gap = cols[:, 3:4]
        tag_i = tag.astype(jnp.int32)
        strip = (tag_i - 1) >> 1
        owned = (strip > strip_prev) & (strip <= strip_last)
        act = jnp.where(owned, gap, 0.0)
        aux_ref[rows, :] = jnp.where(b_lanes == 0, tag * gap, jnp.where(b_lanes == 1, act, 0.0))
        item = tag_i - 1 - base
        mem = one((item == (b_lanes & 15)) & (b_lanes < 48) & owned)
        mem_ref[rows, :] = mem
        ct_s[rows, :] = low(c * act)
        p0 = cols[:, 1:2].astype(jnp.int32)
        p1 = cols[:, 2:3].astype(jnp.int32) + POSITIONS
        spot = iota((BLOCK, 2 * POSITIONS), 1)
        place = one((spot == p0) | (spot == p1))
        res = (
            mm(x, embed) + bias_ref[0:1, :]
            + (mm(place, table_ref[0 : 2 * POSITIONS, :]) + mm(place, table_ref[2 * POSITIONS :, :]))
        )
        res_ref[rows, :] = res
        normed, _ = layer_norm(res)
        ab = mod(mem, 0, 2)
        attn_in = low(normed * (1.0 + ab[:, width:]) + ab[:, :width])
        in_ref[rows, :] = attn_in
        for part, ref in enumerate((q_ref, k_ref, v_ref)):
            value = mm(attn_in, aw_ref[:, part * width : (part + 1) * width])
            if part != 1:
                value = value + bias_ref[9 + part // 2 : 10 + part // 2, :]
            value = low(value)
            if part == 0:
                value = value * BF16(1.0 / math.sqrt(width // HEADS))
            for p in range(pairs):
                ref[p, rows, :] = value[:, p * 128 : (p + 1) * 128]
        return carry

    lax.fori_loop(0, tokens // BLOCK, first, 0)

    for qb in range(tokens // BLOCK):
        qs = slice(qb * BLOCK, (qb + 1) * BLOCK)
        ks = key_range(qb, hp, tokens)
        q_tag = rows_ref[6:7, qs]
        k_tag = aux_ref[ks, 0:1]
        allowed = k_tag == q_tag
        for p in range(pairs):
            query = q_ref[p, qs, :]
            key = k_ref[p, ks, :]
            value = v_ref[p, ks, :]
            halves = []
            for e in range(2):
                scores = jnp.where(allowed, mm_t(key, query * half_lanes[e]), -1e30)
                top = jnp.max(scores, axis=0, keepdims=True)
                expo = jnp.exp(scores - top)
                total = jnp.sum(expo, axis=0, keepdims=True)
                rows_ref[2 * p + e : 2 * p + e + 1, qs] = top + jnp.log(total)
                halves.append(t_mm(low(expo * (1.0 / total)), value))
            at_s[p, qs, :] = low(jnp.where(is_b1, halves[1], halves[0]))

    dacc[...] = jnp.zeros_like(dacc)

    def second(tb, carry):
        t0 = pl.multiple_of(tb * BLOCK, BLOCK)
        rows = pl.ds(t0, BLOCK)
        mem = mem_ref[rows, :]

        def item_sum(b, grad):
            dacc[:, b * width : (b + 1) * width] += t_mm(mem, low(grad))[0:16, :]

        attended = jnp.concatenate([at_s[p, rows, :] for p in range(pairs)], axis=1)
        branch_a = mm(attended, ow_ref[...]) + bias_ref[11:12, :]
        gate_a = mod(mem, 2)
        mid = res_ref[rows, :] + gate_a * branch_a
        norm_mid, inv_mid = layer_norm(mid)
        scale_m = 1.0 + mod(mem, 4)
        mlp_in = low(norm_mid * scale_m + mod(mem, 3))
        mlp_s[rows, :] = mlp_in
        hidden = hw_ref.shape[1]
        branch_m = jnp.zeros((BLOCK, width), F32)
        for n in range(hidden // width):
            part = slice(n * width, (n + 1) * width)
            pre = mm(mlp_in, hw_ref[:, part]) + bias_ref[12 + n : 13 + n, :]
            square = pre * pre
            c0 = math.sqrt(2.0 / math.pi)
            t = jnp.tanh(pre * (c0 + (c0 * 0.044715) * square))
            up = 0.5 + 0.5 * t
            act = low(pre * up)
            gd_s[:, part] = up + (0.5 * pre) * (1.0 - t * t) * (c0 + (3.0 * c0 * 0.044715) * square)
            ha_s[rows, part] = act
            branch_m = branch_m + mm(act, rw_ref[part, :])
        branch_m = branch_m + bias_ref[16:17, :]
        gate_m = mod(mem, 5)
        norm_out, inv_out = layer_norm(mid + gate_m * branch_m)
        scale_f = 1.0 + mod(mem, 7)
        readout_in = low(norm_out * scale_f + mod(mem, 6))
        ri_s[rows, :] = readout_in
        active = aux_ref[rows, 1:2]
        bias_lanes = mm(low(bias_ref[19:20, 0:16] + jnp.zeros((8, 16), F32)), fold)[0:1, :]
        vel_ref[rows, :] = low((mm(readout_in, unread) + bias_lanes) * active)
        d_read = mm_t(ct_s[rows, :], unread)
        item_sum(6, d_read)
        item_sum(7, d_read * norm_out)
        d_out = norm_back(norm_out, inv_out, d_read * scale_f)
        item_sum(5, d_out * branch_m)
        d_bm = low(d_out * gate_m)
        dbm_s[rows, :] = d_bm
        d_mlp = jnp.zeros((BLOCK, width), F32)
        for n in range(hidden // width):
            part = slice(n * width, (n + 1) * width)
            d_hid = low(mm_t(d_bm, rw_ref[part, :]) * gd_s[:, part])
            dh_s[rows, part] = d_hid
            d_mlp = d_mlp + mm_t(d_hid, hw_ref[:, part])
        item_sum(3, d_mlp)
        item_sum(4, d_mlp * norm_mid)
        d_mid = d_out + norm_back(norm_mid, inv_mid, d_mlp * scale_m)
        mid_ref[rows, :] = d_mid
        item_sum(2, d_mid * branch_a)
        d_ba = low(d_mid * gate_a)
        dba_s[rows, :] = d_ba
        d_at = low(mm_t(d_ba, ow_ref[...]))
        for p in range(pairs):
            da_ref[p, rows, :] = d_at[:, p * 128 : (p + 1) * 128]
        return carry

    lax.fori_loop(0, tokens // BLOCK, second, 0)
    dmod_ref[...] = dacc[...]

    g_s[...] = jnp.zeros_like(g_s)
    put = functools.partial(put_rows, g_s, half_rows)
    n_hidden = hw_ref.shape[1] // width
    for n in range(n_hidden):
        part = slice(n * width, (n + 1) * width)
        put(n * width, low(t_mm(ha_s[:, part], dbm_s[...])))
        put((n_hidden + n) * width, low(t_mm(mlp_s[...], dh_s[:, part])))
    attended = jnp.concatenate([at_s[p] for p in range(pairs)], axis=1)
    put(2 * n_hidden * width, low(t_mm(attended, dba_s[...])))
    ones = jnp.ones((8, tokens), BF16)
    small[...] = jnp.zeros_like(small)
    small[0:16, :] = mm(fold, low(t_mm(ct_s[...], ri_s[...])))
    small[16:17, :] = mm(ones, dbm_s[...])[0:1, :]
    for n in range(n_hidden):
        small[17 + n : 18 + n, :] = mm(ones, dh_s[:, n * width : (n + 1) * width])[0:1, :]
    small[21:22, :] = mm(ones, dba_s[...])[0:1, :]
    sums = mm(ones, ct_s[...])
    small[22:23, 0:128] = mm_t(jnp.broadcast_to(low(sums[0:1, :]), (8, 128)), lane_fold(128))[0:1, :]
    put((2 * n_hidden + 1) * width, low(small[...]))
    keep_ref[...] = g_s[core]
    send_ref[...] = g_s[1 - core]


def put_rows(g_s, half_rows, row, value):
    count = value.shape[0]
    done = 0
    while done < count:
        side, at = divmod(row + done, half_rows)
        take = min(count - done, half_rows - at)
        g_s[side, at : at + take, :] = value[done : done + take, :]
        done += take


def key_range(qb, hp, tokens):
    first_col = (qb * BLOCK) // hp
    last_col = ((qb + 1) * BLOCK - 1) // hp
    return slice(max(0, first_col - HALO) * hp, min(tokens, (last_col + 1 + HALO) * hp))


def back_kernel(dims, *refs):
    n_rows, hp, cw, tokens, ni, half_rows = dims
    (q_ref, k_ref, v_ref, da_ref, rows_ref, aux_ref, res_ref, mid_ref, in_ref, x_ref, mem_ref, ms_ref, vel_ref,
     dmod_ref, aw_ref, pw_ref) = refs[0:16]
    keep_ref, send_ref, item_ref = refs[16:19]
    mine_refs = refs[19 : 19 + n_rows]
    over_refs = refs[19 + n_rows : 19 + 2 * n_rows]
    dq_s, dk_s, dv_s, dx_s, di_s, dacc, frame, small, g_s = refs[19 + 2 * n_rows :]
    width = res_ref.shape[1]
    pairs = width // 128
    r = lax.axis_index("row")
    col = lax.axis_index("col")
    core = col & 1
    shift = int(math.log2(hp))
    b_lanes = iota((BLOCK, 128), 1)
    is_b1 = b_lanes >= 64
    half_lanes = (one(b_lanes < 64), one(is_b1))
    scale = 1.0 / math.sqrt(width // HEADS)

    dk_s[...] = jnp.zeros_like(dk_s)
    dv_s[...] = jnp.zeros_like(dv_s)
    for qb in range(tokens // BLOCK):
        qs = slice(qb * BLOCK, (qb + 1) * BLOCK)
        ks = key_range(qb, hp, tokens)
        allowed = aux_ref[ks, 0:1] == rows_ref[6:7, qs]
        for p in range(pairs):
            query = q_ref[p, qs, :]
            key = k_ref[p, ks, :]
            value = v_ref[p, ks, :]
            d_at = da_ref[p, qs, :]
            d_key = 0.0
            d_value = 0.0
            halves = []
            for e in range(2):
                q_half = query * half_lanes[e]
                d_half = d_at * half_lanes[e]
                scores = jnp.where(allowed, mm_t(key, q_half), -1e30)
                probs = jnp.exp(scores - rows_ref[2 * p + e : 2 * p + e + 1, qs])
                d_probs = mm_t(value, d_half)
                inner = jnp.sum(probs * d_probs, axis=0, keepdims=True)
                d_scores = low(probs * (d_probs - inner))
                d_value = d_value + mm(low(probs), d_half)
                d_key = d_key + mm(d_scores, q_half)
                halves.append(t_mm(d_scores, key))
            dk_s[p, ks, :] += d_key
            dv_s[p, ks, :] += d_value
            dq_s[p, qs, :] = low(jnp.where(is_b1, halves[1], halves[0]) * scale)

    embed = low(t_mm(lane_fold(16), pw_ref[...]))
    dacc[...] = jnp.zeros_like(dacc)
    frame[...] = jnp.zeros_like(frame)

    def third(tb, carry):
        t0 = pl.multiple_of(tb * BLOCK, BLOCK)
        rows = pl.ds(t0, BLOCK)
        mem = mem_ref[rows, :]
        for p in range(pairs):
            dx_s[rows, p * 128 : (p + 1) * 128] = dq_s[p, rows, :]
            dx_s[rows, width + p * 128 : width + (p + 1) * 128] = low(dk_s[p, rows, :])
            dx_s[rows, 2 * width + p * 128 : 2 * width + (p + 1) * 128] = low(dv_s[p, rows, :])
        d_attn = mm_t(dx_s[rows, :], aw_ref[...])
        normed, inverse = layer_norm(res_ref[rows, :])
        scale_a = 1.0 + mm(mem, ms_ref[:, width : 2 * width])
        dacc[:, 0:width] += t_mm(mem, low(d_attn))[0:16, :]
        dacc[:, width : 2 * width] += t_mm(mem, low(d_attn * normed))[0:16, :]
        d_in = low(mid_ref[rows, :] + norm_back(normed, inverse, d_attn * scale_a))
        di_s[rows, :] = d_in
        grad = low(mm_t(d_in, embed))
        both = jnp.concatenate([vel_ref[rows, :], grad], axis=1)
        token = t0 + iota((BLOCK, 1), 0)
        j = token >> shift
        i = token & (hp - 1)
        spot = iota((BLOCK, 64 + RIGHT), 1)
        rep = jnp.concatenate([one(spot == r * cw + j), one(spot == r * cw + j + 1)], axis=0)
        side = (iota((BLOCK, 256), 1) >> 6) & 1
        for q in range(n_rows):
            mask = row_mask(q, i, (BLOCK, 256))
            split = jnp.concatenate([both * one(mask & (side == 1)), both * one(mask & (side == 0))], axis=0)
            frame[q] += t_mm(rep, split)
        return carry

    lax.fori_loop(0, tokens // BLOCK, third, 0)

    g_s[...] = jnp.zeros_like(g_s)
    put = functools.partial(put_rows, g_s, half_rows)
    for n in range(3):
        put(n * width, low(t_mm(in_ref[...], dx_s[:, n * width : (n + 1) * width])))
    ones = jnp.ones((8, tokens), BF16)
    small[...] = jnp.zeros_like(small)
    small[0:16, :] = mm(lane_fold(16), low(t_mm(x_ref[...], di_s[...])))
    small[16:17, :] = mm(ones, di_s[...])[0:1, :]
    small[17:18, :] = mm(ones, dx_s[:, 0:width])[0:1, :]
    small[18:19, :] = mm(ones, dx_s[:, 2 * width :])[0:1, :]
    put(3 * width, low(small[...]))
    keep_ref[...] = g_s[core]
    send_ref[...] = g_s[1 - core]

    rows = [dacc[0:ni, 0:width], dacc[0:ni, width : 2 * width]]
    rows += [dmod_ref[0:ni, b * width : (b + 1) * width] for b in range(2, 8)]
    spot = ((core * 2 * n_rows + plane_spot()) * (lax.axis_size("col") // 4) + line_spot()) * ni
    index = iota((8, width), 0) * width + iota((8, width), 1) - spot
    base = rows_ref[7:8, 0:1].astype(jnp.int32)
    number = jnp.where((index >= 0) & (index < ni), base + index, 0)
    rows += [(number >> 8).astype(F32), (number & 255).astype(F32)]
    item_ref[...] = low(jnp.concatenate(rows, axis=0))

    for k in range(n_rows):
        q = lax.rem(r + k, n_rows)
        whole = low(frame[q])
        mine_refs[k][...] = whole[0:64, :]
        over_refs[k][...] = whole[64:, :]


def canvas_kernel(n_rows, *refs):
    mine, over = refs[0:n_rows], refs[n_rows : 2 * n_rows]
    vel_ref, grad_ref = refs[2 * n_rows :]
    total = mine[0][...].astype(F32)
    for ref in mine[1:]:
        total = total + ref[...].astype(F32)
    extra = over[0][...].astype(F32)
    for ref in over[1:]:
        extra = extra + ref[...].astype(F32)
    total = low(total + jnp.concatenate([extra, jnp.zeros((64 - RIGHT, 256), F32)], axis=0))
    for n, ref in enumerate((vel_ref, grad_ref)):
        value = 0.0
        for side in (0, 1):
            pick = one(iota((64, 128), 1) == 2 * iota((64, 128), 0) + side)
            value = value + t_mm(total[:, n * 128 + side * 64 : n * 128 + (side + 1) * 64], pick)
        ref[...] = value.reshape(ref.shape).astype(ref.dtype)


def add_kernel(count, me, *refs):
    outs = refs[len(refs) - count :]
    ins = refs[: len(refs) - count]
    spot = me()
    for m, out in enumerate(outs):
        at = jnp.bitwise_xor(spot, m) if count > 1 else 0
        total = ins[0][at].astype(F32)
        for ref in ins[1:]:
            total = total + ref[at].astype(F32)
        out[...] = low(total)


def plane_spot():
    return lax.axis_index("row") + lax.axis_size("row") * ((lax.axis_index("col") >> 1) & 1)


def line_spot():
    return lax.axis_index("col") >> 2


def send(value, n_rows, n_cols, flip_row=0, flip_col=0):
    route = [
        (i * n_cols + j, (i ^ flip_row) * n_cols + (j ^ flip_col)) for i in range(n_rows) for j in range(n_cols)
    ]
    return lax.ppermute(value, ("row", "col"), route)


def add_up(arrays, count, me):
    n, w = arrays[0].shape
    ins = [a.reshape(count, n // count, w) for a in arrays]
    return call(functools.partial(add_kernel, count, me), [((n // count, w), BF16)] * count, ins)


def scatter_sum(keep, out, n_rows, n_cols):
    go = functools.partial(send, n_rows=n_rows, n_cols=n_cols)
    parts = add_up([keep, go(out, flip_col=1)], 2 * n_rows, plane_spot)
    got = [go(parts[m], flip_row=m % n_rows, flip_col=2 * (m // n_rows)) for m in range(1, 2 * n_rows)]
    line = n_cols // 4
    parts = add_up([parts[0]] + got, line, line_spot)
    got = [go(parts[m], flip_col=4 * m) for m in range(1, line)]
    return add_up([parts[0]] + got, 1, line_spot)[0]


def gather_all(part, n_rows, n_cols):
    go = functools.partial(send, n_rows=n_rows, n_cols=n_cols)
    line = n_cols // 4
    block = jnp.stack([part] + [go(part, flip_col=4 * m) for m in range(1, line)])
    block = jnp.stack(
        [block] + [go(block, flip_row=m % n_rows, flip_col=2 * (m // n_rows)) for m in range(1, 2 * n_rows)]
    )
    return block, go(block, flip_col=1)


def each_part(n_rows, n_cols):
    core = lax.axis_index("col") & 1
    plane, line = plane_spot(), line_spot()
    for c in range(2):
        for m in range(2 * n_rows):
            for n in range(n_cols // 4):
                yield c, m, n, jnp.bitwise_xor(core, c), jnp.bitwise_xor(plane, m), jnp.bitwise_xor(line, n)


def assemble(mesh_shape, own_ref, other_ref, whole):
    n_rows, n_cols = mesh_shape
    for c, m, n, ac, am, an in each_part(n_rows, n_cols):
        whole[(ac * 2 * n_rows + am) * (n_cols // 4) + an] = (own_ref if c == 0 else other_ref)[m, n].astype(F32)


def first_out_kernel(mesh_shape, own_ref, other_ref, ret_ref, hid_ref, out_ref, small_ref, whole):
    assemble(mesh_shape, own_ref, other_ref, whole)
    flat = whole[...].reshape(whole.shape[0] * whole.shape[1], whole.shape[2])
    width = flat.shape[1]
    hidden = ret_ref.shape[0]
    ret_ref[...] = flat[0:hidden]
    for n in range(hidden // width):
        hid_ref[:, n * width : (n + 1) * width] = flat[hidden + n * width : hidden + (n + 1) * width]
    out_ref[...] = flat[2 * hidden : 2 * hidden + width]
    small_ref[...] = flat[2 * hidden + width : 2 * hidden + width + 128]


def second_out_kernel(mesh_shape, own_ref, other_ref, att_ref, small_ref, whole):
    assemble(mesh_shape, own_ref, other_ref, whole)
    flat = whole[...].reshape(whole.shape[0] * whole.shape[1], whole.shape[2])
    width = flat.shape[1]
    for n in range(3):
        att_ref[:, n * width : (n + 1) * width] = flat[n * width : (n + 1) * width]
    small_ref[...] = flat[3 * width : 3 * width + 128]


def condition_kernel(
    mesh_shape, ni, own_ref, other_ref, tl_ref, feat_ref, pre_ref, cond_ref, act_ref, mw_ref, fw_ref, cw_ref,
    mod_ref, fin_ref, table_ref, clock_ref, time_ref, bias_ref, rows_s, dev_s,
):
    n_rows, n_cols = mesh_shape
    width = cw_ref.shape[0]
    items = tl_ref.shape[1]
    ids = jnp.zeros((16, width), F32)
    for c, m, n, ac, am, an in each_part(n_rows, n_cols):
        part = (own_ref if c == 0 else other_ref)[m, n].astype(F32)
        at = (ac * 2 * n_rows + am) * (n_cols // 4) + an
        dev_s[at] = part[0 : 8 * ni]
        ids = ids + part[8 * ni :]
    count = n_rows * n_cols
    numbers = ids[0:8] * 256.0 + ids[8:16]
    number = jnp.concatenate([numbers[k : k + 1, :] for k in range(-(-count * ni // width))], axis=1)[:, : count * ni]
    pick = one(iota((items, count * ni), 0).astype(F32) == number)
    for b in range(8):
        block = jnp.concatenate([dev_s[d, b * ni : (b + 1) * ni, :] for d in range(count)], axis=0)
        rows_s[:, b * width : (b + 1) * width] = low(mm(pick, low(block)))
    ones = jnp.ones((8, items), BF16)
    act = act_ref[...]
    d_cond = jnp.zeros((items, width), F32)
    for b in range(8):
        grad = rows_s[:, b * width : (b + 1) * width]
        bias_ref[b : b + 1, :] = mm(ones, grad)[0:1, :]
        if b < 6:
            mod_ref[:, b * width : (b + 1) * width] = t_mm(act, grad)
            d_cond = d_cond + mm_t(grad, mw_ref[:, b * width : (b + 1) * width])
        else:
            fin_ref[:, (b - 6) * width : (b - 5) * width] = t_mm(act, grad)
            d_cond = d_cond + mm_t(grad, fw_ref[:, (b - 6) * width : (b - 5) * width])
    cond = cond_ref[...]
    sigma = sigmoid(cond)
    d_cond = low(d_cond * (sigma * (1.0 + cond * (1.0 - sigma))))
    pre = pre_ref[...]
    sigma = sigmoid(pre)
    hidden = low(pre * sigma)
    classes = table_ref.shape[0]
    table_ref[...] = mm(one(iota((classes, items), 0) == tl_ref[1:2, :]), d_cond)
    clock_ref[...] = t_mm(hidden, d_cond)
    bias_ref[8:9, :] = mm(ones, d_cond)[0:1, :]
    d_time = low(mm_t(d_cond, cw_ref[...]) * (sigma * (1.0 + pre * (1.0 - sigma))))
    time_ref[...] = mm(feat_ref[...], d_time)
    bias_ref[9:10, :] = mm(ones, d_time)[0:1, :]


def local(
    latent, cotangent, item_ids, positions, gap_mask, timesteps, labels, patch_weight, patch_bias, time_weight,
    time_bias, clock_weight, clock_bias, class_table, modulation_weight, modulation_bias, attention_weight, query_bias,
    value_bias, output_weight, output_bias, hidden_weight, hidden_bias, return_weight, return_bias, final_modulation,
    final_offsets, readout_weight, readout_bias,
):
    n_rows, n_cols = lax.axis_size("row"), lax.axis_size("col")
    row_count, col_count = item_ids.shape
    width = patch_weight.shape[1]
    hidden = hidden_weight.shape[1]
    hp = n_rows * row_count
    cw = col_count // n_rows
    tokens = (cw + HALO) * hp
    ni = 2 * (-(-cw // LEAST))
    items = -(-(timesteps.shape[0] + 16) // 32) * 32
    unit = 8 * n_rows * n_cols
    rows_1 = -(-(2 * hidden + width + 128) // unit) * unit
    rows_2 = -(-(3 * width + 128) // unit) * unit
    pairs = width // 128

    tile, first_cols, last_cols = call(
        tile_kernel,
        [((col_count, 384), BF16), ((RIGHT, 384), BF16), ((LEFT, 384), BF16)],
        [latent, cotangent, item_ids, positions, gap_mask],
    )

    def shift(value, step_row, step_col, wanted):
        route = [
            (i * n_cols + j, (i + step_row) % n_rows * n_cols + j + step_col)
            for i in range(n_rows)
            for j in range(n_cols)
            if 0 <= j + step_col < n_cols and wanted((i + step_row) % n_rows)
        ]
        return lax.ppermute(value, ("row", "col"), route)

    left = shift(last_cols, 0, 1, lambda i: i == 0)
    tiles = [shift(tile, k, 0, lambda i: True) for k in range(1, n_rows)]
    rights = [shift(first_cols, k, -1, lambda i: (i + 1) * cw + HALO + 1 > col_count) for k in range(n_rows)]

    flat_bias = jnp.concatenate(
        [patch_bias, time_bias, clock_bias, modulation_bias, query_bias, value_bias, output_bias, hidden_bias,
         return_bias, final_offsets, readout_bias]
    ).astype(F32)
    biases = jnp.pad(flat_bias, (0, 24 * width - flat_bias.shape[0])).reshape(24, width)
    tl = jnp.pad(jnp.stack([timesteps, labels]), ((0, 6), (0, items - timesteps.shape[0])))

    feat, time_pre, condition, cond_act, table = call(
        item_kernel,
        [((time_weight.shape[0], items), BF16), ((items, width), F32), ((items, width), F32), ((items, width), BF16),
         ((4 * POSITIONS, width), BF16)],
        [tl, time_weight, clock_weight, class_table, biases],
    )

    dims = (n_rows, hp, cw, tokens, ni, rows_1 // 2)
    heads = ((pairs, tokens, 128), BF16)
    got = call(
        functools.partial(main_kernel, dims),
        [heads, heads, heads, heads, ((8, tokens), F32), ((tokens, 128), F32), ((tokens, width), F32),
         ((tokens, width), F32), ((tokens, width), BF16), ((tokens, 128), BF16), ((tokens, 128), BF16),
         ((128, 8 * width), BF16), ((tokens, 128), BF16), ((16, 8 * width), F32),
         ((rows_1 // 2, width), BF16), ((rows_1 // 2, width), BF16)],
        [tile, left, *tiles, *rights, cond_act, table, biases, patch_weight, modulation_weight, final_modulation,
         attention_weight, output_weight, hidden_weight, return_weight, readout_weight],
        [((n_rows, LEFT + 64 + RIGHT, 384), BF16), ((tokens, 128), BF16), ((pairs, tokens, 128), BF16),
         ((tokens, width), BF16), ((tokens, hidden), BF16), ((tokens, hidden), BF16), ((tokens, width), BF16),
         ((tokens, width), BF16), ((tokens, width), BF16), ((BLOCK, hidden), F32), ((16, 8 * width), F32),
         ((128, width), F32), ((2, rows_1 // 2, width), BF16)],
    )
    saved, keep, out = got[:14], got[14], got[15]
    part_1 = scatter_sum(keep, out, n_rows, n_cols)

    dims = (n_rows, hp, cw, tokens, ni, rows_2 // 2)
    got = call(
        functools.partial(back_kernel, dims),
        [((rows_2 // 2, width), BF16), ((rows_2 // 2, width), BF16), ((8 * ni + 16, width), BF16)]
        + [((64, 256), BF16)] * n_rows + [((RIGHT, 256), BF16)] * n_rows,
        [*saved, attention_weight, patch_weight],
        [((pairs, tokens, 128), BF16), ((pairs, tokens, 128), F32), ((pairs, tokens, 128), F32),
         ((tokens, 3 * width), BF16), ((tokens, width), BF16), ((16, 2 * width), F32), ((n_rows, 64 + RIGHT, 256), F32),
         ((128, width), F32), ((2, rows_2 // 2, width), BF16)],
    )
    keep, out, item_rows = got[:3]
    mine, over = got[3 : 3 + n_rows], got[3 + n_rows :]
    part_2 = scatter_sum(keep, out, n_rows, n_cols)

    mine = [mine[0]] + [shift(mine[k], k, 0, lambda i: True) for k in range(1, n_rows)]
    over = [shift(over[k], k, 1, lambda i: True) for k in range(n_rows)]
    velocity, latent_grad = call(
        functools.partial(canvas_kernel, n_rows), [(latent.shape, BF16), (latent.shape, F32)], [*mine, *over]
    )

    shape = (n_rows, n_cols)
    whole_1 = gather_all(part_1, n_rows, n_cols)
    whole_2 = gather_all(part_2, n_rows, n_cols)
    whole_3 = gather_all(item_rows, n_rows, n_cols)
    devices = n_rows * n_cols
    return_grad, hidden_grad, output_grad, small_1 = call(
        functools.partial(first_out_kernel, shape),
        [((hidden, width), F32), ((width, hidden), F32), ((width, width), F32), ((128, width), F32)],
        [*whole_1],
        [((devices, rows_1 // devices, width), F32)],
    )
    attention_grad, small_2 = call(
        functools.partial(second_out_kernel, shape),
        [((width, 3 * width), F32), ((128, width), F32)],
        [*whole_2],
        [((devices, rows_2 // devices, width), F32)],
    )
    modulation_grad, final_grad, table_grad, clock_grad, time_grad, small_3 = call(
        functools.partial(condition_kernel, shape, ni),
        [((width, 6 * width), F32), ((width, 2 * width), F32), (class_table.shape, F32), ((width, width), F32),
         (time_weight.shape, F32), ((16, width), F32)],
        [*whole_3, tl, feat, time_pre, condition, cond_act, modulation_weight, final_modulation, clock_weight],
        [((items, 8 * width), BF16), ((devices, 8 * ni, width), F32)],
    )
    return (
        velocity, latent_grad, small_2[0:16], small_2[16], time_grad, small_3[9], clock_grad, small_3[8], table_grad,
        modulation_grad, small_3[0:6].reshape(-1), attention_grad, small_2[17], small_2[18], output_grad, small_1[21],
        hidden_grad, small_1[17:21].reshape(-1), return_grad, small_1[16], final_grad, small_3[6:8].reshape(-1),
        small_1[0:16].T, small_1[22, 0:16],
    )


def solution(mesh):
    canvas, grid = P(None, "row", "col"), P("row", "col")
    return jax.shard_map(
        local,
        mesh=mesh,
        in_specs=(canvas, canvas, grid, canvas, grid) + (P(),) * 24,
        out_specs=(canvas, canvas) + (P(),) * 22,
        check_vma=False,
    )
```

```python
import functools
import math

import jax
import jax.numpy as jnp
from jax import lax
from jax.experimental import pallas as pl
from jax.experimental.pallas import tpu as pltpu
from jax.sharding import PartitionSpec as P

HEADS = 6
HALO = 16
LEAST = 8
BLOCK = 256
LEFT = 16
RIGHT = 32
POSITIONS = 128
F32 = jnp.float32
BF16 = jnp.bfloat16
FLOPS_US = 1_150_000_000
BYTES_US = 3_700_000


def iota(shape, dim):
    return lax.broadcasted_iota(jnp.int32, shape, dim)


def mm(a, b):
    return jnp.dot(a, b, preferred_element_type=F32)


def mm_t(a, b):
    return lax.dot_general(a, b, (((1,), (1,)), ((), ())), preferred_element_type=F32)


def t_mm(a, b):
    return lax.dot_general(a, b, (((0,), (0,)), ((), ())), preferred_element_type=F32)


def low(v):
    return v.astype(BF16)


def one(cond):
    return jnp.where(cond, 1.0, 0.0).astype(BF16)


def sigmoid(v):
    return 1.0 / (1.0 + jnp.exp(-v))


def layer_norm(v):
    center = v - jnp.mean(v, axis=-1, keepdims=True)
    inverse = lax.rsqrt(jnp.mean(center * center, axis=-1, keepdims=True) + 1e-06)
    return center * inverse, inverse


def norm_back(normed, inverse, grad):
    mean_grad = jnp.mean(grad, axis=-1, keepdims=True)
    mean_cross = jnp.mean(grad * normed, axis=-1, keepdims=True)
    return inverse * (grad - mean_grad - normed * mean_cross)


def call(body, outs, ins, scratch=(), near_in=(), near_out=(), after=(), us=2, room=16):
    spec = pl.BlockSpec(memory_space=pltpu.VMEM)
    used = len(ins)

    def run(*refs):
        body(*refs[:used], *refs[used + len(after) :])

    ins = [pltpu.with_memory_space_constraint(a, pltpu.VMEM) if n in near_in else a for n, a in enumerate(ins)]
    return pl.pallas_call(
        run,
        out_shape=[
            (pltpu.VMEM if n in near_out else jax.ShapeDtypeStruct)(shape, dtype)
            for n, (shape, dtype) in enumerate(outs)
        ],
        in_specs=[spec] * used + [pl.BlockSpec(memory_space=pl.ANY)] * len(after),
        out_specs=[spec] * len(outs),
        scratch_shapes=[pltpu.VMEM(shape, dtype) for shape, dtype in scratch],
        compiler_params=pltpu.CompilerParams(vmem_limit_bytes=room * 1024 * 1024),
        cost_estimate=pl.CostEstimate(flops=us * FLOPS_US, bytes_accessed=us * BYTES_US, transcendentals=0),
    )(*ins, *after)


def line(ref, start=0, count=None):
    count = ref.shape[0] if count is None else count
    return ref[start : start + count].astype(F32).reshape(1, count)


def lane_fold(rows):
    lane = iota((rows, 128), 1)
    feature = 8 * (1 - (lane & 1)) + 4 * (1 - (lane >> 6)) + ((lane >> 4) & 3)
    return one(iota((rows, 128), 0) == feature)


def tile_kernel(lat_ref, cot_ref, ids_ref, pos_ref, gap_ref, tile_ref, first_ref, last_ref):
    cols = ids_ref.shape[1]
    pieces = []
    for ref in (lat_ref, cot_ref):
        flat = ref[...].reshape(64, 2 * cols)
        for side in (0, 1):
            pick = one(iota((cols, 2 * cols), 1) == 2 * iota((cols, 2 * cols), 0) + side)
            pieces.append(mm_t(pick, flat))
    tag = ids_ref[...] + 1
    meta = jnp.concatenate(
        [tag >> 8, tag & 255, pos_ref[0], pos_ref[1], gap_ref[...], jnp.zeros((88, cols), jnp.int32)], axis=0
    ).astype(F32)
    pieces.append(mm_t(one(iota((cols, cols), 0) == iota((cols, cols), 1)), low(meta)))
    tile = low(jnp.concatenate(pieces, axis=1))
    tile_ref[...] = tile
    first_ref[...] = tile[:RIGHT]
    last_ref[...] = tile[cols - LEFT :]


def item_kernel(
    steps_ref, labels_ref, tw_ref, tb_ref, cw_ref, cb_ref, ct_ref, tl_ref, feat_ref, pre_ref, cond_ref, act_ref, table_ref
):
    items = tl_ref.shape[1]
    count = steps_ref.shape[0]
    tl_ref[...] = jnp.zeros_like(tl_ref)
    tl_ref[0:1, 0:count] = steps_ref[...].reshape(1, count)
    tl_ref[1:2, 0:count] = labels_ref[...].reshape(1, count)
    half = tw_ref.shape[0] // 2
    steps = tl_ref[0:1, :].astype(F32)
    freq = jnp.exp(iota((half, 1), 0).astype(F32) * (-math.log(10000.0) / half))
    angle = freq * steps
    feat_ref[0:half, :] = low(jnp.cos(angle))
    feat_ref[half:, :] = low(jnp.sin(angle))
    pre = t_mm(feat_ref[...], tw_ref[...]) + line(tb_ref)
    pre_ref[...] = pre
    hidden = low(pre * sigmoid(pre))
    classes = ct_ref.shape[0]
    pick = one(iota((classes, items), 0) == tl_ref[1:2, :])
    cond = mm(hidden, cw_ref[...]) + line(cb_ref) + t_mm(pick, ct_ref[...])
    cond_ref[...] = cond
    act_ref[...] = low(cond * sigmoid(cond))
    width = table_ref.shape[1]
    quarter = width // 4
    shape = (2 * POSITIONS, width)
    lane = iota(shape, 1)
    row = iota(shape, 0)
    second = lane >= 2 * quarter
    within = jnp.where(second, lane - 2 * quarter, lane)
    cosine = within >= quarter
    index = jnp.where(cosine, within - quarter, within)
    omega = jnp.exp(index.astype(F32) * (-math.log(10000.0) / quarter))
    angle = (row & (POSITIONS - 1)).astype(F32) * omega
    value = jnp.where(cosine, jnp.cos(angle), jnp.sin(angle))
    value = jnp.where(jnp.where(second, 1, 0) == jnp.where(row >= POSITIONS, 1, 0), value, 0.0)
    high = low(value)
    table_ref[0 : 2 * POSITIONS, :] = high
    table_ref[2 * POSITIONS :, :] = low(value - high.astype(F32))


def row_mask(q, i, shape):
    return ((q * 16 + (iota(shape, 1) & 15) - 1) >> 1) == i


def main_kernel(dims, *refs):
    n_rows, hp, cw, tokens, ni, half_rows = dims
    own_ref, left_ref = refs[0:2]
    tiles = refs[2 : 1 + n_rows]
    rights = refs[1 + n_rows : 1 + 2 * n_rows]
    (act_ref, table_ref, pb_ref, mb_ref, qb_ref, vb_ref, ob_ref, hb_ref, rb_ref, fb_ref, lb_ref,
     pw_ref, mw_ref, fw_ref, aw_ref, ow_ref, hw_ref, rw_ref, low_ref,
     q_ref, k_ref, v_ref, da_ref, rows_ref, aux_ref, res_ref, mid_ref, in_ref, x_ref, mem_ref, ms_ref, vel_ref,
     item_ref, keep_ref, send_ref,
     es, ct_s, at_s, mlp_s, ha_s, dh_s, dbm_s, dba_s, ri_s, gd_s, dacc, small, g_s) = refs[1 + 2 * n_rows :]
    width = res_ref.shape[1]
    pairs = width // 128
    r = lax.axis_index("row")
    core = lax.axis_index("col") & 1
    shift = int(math.log2(hp))

    es[...] = jnp.zeros_like(es)
    es[r, LEFT : LEFT + 64, :] = own_ref[...]
    es[r, 0:LEFT, :] = left_ref[...]
    for k in range(1, n_rows):
        es[lax.rem(r - k + n_rows, n_rows), LEFT : LEFT + 64, :] = tiles[k - 1][...]
    for k in range(n_rows):
        es[lax.rem(r - k + n_rows, n_rows), LEFT + 64 :, :] = rights[k][...]
    meta = es[r, :, 256:384].astype(F32)
    lane = iota(meta.shape, 1)
    weighted = meta * jnp.where(lane == 0, 256.0, jnp.where(lane == 8, 1.0, 0.0))
    down = iota(meta.shape, 0)
    start = LEFT + r * cw
    tag_prev = jnp.sum(jnp.where(down == start - 1, weighted, 0.0)).astype(jnp.int32)
    tag_last = jnp.sum(jnp.where(down == start + cw - 1, weighted, 0.0)).astype(jnp.int32)
    tag_first = jnp.sum(jnp.where(down == start, weighted, 0.0)).astype(jnp.int32)
    strip_prev = jnp.where(tag_prev == 0, ((tag_first - 1) >> 1) - 1, (tag_prev - 1) >> 1)
    strip_last = (tag_last - 1) >> 1
    base = 2 * (strip_prev + 1)

    pick = one(iota((16, act_ref.shape[0]), 1) == base + iota((16, act_ref.shape[0]), 0))
    own_act = low(mm(pick, act_ref[...]))
    ms_ref[48:, :] = jnp.zeros_like(ms_ref[48:, :])
    for b in range(8):
        cols = slice(b * width, (b + 1) * width)
        if b < 6:
            value = mm(own_act, mw_ref[:, cols]) + line(mb_ref, b * width, width)
        else:
            value = mm(own_act, fw_ref[:, (b - 6) * width : (b - 5) * width]) + line(fb_ref, (b - 6) * width, width)
        p0 = low(value)
        rest = value - p0.astype(F32)
        p1 = low(rest)
        ms_ref[0:16, cols] = p0
        ms_ref[16:32, cols] = p1
        ms_ref[32:48, cols] = low(rest - p1.astype(F32))

    def mod(mem, b, n=1):
        return mm(mem, ms_ref[:, b * width : (b + n) * width])

    fold = lane_fold(16)
    embed = low(t_mm(fold, pw_ref[...]))
    unread = low(t_mm(low_ref[...], fold))
    b_lanes = iota((BLOCK, 128), 1)
    is_b1 = b_lanes >= 64
    half_lanes = (one(b_lanes < 64), one(is_b1))

    def first(tb, carry):
        t0 = pl.multiple_of(tb * BLOCK, BLOCK)
        rows = pl.ds(t0, BLOCK)
        token = t0 + iota((BLOCK, 1), 0)
        j = token >> shift
        i = token & (hp - 1)
        spot = iota((BLOCK, LEFT + 64 + RIGHT), 1)
        rep0 = one(spot == start + j)
        rep1 = one(spot == start + j + 1)
        x = jnp.zeros((BLOCK, 128), F32)
        c = jnp.zeros((BLOCK, 128), F32)
        m = jnp.zeros((BLOCK, 128), F32)
        for q in range(n_rows):
            here = mm(rep0, es[q])
            beside = mm(rep1, es[q, :, 0:256])
            mask = row_mask(q, i, (BLOCK, 128))
            x = x + jnp.where(mask, jnp.where(is_b1, here[:, 0:128], beside[:, 0:128]), 0.0)
            c = c + jnp.where(mask, jnp.where(is_b1, here[:, 128:256], beside[:, 128:256]), 0.0)
            m = m + jnp.where((q * 8 + (b_lanes & 7)) == i, here[:, 256:384], 0.0)
        x = low(x)
        m = low(m)
        x_ref[rows, :] = x
        ml = iota((128, 128), 0)
        mc = iota((128, 128), 1)
        kind = ml >> 3
        gather = jnp.where(
            (mc == 0) & (kind == 0), 256.0,
            jnp.where(((mc == 0) & (kind == 1)) | ((mc >= 1) & (mc <= 3) & (kind == mc + 1)), 1.0, 0.0),
        ).astype(BF16)
        cols = mm(m, gather)
        rl = iota((8, 128), 1) >> 3
        rr = iota((8, 128), 0)
        row_pick = jnp.where((rr == 6) & (rl == 0), 256.0, jnp.where((rr == 6) & (rl == 1), 1.0, 0.0)).astype(BF16)
        rows_ref[:, rows] = mm_t(row_pick, m)
        tag = cols[:, 0:1]
        gap = cols[:, 3:4]
        tag_i = tag.astype(jnp.int32)
        strip = (tag_i - 1) >> 1
        owned = (strip > strip_prev) & (strip <= strip_last)
        act = jnp.where(owned, gap, 0.0)
        aux_ref[rows, :] = jnp.where(b_lanes == 0, tag * gap, jnp.where(b_lanes == 1, act, 0.0))
        item = tag_i - 1 - base
        mem = one((item == (b_lanes & 15)) & (b_lanes < 48) & owned)
        mem_ref[rows, :] = mem
        ct_s[rows, :] = low(c * act)
        p0 = cols[:, 1:2].astype(jnp.int32)
        p1 = cols[:, 2:3].astype(jnp.int32) + POSITIONS
        spot = iota((BLOCK, 2 * POSITIONS), 1)
        place = one((spot == p0) | (spot == p1))
        res = (
            mm(x, embed) + line(pb_ref)
            + (mm(place, table_ref[0 : 2 * POSITIONS, :]) + mm(place, table_ref[2 * POSITIONS :, :]))
        )
        res_ref[rows, :] = res
        normed, _ = layer_norm(res)
        ab = mod(mem, 0, 2)
        attn_in = low(normed * (1.0 + ab[:, width:]) + ab[:, :width])
        in_ref[rows, :] = attn_in
        for part, ref in enumerate((q_ref, k_ref, v_ref)):
            value = mm(attn_in, aw_ref[:, part * width : (part + 1) * width])
            if part != 1:
                value = value + line(vb_ref if part else qb_ref)
            value = low(value)
            if part == 0:
                value = value * BF16(1.0 / math.sqrt(width // HEADS))
            for p in range(pairs):
                ref[p, rows, :] = value[:, p * 128 : (p + 1) * 128]
        return carry

    lax.fori_loop(0, tokens // BLOCK, first, 0)

    for qb in range(tokens // BLOCK):
        qs = slice(qb * BLOCK, (qb + 1) * BLOCK)
        ks = key_range(qb, hp, tokens)
        q_tag = rows_ref[6:7, qs]
        k_tag = aux_ref[ks, 0:1]
        allowed = k_tag == q_tag
        for p in range(pairs):
            query = q_ref[p, qs, :]
            key = k_ref[p, ks, :]
            value = v_ref[p, ks, :]
            halves = []
            for e in range(2):
                scores = jnp.where(allowed, mm_t(key, query * half_lanes[e]), -1e30)
                top = jnp.max(scores, axis=0, keepdims=True)
                expo = jnp.exp(scores - top)
                total = jnp.sum(expo, axis=0, keepdims=True)
                rows_ref[2 * p + e : 2 * p + e + 1, qs] = top + jnp.log(total)
                halves.append(t_mm(low(expo * (1.0 / total)), value))
            at_s[p, qs, :] = low(jnp.where(is_b1, halves[1], halves[0]))

    dacc[...] = jnp.zeros_like(dacc)

    def second(tb, carry):
        t0 = pl.multiple_of(tb * BLOCK, BLOCK)
        rows = pl.ds(t0, BLOCK)
        mem = mem_ref[rows, :]

        def item_sum(b, grad):
            dacc[:, b * width : (b + 1) * width] += t_mm(mem, low(grad))[0:16, :]

        attended = jnp.concatenate([at_s[p, rows, :] for p in range(pairs)], axis=1)
        branch_a = mm(attended, ow_ref[...]) + line(ob_ref)
        gate_a = mod(mem, 2)
        mid = res_ref[rows, :] + gate_a * branch_a
        norm_mid, inv_mid = layer_norm(mid)
        scale_m = 1.0 + mod(mem, 4)
        mlp_in = low(norm_mid * scale_m + mod(mem, 3))
        mlp_s[rows, :] = mlp_in
        hidden = hw_ref.shape[1]
        branch_m = jnp.zeros((BLOCK, width), F32)
        for n in range(hidden // width):
            part = slice(n * width, (n + 1) * width)
            pre = mm(mlp_in, hw_ref[:, part]) + line(hb_ref, n * width, width)
            square = pre * pre
            c0 = math.sqrt(2.0 / math.pi)
            t = jnp.tanh(pre * (c0 + (c0 * 0.044715) * square))
            up = 0.5 + 0.5 * t
            act = low(pre * up)
            gd_s[:, part] = up + (0.5 * pre) * (1.0 - t * t) * (c0 + (3.0 * c0 * 0.044715) * square)
            ha_s[rows, part] = act
            branch_m = branch_m + mm(act, rw_ref[part, :])
        branch_m = branch_m + line(rb_ref)
        gate_m = mod(mem, 5)
        norm_out, inv_out = layer_norm(mid + gate_m * branch_m)
        scale_f = 1.0 + mod(mem, 7)
        readout_in = low(norm_out * scale_f + mod(mem, 6))
        ri_s[rows, :] = readout_in
        active = aux_ref[rows, 1:2]
        bias_lanes = mm(low(line(lb_ref) + jnp.zeros((8, 16), F32)), fold)[0:1, :]
        vel_ref[rows, :] = low((mm(readout_in, unread) + bias_lanes) * active)
        d_read = mm_t(ct_s[rows, :], unread)
        item_sum(6, d_read)
        item_sum(7, d_read * norm_out)
        d_out = norm_back(norm_out, inv_out, d_read * scale_f)
        item_sum(5, d_out * branch_m)
        d_bm = low(d_out * gate_m)
        dbm_s[rows, :] = d_bm
        d_mlp = jnp.zeros((BLOCK, width), F32)
        for n in range(hidden // width):
            part = slice(n * width, (n + 1) * width)
            d_hid = low(mm_t(d_bm, rw_ref[part, :]) * gd_s[:, part])
            dh_s[rows, part] = d_hid
            d_mlp = d_mlp + mm_t(d_hid, hw_ref[:, part])
        item_sum(3, d_mlp)
        item_sum(4, d_mlp * norm_mid)
        d_mid = d_out + norm_back(norm_mid, inv_mid, d_mlp * scale_m)
        mid_ref[rows, :] = d_mid
        item_sum(2, d_mid * branch_a)
        d_ba = low(d_mid * gate_a)
        dba_s[rows, :] = d_ba
        d_at = low(mm_t(d_ba, ow_ref[...]))
        for p in range(pairs):
            da_ref[p, rows, :] = d_at[:, p * 128 : (p + 1) * 128]
        return carry

    lax.fori_loop(0, tokens // BLOCK, second, 0)
    rows = [dacc[0:ni, b * width : (b + 1) * width] for b in range(2, 8)]
    spot = ((core * 2 * n_rows + plane_spot()) * (lax.axis_size("col") // 4) + line_spot()) * ni
    index = iota((8, width), 0) * width + iota((8, width), 1) - spot
    number = jnp.where((index >= 0) & (index < ni), base + index, 0)
    rows += [(number >> 8).astype(F32), (number & 255).astype(F32)]
    item_ref[...] = low(jnp.concatenate(rows, axis=0))

    g_s[...] = jnp.zeros_like(g_s)
    put = functools.partial(put_rows, g_s, half_rows)
    n_hidden = hw_ref.shape[1] // width
    for n in range(n_hidden):
        part = slice(n * width, (n + 1) * width)
        put(n * width, low(t_mm(ha_s[:, part], dbm_s[...])))
        put((n_hidden + n) * width, low(t_mm(mlp_s[...], dh_s[:, part])))
    attended = jnp.concatenate([at_s[p] for p in range(pairs)], axis=1)
    put(2 * n_hidden * width, low(t_mm(attended, dba_s[...])))
    ones = jnp.ones((8, tokens), BF16)
    small[...] = jnp.zeros_like(small)
    small[0:16, :] = mm(fold, low(t_mm(ct_s[...], ri_s[...])))
    small[16:17, :] = mm(ones, dbm_s[...])[0:1, :]
    for n in range(n_hidden):
        small[17 + n : 18 + n, :] = mm(ones, dh_s[:, n * width : (n + 1) * width])[0:1, :]
    small[21:22, :] = mm(ones, dba_s[...])[0:1, :]
    sums = mm(ones, ct_s[...])
    small[22:23, 0:128] = mm_t(jnp.broadcast_to(low(sums[0:1, :]), (8, 128)), lane_fold(128))[0:1, :]
    put((2 * n_hidden + 1) * width, low(small[...]))
    keep_ref[...] = g_s[core]
    send_ref[...] = g_s[1 - core]


def put_rows(g_s, half_rows, row, value):
    count = value.shape[0]
    done = 0
    while done < count:
        side, at = divmod(row + done, half_rows)
        take = min(count - done, half_rows - at)
        g_s[side, at : at + take, :] = value[done : done + take, :]
        done += take


def key_range(qb, hp, tokens):
    first_col = (qb * BLOCK) // hp
    last_col = ((qb + 1) * BLOCK - 1) // hp
    return slice(max(0, first_col - HALO) * hp, min(tokens, (last_col + 1 + HALO) * hp))


def attend_back_kernel(hp, first, q_ref, k_ref, v_ref, da_ref, rows_ref, aux_ref, dq_ref, dk_ref, dv_ref, dk_s, dv_s):
    tokens = q_ref.shape[1]
    b_lanes = iota((BLOCK, 128), 1)
    is_b1 = b_lanes >= 64
    half_lanes = (one(b_lanes < 64), one(is_b1))
    scale = 1.0 / math.sqrt(q_ref.shape[0] * 128 // HEADS)
    dk_s[...] = jnp.zeros_like(dk_s)
    dv_s[...] = jnp.zeros_like(dv_s)
    for qb in range(tokens // BLOCK):
        qs = slice(qb * BLOCK, (qb + 1) * BLOCK)
        ks = key_range(qb, hp, tokens)
        allowed = aux_ref[ks, 0:1] == rows_ref[6:7, qs]
        for n in range(dq_ref.shape[0]):
            p = first + n
            query = q_ref[p, qs, :]
            key = k_ref[p, ks, :]
            value = v_ref[p, ks, :]
            d_at = da_ref[p, qs, :]
            d_key = 0.0
            d_value = 0.0
            halves = []
            for e in range(2):
                q_half = query * half_lanes[e]
                d_half = d_at * half_lanes[e]
                scores = jnp.where(allowed, mm_t(key, q_half), -1e30)
                probs = jnp.exp(scores - rows_ref[2 * p + e : 2 * p + e + 1, qs])
                d_probs = mm_t(value, d_half)
                inner = jnp.sum(probs * d_probs, axis=0, keepdims=True)
                d_scores = low(probs * (d_probs - inner))
                d_value = d_value + mm(low(probs), d_half)
                d_key = d_key + mm(d_scores, q_half)
                halves.append(t_mm(d_scores, key))
            dk_s[n, ks, :] += d_key
            dv_s[n, ks, :] += d_value
            dq_ref[n, qs, :] = low(jnp.where(is_b1, halves[1], halves[0]) * scale)
    dk_ref[...] = low(dk_s[...])
    dv_ref[...] = low(dv_s[...])


def joined(refs, rows):
    return jnp.concatenate(
        [ref[n, rows, :] for kind in range(3) for ref in refs[kind::3] for n in range(ref.shape[0])], axis=1
    )


def attention_weight_kernel(half_rows, in_ref, *refs):
    parts = refs[:6]
    keep_ref, send_ref, small, g_s = refs[6:]
    tokens, width = in_ref.shape
    core = lax.axis_index("col") & 1
    put = functools.partial(put_rows, g_s, half_rows)
    ones = jnp.ones((8, tokens), BF16)
    g_s[...] = jnp.zeros_like(g_s)
    small[...] = jnp.zeros_like(small)
    whole = joined(parts, slice(None))
    for n in range(3):
        grad = whole[:, n * width : (n + 1) * width]
        put(n * width, low(t_mm(in_ref[...], grad)))
        if n != 1:
            small[n // 2 : n // 2 + 1, :] = mm(ones, grad)[0:1, :]
    put(3 * width, low(small[...]))
    keep_ref[...] = g_s[core]
    send_ref[...] = g_s[1 - core]


def back_kernel(dims, *refs):
    n_rows, hp, cw, tokens, ni = dims
    parts = refs[:6]
    (res_ref, mid_ref, x_ref, mem_ref, ms_ref, vel_ref, aw_ref, pw_ref, item_ref) = refs[6:15]
    mine_refs = refs[15 : 15 + n_rows]
    over_refs = refs[15 + n_rows : 15 + 2 * n_rows]
    di_s, dacc, frame = refs[15 + 2 * n_rows :]
    width = res_ref.shape[1]
    r = lax.axis_index("row")
    shift = int(math.log2(hp))

    embed = low(t_mm(lane_fold(16), pw_ref[...]))
    dacc[...] = jnp.zeros_like(dacc)
    frame[...] = jnp.zeros_like(frame)

    def third(tb, carry):
        t0 = pl.multiple_of(tb * BLOCK, BLOCK)
        rows = pl.ds(t0, BLOCK)
        mem = mem_ref[rows, :]
        d_attn = mm_t(joined(parts, rows), aw_ref[...])
        normed, inverse = layer_norm(res_ref[rows, :])
        scale_a = 1.0 + mm(mem, ms_ref[:, width : 2 * width])
        dacc[:, 0:width] += t_mm(mem, low(d_attn))[0:16, :]
        dacc[:, width : 2 * width] += t_mm(mem, low(d_attn * normed))[0:16, :]
        d_in = low(mid_ref[rows, :] + norm_back(normed, inverse, d_attn * scale_a))
        di_s[rows, :] = d_in
        grad = low(mm_t(d_in, embed))
        both = jnp.concatenate([vel_ref[rows, :], grad], axis=1)
        token = t0 + iota((BLOCK, 1), 0)
        j = token >> shift
        i = token & (hp - 1)
        spot = iota((BLOCK, 64 + RIGHT), 1)
        rep = jnp.concatenate([one(spot == r * cw + j), one(spot == r * cw + j + 1)], axis=0)
        side = (iota((BLOCK, 256), 1) >> 6) & 1
        for q in range(n_rows):
            mask = row_mask(q, i, (BLOCK, 256))
            split = jnp.concatenate([both * one(mask & (side == 1)), both * one(mask & (side == 0))], axis=0)
            frame[q] += t_mm(rep, split)
        return carry

    lax.fori_loop(0, tokens // BLOCK, third, 0)

    ones = jnp.ones((8, tokens), BF16)
    rows = [dacc[0:ni, 0:width], dacc[0:ni, width : 2 * width]]
    rows += [mm(lane_fold(16), low(t_mm(x_ref[...], di_s[...]))), mm(ones, di_s[...])]
    item_ref[...] = low(jnp.concatenate(rows, axis=0))
    for k in range(n_rows):
        q = lax.rem(r + k, n_rows)
        whole = low(frame[q])
        mine_refs[k][...] = whole[0:64, :]
        over_refs[k][...] = whole[64:, :]


def canvas_kernel(n_rows, *refs):
    mine, over = refs[0:n_rows], refs[n_rows : 2 * n_rows]
    vel_ref, grad_ref = refs[2 * n_rows :]
    total = mine[0][...].astype(F32)
    for ref in mine[1:]:
        total = total + ref[...].astype(F32)
    extra = over[0][...].astype(F32)
    for ref in over[1:]:
        extra = extra + ref[...].astype(F32)
    total = low(total + jnp.concatenate([extra, jnp.zeros((64 - RIGHT, 256), F32)], axis=0))
    for n, ref in enumerate((vel_ref, grad_ref)):
        value = 0.0
        for side in (0, 1):
            pick = one(iota((64, 128), 1) == 2 * iota((64, 128), 0) + side)
            value = value + t_mm(total[:, n * 128 + side * 64 : n * 128 + (side + 1) * 64], pick)
        ref[...] = value.reshape(ref.shape).astype(ref.dtype)


def add_kernel(count, me, *refs):
    outs = refs[len(refs) - count :]
    ins = refs[: len(refs) - count]
    spot = me()
    for m, out in enumerate(outs):
        at = jnp.bitwise_xor(spot, m) if count > 1 else 0
        total = ins[0][at].astype(F32)
        for ref in ins[1:]:
            total = total + ref[at].astype(F32)
        out[...] = low(total)


def plane_spot():
    return lax.axis_index("row") + lax.axis_size("row") * ((lax.axis_index("col") >> 1) & 1)


def line_spot():
    return lax.axis_index("col") >> 2


def send(value, n_rows, n_cols, flip_row=0, flip_col=0):
    route = [
        (i * n_cols + j, (i ^ flip_row) * n_cols + (j ^ flip_col)) for i in range(n_rows) for j in range(n_cols)
    ]
    return lax.ppermute(value, ("row", "col"), route)


def add_up(arrays, count, me, after=()):
    n, w = arrays[0].shape
    ins = [a.reshape(count, n // count, w) for a in arrays]
    return call(
        functools.partial(add_kernel, count, me), [((n // count, w), BF16)] * count, ins, after=after,
        near_in=range(len(ins)), near_out=range(count),
    )


def to_plane(parts, n_rows, n_cols):
    return [
        send(parts[m], n_rows, n_cols, flip_row=m % n_rows, flip_col=2 * (m // n_rows)) for m in range(1, 2 * n_rows)
    ]


def to_line(parts, n_rows, n_cols):
    return [send(parts[m], n_rows, n_cols, flip_col=4 * m) for m in range(1, n_cols // 4)]


def gather_all(part, n_rows, n_cols):
    block = jnp.stack([part] + to_line([part] * (n_cols // 4), n_rows, n_cols))
    blocks = [block] + to_plane([block] * (2 * n_rows), n_rows, n_cols)
    return blocks + [send(b, n_rows, n_cols, flip_col=1) for b in blocks]


def each_part(n_rows, n_cols):
    core = lax.axis_index("col") & 1
    plane, line = plane_spot(), line_spot()
    for c in range(2):
        for m in range(2 * n_rows):
            for n in range(n_cols // 4):
                yield c, m, n, jnp.bitwise_xor(core, c), jnp.bitwise_xor(plane, m), jnp.bitwise_xor(line, n)


def assemble(mesh_shape, blocks, whole):
    n_rows, n_cols = mesh_shape
    for c, m, n, ac, am, an in each_part(n_rows, n_cols):
        at = (ac * 2 * n_rows + am) * (n_cols // 4) + an
        whole[at] = blocks[c * 2 * n_rows + m][n, 0 : whole.shape[1], :].astype(F32)
    return whole[...].reshape(whole.shape[0] * whole.shape[1], whole.shape[2])


def first_out_kernel(mesh_shape, *refs):
    blocks = refs[: 4 * mesh_shape[0]]
    ret_ref, hid_ref, out_ref, read_ref, rb_ref, hb_ref, ob_ref, lb_ref, whole = refs[4 * mesh_shape[0] :]
    flat = assemble(mesh_shape, blocks, whole)
    width = flat.shape[1]
    hidden = ret_ref.shape[0]
    ret_ref[...] = flat[0:hidden]
    for n in range(hidden // width):
        hid_ref[:, n * width : (n + 1) * width] = flat[hidden + n * width : hidden + (n + 1) * width]
    out_ref[...] = flat[2 * hidden : 2 * hidden + width]
    at = 2 * hidden + width
    small = flat[at : at + 24]
    read_ref[...] = small[0:16]
    rb_ref[...] = small[16]
    for n in range(hidden // width):
        hb_ref[n * width : (n + 1) * width] = small[17 + n]
    ob_ref[...] = small[21]
    lb_ref[...] = small[22, 0:16]


def second_out_kernel(mesh_shape, *refs):
    blocks = refs[: 4 * mesh_shape[0]]
    att_ref, qb_ref, vb_ref, whole = refs[4 * mesh_shape[0] :]
    flat = assemble(mesh_shape, blocks, whole)
    width = flat.shape[1]
    for n in range(3):
        att_ref[:, n * width : (n + 1) * width] = flat[n * width : (n + 1) * width]
    small = flat[3 * width : 3 * width + 8]
    qb_ref[...] = small[0]
    vb_ref[...] = small[1]


def condition_kernel(mesh_shape, ni, *refs):
    n_rows, n_cols = mesh_shape
    main_blocks, back_blocks = refs[: 4 * n_rows], refs[4 * n_rows : 8 * n_rows]
    (tl_ref, feat_ref, pre_ref, cond_ref, act_ref, mw_ref, fw_ref, cw_ref, mod_ref, fin_ref, table_ref, clock_ref, time_ref,
     mb_ref, fb_ref, cb_ref, tb_ref, patch_ref, pb_ref, rows_s, dev_s, patch_s) = refs[8 * n_rows :]
    width = cw_ref.shape[0]
    items = tl_ref.shape[1]
    ids = jnp.zeros((16, width), F32)
    for c, m, n, ac, am, an in each_part(n_rows, n_cols):
        at = (ac * 2 * n_rows + am) * (n_cols // 4) + an
        part = back_blocks[c * 2 * n_rows + m][n].astype(F32)
        dev_s[at, 0 : 2 * ni] = part[0 : 2 * ni]
        patch_s[at] = part[2 * ni :]
        part = main_blocks[c * 2 * n_rows + m][n].astype(F32)
        dev_s[at, 2 * ni :] = part[0 : 6 * ni]
        ids = ids + part[6 * ni :]
    patch = jnp.sum(patch_s[...], axis=0)
    patch_ref[...] = patch[0:16]
    pb_ref[...] = patch[16]
    count = n_rows * n_cols
    numbers = ids[0:8] * 256.0 + ids[8:16]
    number = jnp.concatenate([numbers[k : k + 1, :] for k in range(-(-count * ni // width))], axis=1)[:, : count * ni]
    pick = one(iota((items, count * ni), 0).astype(F32) == number)
    for b in range(8):
        block = jnp.concatenate([dev_s[d, b * ni : (b + 1) * ni, :] for d in range(count)], axis=0)
        rows_s[:, b * width : (b + 1) * width] = low(mm(pick, low(block)))
    ones = jnp.ones((8, items), BF16)
    act = act_ref[...]
    d_cond = jnp.zeros((items, width), F32)
    for b in range(8):
        grad = rows_s[:, b * width : (b + 1) * width]
        total = mm(ones, grad)[0]
        if b < 6:
            mb_ref[b * width : (b + 1) * width] = total
            mod_ref[:, b * width : (b + 1) * width] = t_mm(act, grad)
            d_cond = d_cond + mm_t(grad, mw_ref[:, b * width : (b + 1) * width])
        else:
            fb_ref[(b - 6) * width : (b - 5) * width] = total
            fin_ref[:, (b - 6) * width : (b - 5) * width] = t_mm(act, grad)
            d_cond = d_cond + mm_t(grad, fw_ref[:, (b - 6) * width : (b - 5) * width])
    cond = cond_ref[...]
    sigma = sigmoid(cond)
    d_cond = low(d_cond * (sigma * (1.0 + cond * (1.0 - sigma))))
    pre = pre_ref[...]
    sigma = sigmoid(pre)
    hidden = low(pre * sigma)
    classes = table_ref.shape[0]
    table_ref[...] = mm(one(iota((classes, items), 0) == tl_ref[1:2, :]), d_cond)
    clock_ref[...] = t_mm(hidden, d_cond)
    cb_ref[...] = mm(ones, d_cond)[0]
    d_time = low(mm_t(d_cond, cw_ref[...]) * (sigma * (1.0 + pre * (1.0 - sigma))))
    time_ref[...] = mm(feat_ref[...], d_time)
    tb_ref[...] = mm(ones, d_time)[0]


def local(
    latent, cotangent, item_ids, positions, gap_mask, timesteps, labels, patch_weight, patch_bias, time_weight,
    time_bias, clock_weight, clock_bias, class_table, modulation_weight, modulation_bias, attention_weight, query_bias,
    value_bias, output_weight, output_bias, hidden_weight, hidden_bias, return_weight, return_bias, final_modulation,
    final_offsets, readout_weight, readout_bias,
):
    n_rows, n_cols = lax.axis_size("row"), lax.axis_size("col")
    row_count, col_count = item_ids.shape
    width = patch_weight.shape[1]
    hidden = hidden_weight.shape[1]
    hp = n_rows * row_count
    cw = col_count // n_rows
    tokens = (cw + HALO) * hp
    ni = 2 * (-(-cw // LEAST))
    items = -(-(timesteps.shape[0] + 16) // 32) * 32
    unit = 8 * n_rows * n_cols
    rows_1 = -(-(2 * hidden + width + 128) // unit) * unit
    rows_2 = -(-(3 * width + 128) // unit) * unit
    pairs = width // 128

    tile, first_cols, last_cols = call(
        tile_kernel,
        [((col_count, 384), BF16), ((RIGHT, 384), BF16), ((LEFT, 384), BF16)],
        [latent, cotangent, item_ids, positions, gap_mask],
    )

    def shift(value, step_row, step_col, wanted):
        route = [
            (i * n_cols + j, (i + step_row) % n_rows * n_cols + j + step_col)
            for i in range(n_rows)
            for j in range(n_cols)
            if 0 <= j + step_col < n_cols and wanted((i + step_row) % n_rows)
        ]
        return lax.ppermute(value, ("row", "col"), route)

    left = shift(last_cols, 0, 1, lambda i: i == 0)
    tiles = [shift(tile, k, 0, lambda i: True) for k in range(1, n_rows)]
    rights = [shift(first_cols, k, -1, lambda i: (i + 1) * cw + HALO + 1 > col_count) for k in range(n_rows)]

    tl, feat, time_pre, condition, cond_act, table = call(
        item_kernel,
        [((8, items), jnp.int32), ((time_weight.shape[0], items), BF16), ((items, width), F32), ((items, width), F32),
         ((items, width), BF16), ((4 * POSITIONS, width), BF16)],
        [timesteps, labels, time_weight, time_bias, clock_weight, clock_bias, class_table],
        us=5,
    )

    dims = (n_rows, hp, cw, tokens, ni, rows_1 // 2)
    heads = ((pairs, tokens, 128), BF16)
    ins = [tile, left, *tiles, *rights, cond_act, table, patch_bias, modulation_bias, query_bias, value_bias, output_bias,
           hidden_bias, return_bias, final_offsets, readout_bias, patch_weight, modulation_weight, final_modulation,
           attention_weight, output_weight, hidden_weight, return_weight, readout_weight.T]
    q, k, v, d_at, rows, aux, res, mid, attn_in, patches, member, spread, velocity, item_main, keep, out = call(
        functools.partial(main_kernel, dims),
        [heads, heads, heads, heads, ((8, tokens), F32), ((tokens, 128), F32), ((tokens, width), F32),
         ((tokens, width), F32), ((tokens, width), BF16), ((tokens, 128), BF16), ((tokens, 128), BF16),
         ((128, 8 * width), BF16), ((tokens, 128), BF16), ((6 * ni + 16, width), BF16),
         ((rows_1 // 2, width), BF16), ((rows_1 // 2, width), BF16)],
        ins,
        [((n_rows, LEFT + 64 + RIGHT, 384), BF16), ((tokens, 128), BF16), ((pairs, tokens, 128), BF16),
         ((tokens, width), BF16), ((tokens, hidden), BF16), ((tokens, hidden), BF16), ((tokens, width), BF16),
         ((tokens, width), BF16), ((tokens, width), BF16), ((BLOCK, hidden), F32), ((16, 8 * width), F32),
         ((128, width), F32), ((2, rows_1 // 2, width), BF16)],
        us=35, room=44, near_out=range(16), near_in=(),
    )
    shape = (n_rows, n_cols)
    lines = n_cols // 4
    got = send(out, *shape, flip_col=1)
    line_main = to_line([item_main] * lines, *shape)

    def attend_back(first, count, after):
        part = ((count, tokens, 128), BF16)
        total = ((count, tokens, 128), F32)
        return call(
            functools.partial(attend_back_kernel, hp, first), [part] * 3, [q, k, v, d_at, rows, aux], [total] * 2,
            after=after, us=5 * count, room=24, near_in=range(6), near_out=range(3),
        )

    d_first = attend_back(0, 1, [])
    parts = add_up([keep, got], 2 * n_rows, plane_spot, after=[d_first[0]])
    got = to_plane(parts, *shape)
    d_heads = [*d_first, *attend_back(1, pairs - 1, [parts[0]])]
    keep_2, out_2 = call(
        functools.partial(attention_weight_kernel, rows_2 // 2),
        [((rows_2 // 2, width), BF16)] * 2,
        [attn_in, *d_heads],
        [((128, width), F32), ((2, rows_2 // 2, width), BF16)],
        us=4, room=24, near_in=range(7), near_out=range(2),
    )
    got_2 = send(out_2, *shape, flip_col=1)
    block_main = jnp.stack([item_main] + line_main)
    plane_main = [block_main] + to_plane([block_main] * (2 * n_rows), *shape)
    dims = (n_rows, hp, cw, tokens, ni)
    result = call(
        functools.partial(back_kernel, dims),
        [((2 * ni + 24, width), BF16)] + [((64, 256), BF16)] * n_rows + [((RIGHT, 256), BF16)] * n_rows,
        [*d_heads, res, mid, patches, member, spread, velocity, attention_weight, patch_weight],
        [((tokens, width), BF16), ((16, 2 * width), F32), ((n_rows, 64 + RIGHT, 256), F32)],
        us=8, after=[keep_2], room=24, near_in=range(12), near_out=range(5),
    )
    item_back = result[0]
    mine, over = result[1 : 1 + n_rows], result[1 + n_rows :]
    parts_2 = add_up([keep_2, got_2], 2 * n_rows, plane_spot, after=[item_back])
    got_2 = to_plane(parts_2, *shape)
    parts = add_up([parts[0]] + got, lines, line_spot, after=[parts_2[0]])
    got = to_line(parts, *shape)
    blocks_back = gather_all(item_back, *shape)

    mine = [mine[0]] + [shift(mine[k], k, 0, lambda i: True) for k in range(1, n_rows)]
    over = [shift(over[k], k, 1, lambda i: True) for k in range(n_rows)]

    share_1, share_2 = rows_1 // (n_rows * n_cols), rows_2 // (n_rows * n_cols)
    parts_2 = add_up([parts_2[0]] + got_2, lines, line_spot, after=[parts[0]])
    got_2 = to_line(parts_2, *shape)
    (part,) = add_up([parts[0]] + got, 1, line_spot, after=[parts_2[0]])
    blocks = gather_all(part.reshape(share_1, width), *shape)
    (part_2,) = add_up([parts_2[0]] + got_2, 1, line_spot, after=[part])
    blocks_2 = gather_all(part_2.reshape(share_2, width), *shape)
    blocks_main = plane_main + [send(b, *shape, flip_col=1) for b in plane_main]

    velocity, latent_grad = call(
        functools.partial(canvas_kernel, n_rows), [(latent.shape, BF16), (latent.shape, F32)], [*mine, *over],
        near_in=range(2 * n_rows),
    )
    devices = n_rows * n_cols
    vector = ((width,), F32)
    return_grad, hidden_grad, output_grad, readout_grad, return_b, hidden_b, output_b, readout_b = call(
        functools.partial(first_out_kernel, shape),
        [((hidden, width), F32), ((width, hidden), F32), ((width, width), F32), ((16, width), F32), vector,
         ((hidden,), F32), vector, ((16,), F32)],
        blocks,
        [((devices, share_1, width), F32)],
        us=5, room=32, near_in=range(4 * n_rows),
    )
    (modulation_grad, final_grad, table_grad, clock_grad, time_grad, modulation_b, final_b, clock_b, time_b, patch_grad,
     patch_b) = call(
        functools.partial(condition_kernel, shape, ni),
        [((width, 6 * width), F32), ((width, 2 * width), F32), (class_table.shape, F32), ((width, width), F32),
         (time_weight.shape, F32), ((6 * width,), F32), ((2 * width,), F32), vector, vector, ((16, width), F32), vector],
        [*blocks_main, *blocks_back, tl, feat, time_pre, condition, cond_act, modulation_weight, final_modulation,
         clock_weight],
        [((items, 8 * width), BF16), ((devices, 8 * ni, width), F32), ((devices, 24, width), F32)],
        us=10, room=40, near_in=range(8 * n_rows),
    )
    attention_grad, query_b, value_b = call(
        functools.partial(second_out_kernel, shape),
        [((width, 3 * width), F32), vector, vector],
        blocks_2,
        [((devices, share_2, width), F32)],
        near_in=range(4 * n_rows),
    )
    return (
        velocity, latent_grad, patch_grad, patch_b, time_grad, time_b, clock_grad, clock_b, table_grad, modulation_grad,
        modulation_b, attention_grad, query_b, value_b, output_grad, output_b, hidden_grad, hidden_b, return_grad,
        return_b, final_grad, final_b, readout_grad.T, readout_b,
    )


def solution(mesh):
    canvas, grid = P(None, "row", "col"), P("row", "col")
    return jax.shard_map(
        local,
        mesh=mesh,
        in_specs=(canvas, canvas, grid, canvas, grid) + (P(),) * 24,
        out_specs=(canvas, canvas) + (P(),) * 22,
        check_vma=False,
    )
```

```python
import functools
import math

import jax
import jax.numpy as jnp
from jax import lax
from jax.experimental import pallas as pl
from jax.experimental.pallas import tpu as pltpu
from jax.sharding import PartitionSpec as P

HEADS = 6
HALO = 16
LEAST = 8
BLOCK = 256
LEFT = 16
RIGHT = 32
POSITIONS = 128
F32 = jnp.float32
BF16 = jnp.bfloat16
FLOPS_US = 1_150_000_000
BYTES_US = 3_700_000


def iota(shape, dim):
    return lax.broadcasted_iota(jnp.int32, shape, dim)


def mm(a, b):
    return jnp.dot(a, b, preferred_element_type=F32)


def mm_t(a, b):
    return lax.dot_general(a, b, (((1,), (1,)), ((), ())), preferred_element_type=F32)


def t_mm(a, b):
    return lax.dot_general(a, b, (((0,), (0,)), ((), ())), preferred_element_type=F32)


def low(v):
    return v.astype(BF16)


def one(cond):
    return jnp.where(cond, 1.0, 0.0).astype(BF16)


def sigmoid(v):
    return 1.0 / (1.0 + jnp.exp(-v))


def layer_norm(v):
    center = v - jnp.mean(v, axis=-1, keepdims=True)
    inverse = lax.rsqrt(jnp.mean(center * center, axis=-1, keepdims=True) + 1e-06)
    return center * inverse, inverse


def norm_back(normed, inverse, grad):
    mean_grad = jnp.mean(grad, axis=-1, keepdims=True)
    mean_cross = jnp.mean(grad * normed, axis=-1, keepdims=True)
    return inverse * (grad - mean_grad - normed * mean_cross)


def call(body, outs, ins, scratch=(), near_in=(), near_out=(), after=(), us=2, room=16):
    spec = pl.BlockSpec(memory_space=pltpu.VMEM)
    used = len(ins)

    def run(*refs):
        body(*refs[:used], *refs[used + len(after) :])

    ins = [pltpu.with_memory_space_constraint(a, pltpu.VMEM) if n in near_in else a for n, a in enumerate(ins)]
    return pl.pallas_call(
        run,
        out_shape=[
            (pltpu.VMEM if n in near_out else jax.ShapeDtypeStruct)(shape, dtype)
            for n, (shape, dtype) in enumerate(outs)
        ],
        in_specs=[spec] * used + [pl.BlockSpec(memory_space=pl.ANY)] * len(after),
        out_specs=[spec] * len(outs),
        scratch_shapes=[pltpu.VMEM(shape, dtype) for shape, dtype in scratch],
        compiler_params=pltpu.CompilerParams(vmem_limit_bytes=room * 1024 * 1024),
        cost_estimate=pl.CostEstimate(flops=us * FLOPS_US, bytes_accessed=us * BYTES_US, transcendentals=0),
    )(*ins, *after)


def line(ref, start=0, count=None):
    count = ref.shape[0] if count is None else count
    return ref[start : start + count].astype(F32).reshape(1, count)


def lane_fold(rows):
    lane = iota((rows, 128), 1)
    feature = 8 * (1 - (lane & 1)) + 4 * (1 - (lane >> 6)) + ((lane >> 4) & 3)
    return one(iota((rows, 128), 0) == feature)


def tile_kernel(lat_ref, cot_ref, ids_ref, pos_ref, gap_ref, tile_ref, first_ref, last_ref):
    cols = ids_ref.shape[1]
    pieces = []
    for ref in (lat_ref, cot_ref):
        flat = ref[...].reshape(64, 2 * cols)
        for side in (0, 1):
            pick = one(iota((cols, 2 * cols), 1) == 2 * iota((cols, 2 * cols), 0) + side)
            pieces.append(mm_t(pick, flat))
    tag = ids_ref[...] + 1
    meta = jnp.concatenate(
        [tag >> 8, tag & 255, pos_ref[0], pos_ref[1], gap_ref[...], jnp.zeros((88, cols), jnp.int32)], axis=0
    ).astype(F32)
    pieces.append(mm_t(one(iota((cols, cols), 0) == iota((cols, cols), 1)), low(meta)))
    tile = low(jnp.concatenate(pieces, axis=1))
    tile_ref[...] = tile
    first_ref[...] = tile[:RIGHT]
    last_ref[...] = tile[cols - LEFT :]


def item_kernel(
    steps_ref, labels_ref, tw_ref, tb_ref, cw_ref, cb_ref, ct_ref, tl_ref, feat_ref, pre_ref, cond_ref, act_ref, table_ref
):
    items = tl_ref.shape[1]
    count = steps_ref.shape[0]
    tl_ref[...] = jnp.zeros_like(tl_ref)
    tl_ref[0:1, 0:count] = steps_ref[...].reshape(1, count)
    tl_ref[1:2, 0:count] = labels_ref[...].reshape(1, count)
    half = tw_ref.shape[0] // 2
    steps = tl_ref[0:1, :].astype(F32)
    freq = jnp.exp(iota((half, 1), 0).astype(F32) * (-math.log(10000.0) / half))
    angle = freq * steps
    feat_ref[0:half, :] = low(jnp.cos(angle))
    feat_ref[half:, :] = low(jnp.sin(angle))
    pre = t_mm(feat_ref[...], tw_ref[...]) + line(tb_ref)
    pre_ref[...] = pre
    hidden = low(pre * sigmoid(pre))
    classes = ct_ref.shape[0]
    pick = one(iota((classes, items), 0) == tl_ref[1:2, :])
    cond = mm(hidden, cw_ref[...]) + line(cb_ref) + t_mm(pick, ct_ref[...])
    cond_ref[...] = cond
    act_ref[...] = low(cond * sigmoid(cond))
    width = table_ref.shape[1]
    quarter = width // 4
    shape = (2 * POSITIONS, width)
    lane = iota(shape, 1)
    row = iota(shape, 0)
    second = lane >= 2 * quarter
    within = jnp.where(second, lane - 2 * quarter, lane)
    cosine = within >= quarter
    index = jnp.where(cosine, within - quarter, within)
    omega = jnp.exp(index.astype(F32) * (-math.log(10000.0) / quarter))
    angle = (row & (POSITIONS - 1)).astype(F32) * omega
    value = jnp.where(cosine, jnp.cos(angle), jnp.sin(angle))
    value = jnp.where(jnp.where(second, 1, 0) == jnp.where(row >= POSITIONS, 1, 0), value, 0.0)
    high = low(value)
    table_ref[0 : 2 * POSITIONS, :] = high
    table_ref[2 * POSITIONS :, :] = low(value - high.astype(F32))


def row_mask(q, i, shape):
    return ((q * 16 + (iota(shape, 1) & 15) - 1) >> 1) == i


def main_kernel(dims, *refs):
    n_rows, hp, cw, tokens, ni, half_rows = dims
    own_ref, left_ref = refs[0:2]
    tiles = refs[2 : 1 + n_rows]
    rights = refs[1 + n_rows : 1 + 2 * n_rows]
    (act_ref, table_ref, pb_ref, mb_ref, qb_ref, vb_ref, ob_ref, hb_ref, rb_ref, fb_ref, lb_ref,
     pw_ref, mw_ref, fw_ref, aw_ref, ow_ref, hw_ref, rw_ref, low_ref,
     q_ref, k_ref, v_ref, da_ref, rows_ref, aux_ref, res_ref, mid_ref, in_ref, x_ref, mem_ref, ms_ref, vel_ref,
     item_ref, keep_ref, send_ref,
     es, ct_s, at_s, mlp_s, ha_s, dh_s, dbm_s, dba_s, ri_s, gd_s, dacc, small, g_s) = refs[1 + 2 * n_rows :]
    width = res_ref.shape[1]
    pairs = width // 128
    r = lax.axis_index("row")
    core = lax.axis_index("col") & 1
    shift = int(math.log2(hp))

    es[...] = jnp.zeros_like(es)
    es[r, LEFT : LEFT + 64, :] = own_ref[...]
    es[r, 0:LEFT, :] = left_ref[...]
    for k in range(1, n_rows):
        es[lax.rem(r - k + n_rows, n_rows), LEFT : LEFT + 64, :] = tiles[k - 1][...]
    for k in range(n_rows):
        es[lax.rem(r - k + n_rows, n_rows), LEFT + 64 :, :] = rights[k][...]
    meta = es[r, :, 256:384].astype(F32)
    lane = iota(meta.shape, 1)
    weighted = meta * jnp.where(lane == 0, 256.0, jnp.where(lane == 8, 1.0, 0.0))
    down = iota(meta.shape, 0)
    start = LEFT + r * cw
    tag_prev = jnp.sum(jnp.where(down == start - 1, weighted, 0.0)).astype(jnp.int32)
    tag_last = jnp.sum(jnp.where(down == start + cw - 1, weighted, 0.0)).astype(jnp.int32)
    tag_first = jnp.sum(jnp.where(down == start, weighted, 0.0)).astype(jnp.int32)
    strip_prev = jnp.where(tag_prev == 0, ((tag_first - 1) >> 1) - 1, (tag_prev - 1) >> 1)
    strip_last = (tag_last - 1) >> 1
    base = 2 * (strip_prev + 1)

    pick = one(iota((16, act_ref.shape[0]), 1) == base + iota((16, act_ref.shape[0]), 0))
    own_act = low(mm(pick, act_ref[...]))
    ms_ref[48:, :] = jnp.zeros_like(ms_ref[48:, :])
    for b in range(8):
        cols = slice(b * width, (b + 1) * width)
        if b < 6:
            value = mm(own_act, mw_ref[:, cols]) + line(mb_ref, b * width, width)
        else:
            value = mm(own_act, fw_ref[:, (b - 6) * width : (b - 5) * width]) + line(fb_ref, (b - 6) * width, width)
        p0 = low(value)
        rest = value - p0.astype(F32)
        p1 = low(rest)
        ms_ref[0:16, cols] = p0
        ms_ref[16:32, cols] = p1
        ms_ref[32:48, cols] = low(rest - p1.astype(F32))

    def mod(mem, b, n=1):
        return mm(mem, ms_ref[:, b * width : (b + n) * width])

    fold = lane_fold(16)
    embed = low(t_mm(fold, pw_ref[...]))
    unread = low(t_mm(low_ref[...], fold))
    b_lanes = iota((BLOCK, 128), 1)
    is_b1 = b_lanes >= 64
    half_lanes = (one(b_lanes < 64), one(is_b1))

    def first(tb, carry):
        t0 = pl.multiple_of(tb * BLOCK, BLOCK)
        rows = pl.ds(t0, BLOCK)
        token = t0 + iota((BLOCK, 1), 0)
        j = token >> shift
        i = token & (hp - 1)
        spot = iota((BLOCK, LEFT + 64 + RIGHT), 1)
        rep0 = one(spot == start + j)
        rep1 = one(spot == start + j + 1)
        x = jnp.zeros((BLOCK, 128), F32)
        c = jnp.zeros((BLOCK, 128), F32)
        m = jnp.zeros((BLOCK, 128), F32)
        for q in range(n_rows):
            here = mm(rep0, es[q])
            beside = mm(rep1, es[q, :, 0:256])
            mask = row_mask(q, i, (BLOCK, 128))
            x = x + jnp.where(mask, jnp.where(is_b1, here[:, 0:128], beside[:, 0:128]), 0.0)
            c = c + jnp.where(mask, jnp.where(is_b1, here[:, 128:256], beside[:, 128:256]), 0.0)
            m = m + jnp.where((q * 8 + (b_lanes & 7)) == i, here[:, 256:384], 0.0)
        x = low(x)
        m = low(m)
        x_ref[rows, :] = x
        ml = iota((128, 128), 0)
        mc = iota((128, 128), 1)
        kind = ml >> 3
        gather = jnp.where(
            (mc == 0) & (kind == 0), 256.0,
            jnp.where(((mc == 0) & (kind == 1)) | ((mc >= 1) & (mc <= 3) & (kind == mc + 1)), 1.0, 0.0),
        ).astype(BF16)
        cols = mm(m, gather)
        rl = iota((8, 128), 1) >> 3
        rr = iota((8, 128), 0)
        row_pick = jnp.where((rr == 6) & (rl == 0), 256.0, jnp.where((rr == 6) & (rl == 1), 1.0, 0.0)).astype(BF16)
        rows_ref[:, rows] = mm_t(row_pick, m)
        tag = cols[:, 0:1]
        gap = cols[:, 3:4]
        tag_i = tag.astype(jnp.int32)
        strip = (tag_i - 1) >> 1
        owned = (strip > strip_prev) & (strip <= strip_last)
        act = jnp.where(owned, gap, 0.0)
        aux_ref[rows, :] = jnp.where(b_lanes == 0, tag * gap, jnp.where(b_lanes == 1, act, 0.0))
        item = tag_i - 1 - base
        mem = one((item == (b_lanes & 15)) & (b_lanes < 48) & owned)
        mem_ref[rows, :] = mem
        ct_s[rows, :] = low(c * act)
        p0 = cols[:, 1:2].astype(jnp.int32)
        p1 = cols[:, 2:3].astype(jnp.int32) + POSITIONS
        spot = iota((BLOCK, 2 * POSITIONS), 1)
        place = one((spot == p0) | (spot == p1))
        res = (
            mm(x, embed) + line(pb_ref)
            + (mm(place, table_ref[0 : 2 * POSITIONS, :]) + mm(place, table_ref[2 * POSITIONS :, :]))
        )
        res_ref[rows, :] = res
        normed, _ = layer_norm(res)
        ab = mod(mem, 0, 2)
        attn_in = low(normed * (1.0 + ab[:, width:]) + ab[:, :width])
        in_ref[rows, :] = attn_in
        for part, ref in enumerate((q_ref, k_ref, v_ref)):
            value = mm(attn_in, aw_ref[:, part * width : (part + 1) * width])
            if part != 1:
                value = value + line(vb_ref if part else qb_ref)
            value = low(value)
            if part == 0:
                value = value * BF16(1.0 / math.sqrt(width // HEADS))
            for p in range(pairs):
                ref[p, rows, :] = value[:, p * 128 : (p + 1) * 128]
        return carry

    lax.fori_loop(0, tokens // BLOCK, first, 0)

    for qb in range(tokens // BLOCK):
        qs = slice(qb * BLOCK, (qb + 1) * BLOCK)
        ks = key_range(qb, hp, tokens)
        q_tag = rows_ref[6:7, qs]
        k_tag = aux_ref[ks, 0:1]
        allowed = k_tag == q_tag
        for p in range(pairs):
            query = q_ref[p, qs, :]
            key = k_ref[p, ks, :]
            value = v_ref[p, ks, :]
            halves = []
            for e in range(2):
                scores = jnp.where(allowed, mm_t(key, query * half_lanes[e]), -1e30)
                top = jnp.max(scores, axis=0, keepdims=True)
                expo = jnp.exp(scores - top)
                total = jnp.sum(expo, axis=0, keepdims=True)
                rows_ref[2 * p + e : 2 * p + e + 1, qs] = top + jnp.log(total)
                halves.append(t_mm(low(expo * (1.0 / total)), value))
            at_s[p, qs, :] = low(jnp.where(is_b1, halves[1], halves[0]))

    dacc[...] = jnp.zeros_like(dacc)

    def second(tb, carry):
        t0 = pl.multiple_of(tb * BLOCK, BLOCK)
        rows = pl.ds(t0, BLOCK)
        mem = mem_ref[rows, :]

        def item_sum(b, grad):
            dacc[:, b * width : (b + 1) * width] += t_mm(mem, low(grad))[0:16, :]

        attended = jnp.concatenate([at_s[p, rows, :] for p in range(pairs)], axis=1)
        branch_a = mm(attended, ow_ref[...]) + line(ob_ref)
        gate_a = mod(mem, 2)
        mid = res_ref[rows, :] + gate_a * branch_a
        norm_mid, inv_mid = layer_norm(mid)
        scale_m = 1.0 + mod(mem, 4)
        mlp_in = low(norm_mid * scale_m + mod(mem, 3))
        mlp_s[rows, :] = mlp_in
        hidden = hw_ref.shape[1]
        branch_m = jnp.zeros((BLOCK, width), F32)
        for n in range(hidden // width):
            part = slice(n * width, (n + 1) * width)
            pre = mm(mlp_in, hw_ref[:, part]) + line(hb_ref, n * width, width)
            square = pre * pre
            c0 = math.sqrt(2.0 / math.pi)
            t = jnp.tanh(pre * (c0 + (c0 * 0.044715) * square))
            up = 0.5 + 0.5 * t
            act = low(pre * up)
            gd_s[:, part] = up + (0.5 * pre) * (1.0 - t * t) * (c0 + (3.0 * c0 * 0.044715) * square)
            ha_s[rows, part] = act
            branch_m = branch_m + mm(act, rw_ref[part, :])
        branch_m = branch_m + line(rb_ref)
        gate_m = mod(mem, 5)
        norm_out, inv_out = layer_norm(mid + gate_m * branch_m)
        scale_f = 1.0 + mod(mem, 7)
        readout_in = low(norm_out * scale_f + mod(mem, 6))
        ri_s[rows, :] = readout_in
        active = aux_ref[rows, 1:2]
        bias_lanes = mm(low(line(lb_ref) + jnp.zeros((8, 16), F32)), fold)[0:1, :]
        vel_ref[rows, :] = low((mm(readout_in, unread) + bias_lanes) * active)
        d_read = mm_t(ct_s[rows, :], unread)
        item_sum(6, d_read)
        item_sum(7, d_read * norm_out)
        d_out = norm_back(norm_out, inv_out, d_read * scale_f)
        item_sum(5, d_out * branch_m)
        d_bm = low(d_out * gate_m)
        dbm_s[rows, :] = d_bm
        d_mlp = jnp.zeros((BLOCK, width), F32)
        for n in range(hidden // width):
            part = slice(n * width, (n + 1) * width)
            d_hid = low(mm_t(d_bm, rw_ref[part, :]) * gd_s[:, part])
            dh_s[rows, part] = d_hid
            d_mlp = d_mlp + mm_t(d_hid, hw_ref[:, part])
        item_sum(3, d_mlp)
        item_sum(4, d_mlp * norm_mid)
        d_mid = d_out + norm_back(norm_mid, inv_mid, d_mlp * scale_m)
        mid_ref[rows, :] = d_mid
        item_sum(2, d_mid * branch_a)
        d_ba = low(d_mid * gate_a)
        dba_s[rows, :] = d_ba
        d_at = low(mm_t(d_ba, ow_ref[...]))
        for p in range(pairs):
            da_ref[p, rows, :] = d_at[:, p * 128 : (p + 1) * 128]
        return carry

    lax.fori_loop(0, tokens // BLOCK, second, 0)
    rows = [dacc[0:ni, b * width : (b + 1) * width] for b in range(2, 8)]
    spot = ((core * 2 * n_rows + plane_spot()) * (lax.axis_size("col") // 4) + line_spot()) * ni
    index = iota((8, width), 0) * width + iota((8, width), 1) - spot
    number = jnp.where((index >= 0) & (index < ni), base + index, 0)
    rows += [(number >> 8).astype(F32), (number & 255).astype(F32)]
    item_ref[...] = low(jnp.concatenate(rows, axis=0))

    g_s[...] = jnp.zeros_like(g_s)
    put = functools.partial(put_rows, g_s, half_rows)
    n_hidden = hw_ref.shape[1] // width
    for n in range(n_hidden):
        part = slice(n * width, (n + 1) * width)
        put(n * width, low(t_mm(ha_s[:, part], dbm_s[...])))
        put((n_hidden + n) * width, low(t_mm(mlp_s[...], dh_s[:, part])))
    attended = jnp.concatenate([at_s[p] for p in range(pairs)], axis=1)
    put(2 * n_hidden * width, low(t_mm(attended, dba_s[...])))
    ones = jnp.ones((8, tokens), BF16)
    small[...] = jnp.zeros_like(small)
    small[0:16, :] = mm(fold, low(t_mm(ct_s[...], ri_s[...])))
    small[16:17, :] = mm(ones, dbm_s[...])[0:1, :]
    for n in range(n_hidden):
        small[17 + n : 18 + n, :] = mm(ones, dh_s[:, n * width : (n + 1) * width])[0:1, :]
    small[21:22, :] = mm(ones, dba_s[...])[0:1, :]
    sums = mm(ones, ct_s[...])
    small[22:23, 0:128] = mm_t(jnp.broadcast_to(low(sums[0:1, :]), (8, 128)), lane_fold(128))[0:1, :]
    put((2 * n_hidden + 1) * width, low(small[...]))
    keep_ref[...] = g_s[core]
    send_ref[...] = g_s[1 - core]


def put_rows(g_s, half_rows, row, value):
    count = value.shape[0]
    done = 0
    while done < count:
        side, at = divmod(row + done, half_rows)
        take = min(count - done, half_rows - at)
        g_s[side, at : at + take, :] = value[done : done + take, :]
        done += take


def key_range(qb, hp, tokens):
    first_col = (qb * BLOCK) // hp
    last_col = ((qb + 1) * BLOCK - 1) // hp
    return slice(max(0, first_col - HALO) * hp, min(tokens, (last_col + 1 + HALO) * hp))


def attend_back_kernel(hp, first, q_ref, k_ref, v_ref, da_ref, rows_ref, aux_ref, dq_ref, dk_ref, dv_ref, dk_s, dv_s):
    tokens = q_ref.shape[1]
    b_lanes = iota((BLOCK, 128), 1)
    is_b1 = b_lanes >= 64
    half_lanes = (one(b_lanes < 64), one(is_b1))
    scale = 1.0 / math.sqrt(q_ref.shape[0] * 128 // HEADS)
    dk_s[...] = jnp.zeros_like(dk_s)
    dv_s[...] = jnp.zeros_like(dv_s)
    for qb in range(tokens // BLOCK):
        qs = slice(qb * BLOCK, (qb + 1) * BLOCK)
        ks = key_range(qb, hp, tokens)
        allowed = aux_ref[ks, 0:1] == rows_ref[6:7, qs]
        for n in range(dq_ref.shape[0]):
            p = first + n
            query = q_ref[p, qs, :]
            key = k_ref[p, ks, :]
            value = v_ref[p, ks, :]
            d_at = da_ref[p, qs, :]
            d_key = 0.0
            d_value = 0.0
            halves = []
            for e in range(2):
                q_half = query * half_lanes[e]
                d_half = d_at * half_lanes[e]
                scores = jnp.where(allowed, mm_t(key, q_half), -1e30)
                probs = jnp.exp(scores - rows_ref[2 * p + e : 2 * p + e + 1, qs])
                d_probs = mm_t(value, d_half)
                inner = jnp.sum(probs * d_probs, axis=0, keepdims=True)
                d_scores = low(probs * (d_probs - inner))
                d_value = d_value + mm(low(probs), d_half)
                d_key = d_key + mm(d_scores, q_half)
                halves.append(t_mm(d_scores, key))
            dk_s[n, ks, :] += d_key
            dv_s[n, ks, :] += d_value
            dq_ref[n, qs, :] = low(jnp.where(is_b1, halves[1], halves[0]) * scale)
    dk_ref[...] = low(dk_s[...])
    dv_ref[...] = low(dv_s[...])


def joined(refs, rows):
    return jnp.concatenate(
        [ref[n, rows, :] for kind in range(3) for ref in refs[kind::3] for n in range(ref.shape[0])], axis=1
    )


def weigh_attention(half_rows, in_ref, parts, keep_ref, send_ref, small, g_s):
    tokens, width = in_ref.shape
    core = lax.axis_index("col") & 1
    put = functools.partial(put_rows, g_s, half_rows)
    ones = jnp.ones((8, tokens), BF16)
    g_s[...] = jnp.zeros_like(g_s)
    small[...] = jnp.zeros_like(small)
    whole = joined(parts, slice(None))
    for n in range(3):
        grad = whole[:, n * width : (n + 1) * width]
        put(n * width, low(t_mm(in_ref[...], grad)))
        if n != 1:
            small[n // 2 : n // 2 + 1, :] = mm(ones, grad)[0:1, :]
    put(3 * width, low(small[...]))
    keep_ref[...] = g_s[core]
    send_ref[...] = g_s[1 - core]


def back_kernel(dims, *refs):
    n_rows, hp, cw, tokens, ni, half_rows = dims
    heads, done = refs[:6], refs[6:9]
    (in_ref, res_ref, mid_ref, x_ref, mem_ref, ms_ref, vel_ref, aw_ref, pw_ref, keep_ref, send_ref, item_ref) = refs[9:21]
    mine_refs = refs[21 : 21 + n_rows]
    over_refs = refs[21 + n_rows : 21 + 2 * n_rows]
    *rest, dk_s, dv_s, small, g_s, di_s, dacc, frame = refs[21 + 2 * n_rows :]
    parts = [*done, *rest]
    attend_back_kernel(hp, done[0].shape[0], *heads, *rest, dk_s, dv_s)
    weigh_attention(half_rows, in_ref, parts, keep_ref, send_ref, small, g_s)
    width = res_ref.shape[1]
    r = lax.axis_index("row")
    shift = int(math.log2(hp))

    embed = low(t_mm(lane_fold(16), pw_ref[...]))
    dacc[...] = jnp.zeros_like(dacc)
    frame[...] = jnp.zeros_like(frame)

    def third(tb, carry):
        t0 = pl.multiple_of(tb * BLOCK, BLOCK)
        rows = pl.ds(t0, BLOCK)
        mem = mem_ref[rows, :]
        d_attn = mm_t(joined(parts, rows), aw_ref[...])
        normed, inverse = layer_norm(res_ref[rows, :])
        scale_a = 1.0 + mm(mem, ms_ref[:, width : 2 * width])
        dacc[:, 0:width] += t_mm(mem, low(d_attn))[0:16, :]
        dacc[:, width : 2 * width] += t_mm(mem, low(d_attn * normed))[0:16, :]
        d_in = low(mid_ref[rows, :] + norm_back(normed, inverse, d_attn * scale_a))
        di_s[rows, :] = d_in
        grad = low(mm_t(d_in, embed))
        both = jnp.concatenate([vel_ref[rows, :], grad], axis=1)
        token = t0 + iota((BLOCK, 1), 0)
        j = token >> shift
        i = token & (hp - 1)
        spot = iota((BLOCK, 64 + RIGHT), 1)
        rep = jnp.concatenate([one(spot == r * cw + j), one(spot == r * cw + j + 1)], axis=0)
        side = (iota((BLOCK, 256), 1) >> 6) & 1
        for q in range(n_rows):
            mask = row_mask(q, i, (BLOCK, 256))
            split = jnp.concatenate([both * one(mask & (side == 1)), both * one(mask & (side == 0))], axis=0)
            frame[q] += t_mm(rep, split)
        return carry

    lax.fori_loop(0, tokens // BLOCK, third, 0)

    ones = jnp.ones((8, tokens), BF16)
    rows = [dacc[0:ni, 0:width], dacc[0:ni, width : 2 * width]]
    rows += [mm(lane_fold(16), low(t_mm(x_ref[...], di_s[...]))), mm(ones, di_s[...])]
    item_ref[...] = low(jnp.concatenate(rows, axis=0))
    for k in range(n_rows):
        q = lax.rem(r + k, n_rows)
        whole = low(frame[q])
        mine_refs[k][...] = whole[0:64, :]
        over_refs[k][...] = whole[64:, :]


def canvas_kernel(n_rows, *refs):
    mine, over = refs[0:n_rows], refs[n_rows : 2 * n_rows]
    vel_ref, grad_ref = refs[2 * n_rows :]
    total = mine[0][...].astype(F32)
    for ref in mine[1:]:
        total = total + ref[...].astype(F32)
    extra = over[0][...].astype(F32)
    for ref in over[1:]:
        extra = extra + ref[...].astype(F32)
    total = low(total + jnp.concatenate([extra, jnp.zeros((64 - RIGHT, 256), F32)], axis=0))
    for n, ref in enumerate((vel_ref, grad_ref)):
        value = 0.0
        for side in (0, 1):
            pick = one(iota((64, 128), 1) == 2 * iota((64, 128), 0) + side)
            value = value + t_mm(total[:, n * 128 + side * 64 : n * 128 + (side + 1) * 64], pick)
        ref[...] = value.reshape(ref.shape).astype(ref.dtype)


def add_kernel(count, me, *refs):
    outs = refs[len(refs) - count :]
    ins = refs[: len(refs) - count]
    spot = me()
    for m, out in enumerate(outs):
        at = jnp.bitwise_xor(spot, m) if count > 1 else 0
        total = ins[0][at].astype(F32)
        for ref in ins[1:]:
            total = total + ref[at].astype(F32)
        out[...] = low(total)


def plane_spot():
    return lax.axis_index("row") + lax.axis_size("row") * ((lax.axis_index("col") >> 1) & 1)


def line_spot():
    return lax.axis_index("col") >> 2


def send(value, n_rows, n_cols, flip_row=0, flip_col=0):
    route = [
        (i * n_cols + j, (i ^ flip_row) * n_cols + (j ^ flip_col)) for i in range(n_rows) for j in range(n_cols)
    ]
    return lax.ppermute(value, ("row", "col"), route)


def add_up(arrays, count, me, after=()):
    n, w = arrays[0].shape
    ins = [a.reshape(count, n // count, w) for a in arrays]
    return call(
        functools.partial(add_kernel, count, me), [((n // count, w), BF16)] * count, ins, after=after,
        near_in=range(len(ins)), near_out=range(count),
    )


def add_below_kernel(*refs):
    *ins, more, out = refs
    total = ins[0][...].astype(F32)
    for ref in ins[1:]:
        total = total + ref[...].astype(F32)
    out[...] = jnp.concatenate([low(total), more[...]], axis=0)


def add_below(arrays, more, after=()):
    n, w = arrays[0].shape
    ins = [*arrays, more]
    return call(
        add_below_kernel, [((n + more.shape[0], w), BF16)], ins, after=after, near_in=range(len(ins)), near_out=(0,)
    )[0]


def line_kernel(share, *refs):
    *ins, out, rows = refs
    spot = line_spot()
    for m, ref in enumerate(ins):
        rows[jnp.bitwise_xor(spot, m)] = ref[0:share, :].astype(F32)
    more = ins[0].shape[0] - share
    out[0:share, :] = low(jnp.sum(rows[...], axis=0))
    for m, ref in enumerate(ins):
        out[share + m * more : share + (m + 1) * more, :] = ref[share:, :]


def to_plane(parts, n_rows, n_cols):
    return [
        send(parts[m], n_rows, n_cols, flip_row=m % n_rows, flip_col=2 * (m // n_rows)) for m in range(1, 2 * n_rows)
    ]


def to_line(parts, n_rows, n_cols):
    return [send(parts[m], n_rows, n_cols, flip_col=4 * m) for m in range(1, n_cols // 4)]


def stack_kernel(*refs):
    *ins, out = refs
    for n, ref in enumerate(ins):
        out[n] = ref[...]


def stack(arrays, after=()):
    return call(
        stack_kernel, [((len(arrays), *arrays[0].shape), BF16)], arrays, after=after, near_in=range(len(arrays)),
        near_out=(0,),
    )[0]


def each_plane(n_rows):
    core = lax.axis_index("col") & 1
    plane = plane_spot()
    for c in range(2):
        for m in range(2 * n_rows):
            yield c, m, jnp.bitwise_xor(core, c) * 2 * n_rows + jnp.bitwise_xor(plane, m)


def each_part(n_rows, n_cols):
    line = line_spot()
    for c, m, at in each_plane(n_rows):
        for n in range(n_cols // 4):
            yield c, m, n, at * (n_cols // 4) + jnp.bitwise_xor(line, n)


def first_out_kernel(mesh_shape, *refs):
    n_rows, n_cols = mesh_shape
    blocks = refs[:2]
    ret_ref, hid_ref, out_ref, read_ref, rb_ref, hb_ref, ob_ref, lb_ref, whole = refs[2:]
    for c, m, n, at in each_part(n_rows, n_cols):
        whole[at] = blocks[c][m, n, 0 : whole.shape[1], :].astype(F32)
    flat = whole[...].reshape(whole.shape[0] * whole.shape[1], whole.shape[2])
    width = flat.shape[1]
    hidden = ret_ref.shape[0]
    ret_ref[...] = flat[0:hidden]
    for n in range(hidden // width):
        hid_ref[:, n * width : (n + 1) * width] = flat[hidden + n * width : hidden + (n + 1) * width]
    out_ref[...] = flat[2 * hidden : 2 * hidden + width]
    at = 2 * hidden + width
    small = flat[at : at + 24]
    read_ref[...] = small[0:16]
    rb_ref[...] = small[16]
    for n in range(hidden // width):
        hb_ref[n * width : (n + 1) * width] = small[17 + n]
    ob_ref[...] = small[21]
    lb_ref[...] = small[22, 0:16]


def second_out_kernel(mesh_shape, own_ref, other_ref, att_ref, qb_ref, vb_ref, whole):
    for c, m, at in each_plane(mesh_shape[0]):
        whole[at] = (own_ref, other_ref)[c][m, 0 : whole.shape[1], :].astype(F32)
    flat = whole[...].reshape(whole.shape[0] * whole.shape[1], whole.shape[2])
    width = flat.shape[1]
    for n in range(3):
        att_ref[:, n * width : (n + 1) * width] = flat[n * width : (n + 1) * width]
    small = flat[3 * width : 3 * width + 8]
    qb_ref[...] = small[0]
    vb_ref[...] = small[1]


def item_condition_kernel(
    mesh_shape, ni, above, own_ref, other_ref, tl_ref, act_ref, mw_ref, fw_ref,
    mod_ref, fin_ref, mb_ref, fb_ref, cond_ref, pick_ref, dev_s,
):
    n_rows, n_cols = mesh_shape
    width = own_ref.shape[-1]
    items = tl_ref.shape[1]
    ids = jnp.zeros((16, width), F32)
    for c, m, n, at in each_part(n_rows, n_cols):
        part = (own_ref, other_ref)[c][m, n, above:, :].astype(F32)
        dev_s[at] = part[0 : 6 * ni]
        ids = ids + part[6 * ni :]
    count = n_rows * n_cols
    numbers = ids[0:8] * 256.0 + ids[8:16]
    number = jnp.concatenate([numbers[k : k + 1, :] for k in range(-(-count * ni // width))], axis=1)[:, : count * ni]
    pick = one(iota((items, count * ni), 0).astype(F32) == number)
    pick_ref[...] = pick
    ones = jnp.ones((8, items), BF16)
    act = act_ref[...]
    d_cond = jnp.zeros((items, width), F32)
    for b in range(6):
        block = jnp.concatenate([dev_s[d, b * ni : (b + 1) * ni, :] for d in range(count)], axis=0)
        grad = low(mm(pick, low(block)))
        total = mm(ones, grad)[0]
        cols = slice(b * width, (b + 1) * width)
        if b < 4:
            mb_ref[cols] = total
            mod_ref[:, cols] = t_mm(act, grad)
            d_cond = d_cond + mm_t(grad, mw_ref[:, (b + 2) * width : (b + 3) * width])
        else:
            cols = slice((b - 4) * width, (b - 3) * width)
            fb_ref[cols] = total
            fin_ref[:, cols] = t_mm(act, grad)
            d_cond = d_cond + mm_t(grad, fw_ref[:, cols])
    cond_ref[...] = d_cond


def condition_kernel(
    mesh_shape, ni, share, own_ref, other_ref, tl_ref, feat_ref, pre_ref, cond_ref, act_ref, mw_ref, cw_ref,
    part_ref, part_b_ref, d_cond_ref, pick_ref,
    mod_ref, table_ref, clock_ref, time_ref, mb_ref, cb_ref, tb_ref, patch_ref, pb_ref, dev_s,
):
    n_rows, n_cols = mesh_shape
    width = cw_ref.shape[0]
    items = tl_ref.shape[1]
    count = n_rows * n_cols
    line = n_cols // 4
    more = (own_ref.shape[1] - share) // line
    for c, m, n, at in each_part(n_rows, n_cols):
        dev_s[at] = (own_ref, other_ref)[c][m, share + n * more : share + (n + 1) * more, :].astype(F32)
    patch = jnp.sum(dev_s[:, 2 * ni :, :], axis=0)
    patch_ref[...] = patch[0:16]
    pb_ref[...] = patch[16]
    ones = jnp.ones((8, items), BF16)
    act = act_ref[...]
    d_cond = d_cond_ref[...]
    for b in range(2):
        block = jnp.concatenate([dev_s[d, b * ni : (b + 1) * ni, :] for d in range(count)], axis=0)
        grad = low(mm(pick_ref[...], low(block)))
        cols = slice(b * width, (b + 1) * width)
        mb_ref[cols] = mm(ones, grad)[0]
        mod_ref[:, cols] = t_mm(act, grad)
        d_cond = d_cond + mm_t(grad, mw_ref[:, cols])
    mb_ref[2 * width :] = part_b_ref[...]
    mod_ref[:, 2 * width :] = part_ref[...]
    cond = cond_ref[...]
    sigma = sigmoid(cond)
    d_cond = low(d_cond * (sigma * (1.0 + cond * (1.0 - sigma))))
    pre = pre_ref[...]
    sigma = sigmoid(pre)
    hidden = low(pre * sigma)
    classes = table_ref.shape[0]
    table_ref[...] = mm(one(iota((classes, items), 0) == tl_ref[1:2, :]), d_cond)
    clock_ref[...] = t_mm(hidden, d_cond)
    cb_ref[...] = mm(ones, d_cond)[0]
    d_time = low(mm_t(d_cond, cw_ref[...]) * (sigma * (1.0 + pre * (1.0 - sigma))))
    time_ref[...] = mm(feat_ref[...], d_time)
    tb_ref[...] = mm(ones, d_time)[0]


def local(
    latent, cotangent, item_ids, positions, gap_mask, timesteps, labels, patch_weight, patch_bias, time_weight,
    time_bias, clock_weight, clock_bias, class_table, modulation_weight, modulation_bias, attention_weight, query_bias,
    value_bias, output_weight, output_bias, hidden_weight, hidden_bias, return_weight, return_bias, final_modulation,
    final_offsets, readout_weight, readout_bias,
):
    n_rows, n_cols = lax.axis_size("row"), lax.axis_size("col")
    row_count, col_count = item_ids.shape
    width = patch_weight.shape[1]
    hidden = hidden_weight.shape[1]
    hp = n_rows * row_count
    cw = col_count // n_rows
    tokens = (cw + HALO) * hp
    ni = 2 * (-(-cw // LEAST))
    items = -(-(timesteps.shape[0] + 16) // 32) * 32
    unit = 8 * n_rows * n_cols
    rows_1 = -(-(2 * hidden + width + 128) // unit) * unit
    rows_2 = -(-(3 * width + 128) // unit) * unit
    pairs = width // 128

    tile, first_cols, last_cols = call(
        tile_kernel,
        [((col_count, 384), BF16), ((RIGHT, 384), BF16), ((LEFT, 384), BF16)],
        [latent, cotangent, item_ids, positions, gap_mask],
    )

    def shift(value, step_row, step_col, wanted):
        route = [
            (i * n_cols + j, (i + step_row) % n_rows * n_cols + j + step_col)
            for i in range(n_rows)
            for j in range(n_cols)
            if 0 <= j + step_col < n_cols and wanted((i + step_row) % n_rows)
        ]
        return lax.ppermute(value, ("row", "col"), route)

    left = shift(last_cols, 0, 1, lambda i: i == 0)
    tiles = [shift(tile, k, 0, lambda i: True) for k in range(1, n_rows)]
    rights = [shift(first_cols, k, -1, lambda i: (i + 1) * cw + HALO + 1 > col_count) for k in range(n_rows)]

    tl, feat, time_pre, condition, cond_act, table = call(
        item_kernel,
        [((8, items), jnp.int32), ((time_weight.shape[0], items), BF16), ((items, width), F32), ((items, width), F32),
         ((items, width), BF16), ((4 * POSITIONS, width), BF16)],
        [timesteps, labels, time_weight, time_bias, clock_weight, clock_bias, class_table],
        us=5,
    )

    dims = (n_rows, hp, cw, tokens, ni, rows_1 // 2)
    heads = ((pairs, tokens, 128), BF16)
    ins = [tile, left, *tiles, *rights, cond_act, table, patch_bias, modulation_bias, query_bias, value_bias, output_bias,
           hidden_bias, return_bias, final_offsets, readout_bias, patch_weight, modulation_weight, final_modulation,
           attention_weight, output_weight, hidden_weight, return_weight, readout_weight.T]
    q, k, v, d_at, rows, aux, res, mid, attn_in, patches, member, spread, spoken, item_main, keep, out = call(
        functools.partial(main_kernel, dims),
        [heads, heads, heads, heads, ((8, tokens), F32), ((tokens, 128), F32), ((tokens, width), F32),
         ((tokens, width), F32), ((tokens, width), BF16), ((tokens, 128), BF16), ((tokens, 128), BF16),
         ((128, 8 * width), BF16), ((tokens, 128), BF16), ((6 * ni + 16, width), BF16),
         ((rows_1 // 2, width), BF16), ((rows_1 // 2, width), BF16)],
        ins,
        [((n_rows, LEFT + 64 + RIGHT, 384), BF16), ((tokens, 128), BF16), ((pairs, tokens, 128), BF16),
         ((tokens, width), BF16), ((tokens, hidden), BF16), ((tokens, hidden), BF16), ((tokens, width), BF16),
         ((tokens, width), BF16), ((tokens, width), BF16), ((BLOCK, hidden), F32), ((16, 8 * width), F32),
         ((128, width), F32), ((2, rows_1 // 2, width), BF16)],
        us=35, room=44, near_out=range(16), near_in=(),
    )
    shape = (n_rows, n_cols)
    lines = n_cols // 4
    got = send(out, *shape, flip_col=1)

    part = ((1, tokens, 128), BF16)
    total = ((1, tokens, 128), F32)
    d_first = call(
        functools.partial(attend_back_kernel, hp, 0), [part] * 3, [q, k, v, d_at, rows, aux], [total] * 2,
        us=4, room=24, near_in=range(6), near_out=range(3),
    )
    parts = add_up([keep, got], 2 * n_rows, plane_spot, after=[d_first[0]])
    got = to_plane(parts, *shape)
    dims = (n_rows, hp, cw, tokens, ni, rows_2 // 2)
    part = ((pairs - 1, tokens, 128), BF16)
    total = ((pairs - 1, tokens, 128), F32)
    result = call(
        functools.partial(back_kernel, dims),
        [((rows_2 // 2, width), BF16)] * 2 + [((2 * ni + 24, width), BF16)]
        + [((64, 256), BF16)] * n_rows + [((RIGHT, 256), BF16)] * n_rows,
        [q, k, v, d_at, rows, aux, *d_first, attn_in, res, mid, patches, member, spread, spoken, attention_weight,
         patch_weight],
        [part] * 3 + [total] * 2 + [((128, width), F32), ((2, rows_2 // 2, width), BF16)]
        + [((tokens, width), BF16), ((16, 2 * width), F32), ((n_rows, 64 + RIGHT, 256), F32)],
        us=14, after=[parts[0]], room=32, near_in=range(16), near_out=range(3 + 2 * n_rows),
    )
    keep_2, out_2, item_back = result[:3]
    got_2 = send(out_2, *shape, flip_col=1)
    mine, over = result[3 : 3 + n_rows], result[3 + n_rows :]
    share_1 = rows_1 // (n_rows * n_cols)
    share_2 = rows_2 // (4 * n_rows)

    parts = add_up([parts[0]] + got, lines, line_spot, after=[item_back])
    got = to_line(parts, *shape)
    parts_2 = add_up([keep_2, got_2], 2 * n_rows, plane_spot, after=[parts[0]])
    got_2 = to_plane(parts_2, *shape)
    part_2 = add_below([parts_2[0]] + got_2, item_back)
    part = add_below([parts[0]] + got, item_main, after=[part_2])
    mine = [mine[0]] + [shift(mine[k], k, 0, lambda i: True) for k in range(1, n_rows)]
    over = [shift(over[k], k, 1, lambda i: True) for k in range(n_rows)]
    velocity, latent_grad = call(
        functools.partial(canvas_kernel, n_rows), [(latent.shape, BF16), (latent.shape, F32)], [*mine, *over],
        near_in=range(2 * n_rows),
    )
    block = stack([part] + to_line([part] * lines, *shape), after=[velocity])
    lists = [part_2] + to_line([part_2] * lines, *shape)
    (block_2,) = call(
        functools.partial(line_kernel, share_2), [((share_2 + lines * item_back.shape[0], width), BF16)], lists,
        [((lines, share_2, width), F32)], near_in=range(lines), near_out=(0,),
    )
    plane = stack([block] + to_plane([block] * (2 * n_rows), *shape), after=[block_2])
    blocks = plane, send(plane, *shape, flip_col=1)
    got_2 = to_plane([block_2] * (2 * n_rows), *shape)
    devices = n_rows * n_cols
    vector = ((width,), F32)
    return_grad, hidden_grad, output_grad, readout_grad, return_b, hidden_b, output_b, readout_b = call(
        functools.partial(first_out_kernel, shape),
        [((hidden, width), F32), ((width, hidden), F32), ((width, width), F32), ((16, width), F32), vector,
         ((hidden,), F32), vector, ((16,), F32)],
        blocks,
        [((devices, share_1, width), F32)],
        us=3, room=32, near_in=range(2),
    )
    part_mod, final_grad, part_b, final_b, d_cond, pick = call(
        functools.partial(item_condition_kernel, shape, ni, share_1),
        [((width, 4 * width), F32), ((width, 2 * width), F32), ((4 * width,), F32), ((2 * width,), F32),
         ((items, width), F32), ((items, devices * ni), BF16)],
        [*blocks, tl, cond_act, modulation_weight, final_modulation],
        [((devices, 6 * ni, width), F32)],
        us=5, room=32, near_in=range(2), near_out=(0, 2, 4, 5),
    )
    plane = stack([block_2] + got_2, after=[return_b, d_cond])
    blocks_2 = plane, send(plane, *shape, flip_col=1)

    modulation_grad, table_grad, clock_grad, time_grad, modulation_b, clock_b, time_b, patch_grad, patch_b = call(
        functools.partial(condition_kernel, shape, ni, share_2),
        [((width, 6 * width), F32), (class_table.shape, F32), ((width, width), F32), (time_weight.shape, F32),
         ((6 * width,), F32), vector, vector, ((16, width), F32), vector],
        [*blocks_2, tl, feat, time_pre, condition, cond_act, modulation_weight, clock_weight, part_mod, part_b, d_cond,
         pick],
        [((devices, 2 * ni + 24, width), F32)],
        us=5, room=32, near_in=(0, 1, 9, 10, 11, 12),
    )
    attention_grad, query_b, value_b = call(
        functools.partial(second_out_kernel, shape),
        [((width, 3 * width), F32), vector, vector],
        blocks_2,
        [((4 * n_rows, share_2, width), F32)],
        near_in=range(2),
    )
    return (
        velocity, latent_grad, patch_grad, patch_b, time_grad, time_b, clock_grad, clock_b, table_grad, modulation_grad,
        modulation_b, attention_grad, query_b, value_b, output_grad, output_b, hidden_grad, hidden_b, return_grad,
        return_b, final_grad, final_b, readout_grad.T, readout_b,
    )


def solution(mesh):
    canvas, grid = P(None, "row", "col"), P("row", "col")
    return jax.shard_map(
        local,
        mesh=mesh,
        in_specs=(canvas, canvas, grid, canvas, grid) + (P(),) * 24,
        out_specs=(canvas, canvas) + (P(),) * 22,
        check_vma=False,
    )
```

```python
import functools
import math

import jax
import jax.numpy as jnp
from jax import lax
from jax.experimental import pallas as pl
from jax.experimental.pallas import tpu as pltpu
from jax.sharding import PartitionSpec as P

HEADS = 6
HALO = 16
LEAST = 8
BLOCK = 256
FIRST, SECOND, THIRD = 384, 256, 384
LEFT = 16
RIGHT = 32
POSITIONS = 128
F32 = jnp.float32
BF16 = jnp.bfloat16
FLOPS_US = 1_150_000_000
BYTES_US = 3_700_000


def iota(shape, dim):
    return lax.broadcasted_iota(jnp.int32, shape, dim)


def mm(a, b):
    return jnp.dot(a, b, preferred_element_type=F32)


def mm_t(a, b):
    return lax.dot_general(a, b, (((1,), (1,)), ((), ())), preferred_element_type=F32)


def t_mm(a, b):
    return lax.dot_general(a, b, (((0,), (0,)), ((), ())), preferred_element_type=F32)


def low(v):
    return v.astype(BF16)


def one(cond):
    return jnp.where(cond, 1.0, 0.0).astype(BF16)


def sigmoid(v):
    return 1.0 / (1.0 + jnp.exp(-v))


def layer_norm(v):
    center = v - jnp.mean(v, axis=-1, keepdims=True)
    inverse = lax.rsqrt(jnp.mean(center * center, axis=-1, keepdims=True) + 1e-06)
    return center * inverse, inverse


def norm_back(normed, inverse, grad):
    mean_grad = jnp.mean(grad, axis=-1, keepdims=True)
    mean_cross = jnp.mean(grad * normed, axis=-1, keepdims=True)
    return inverse * (grad - mean_grad - normed * mean_cross)


def call(
    body, outs, ins, scratch=(), near_in=(), near_out=(), far_in=(), hand_out=(), alias=None, after=(), us=2, room=16
):
    spec = pl.BlockSpec(memory_space=pltpu.VMEM)
    away = pl.BlockSpec(memory_space=pl.ANY)
    used = len(ins)

    def run(*refs):
        body(*refs[:used], *refs[used + len(after) :])

    ins = [
        pltpu.with_memory_space_constraint(a, pltpu.VMEM if n in near_in else pltpu.HBM)
        if n in near_in or n in far_in else a
        for n, a in enumerate(ins)
    ]
    return pl.pallas_call(
        run,
        out_shape=[
            (pltpu.VMEM if n in near_out else jax.ShapeDtypeStruct)(shape, dtype)
            for n, (shape, dtype) in enumerate(outs)
        ],
        in_specs=[away if n == alias else spec for n in range(used)] + [away] * len(after),
        out_specs=[away if n in hand_out else spec for n in range(len(outs))],
        scratch_shapes=[pltpu.VMEM(shape, dtype) for shape, dtype in scratch]
        + [pltpu.SemaphoreType.DMA(())] * len(hand_out),
        input_output_aliases={} if alias is None else {alias: 0},
        compiler_params=pltpu.CompilerParams(vmem_limit_bytes=room * 1024 * 1024),
        cost_estimate=pl.CostEstimate(flops=us * FLOPS_US, bytes_accessed=us * BYTES_US, transcendentals=0),
    )(*ins, *after)


def line(ref, start=0, count=None):
    count = ref.shape[0] if count is None else count
    return ref[start : start + count].astype(F32).reshape(1, count)


def lane_fold(rows):
    lane = iota((rows, 128), 1)
    feature = 8 * (1 - (lane & 1)) + 4 * (1 - (lane >> 6)) + ((lane >> 4) & 3)
    return one(iota((rows, 128), 0) == feature)


def tile_kernel(lat_ref, cot_ref, ids_ref, pos_ref, gap_ref, tile_ref, first_ref, side_ref):
    cols = ids_ref.shape[1]
    pieces = []
    for ref in (lat_ref, cot_ref):
        flat = ref[...].reshape(64, 2 * cols)
        for side in (0, 1):
            pick = one(iota((cols, 2 * cols), 1) == 2 * iota((cols, 2 * cols), 0) + side)
            pieces.append(mm_t(pick, flat))
    tag = ids_ref[...] + 1
    meta = jnp.concatenate(
        [tag >> 8, tag & 255, pos_ref[0], pos_ref[1], gap_ref[...], jnp.zeros((88, cols), jnp.int32)], axis=0
    ).astype(F32)
    pieces.append(mm_t(one(iota((cols, cols), 0) == iota((cols, cols), 1)), low(meta)))
    tile = low(jnp.concatenate(pieces, axis=1))
    tile_ref[...] = tile
    first_ref[...] = tile[:RIGHT]
    side_ref[...] = tile[:RIGHT]

    @pl.when(lax.axis_index("row") == 0)
    def _():
        side_ref[0:LEFT, :] = tile[cols - LEFT :]


def item_kernel(
    steps_ref, labels_ref, tw_ref, tb_ref, cw_ref, cb_ref, ct_ref, tl_ref, feat_ref, pre_ref, cond_ref, act_ref, table_ref
):
    items = tl_ref.shape[1]
    count = steps_ref.shape[0]
    tl_ref[...] = jnp.zeros_like(tl_ref)
    tl_ref[0:1, 0:count] = steps_ref[...].reshape(1, count)
    tl_ref[1:2, 0:count] = labels_ref[...].reshape(1, count)
    half = tw_ref.shape[0] // 2
    steps = tl_ref[0:1, :].astype(F32)
    freq = jnp.exp(iota((half, 1), 0).astype(F32) * (-math.log(10000.0) / half))
    angle = freq * steps
    feat_ref[0:half, :] = low(jnp.cos(angle))
    feat_ref[half:, :] = low(jnp.sin(angle))
    pre = t_mm(feat_ref[...], tw_ref[...]) + line(tb_ref)
    pre_ref[...] = pre
    hidden = low(pre * sigmoid(pre))
    classes = ct_ref.shape[0]
    pick = one(iota((classes, items), 0) == tl_ref[1:2, :])
    cond = mm(hidden, cw_ref[...]) + line(cb_ref) + t_mm(pick, ct_ref[...])
    cond_ref[...] = cond
    act_ref[...] = low(cond * sigmoid(cond))
    width = table_ref.shape[1]
    quarter = width // 4
    shape = (2 * POSITIONS, width)
    lane = iota(shape, 1)
    row = iota(shape, 0)
    second = lane >= 2 * quarter
    within = jnp.where(second, lane - 2 * quarter, lane)
    cosine = within >= quarter
    index = jnp.where(cosine, within - quarter, within)
    omega = jnp.exp(index.astype(F32) * (-math.log(10000.0) / quarter))
    angle = (row & (POSITIONS - 1)).astype(F32) * omega
    value = jnp.where(cosine, jnp.cos(angle), jnp.sin(angle))
    value = jnp.where(jnp.where(second, 1, 0) == jnp.where(row >= POSITIONS, 1, 0), value, 0.0)
    high = low(value)
    table_ref[0 : 2 * POSITIONS, :] = high
    table_ref[2 * POSITIONS :, :] = low(value - high.astype(F32))


def row_mask(q, i, shape):
    return ((q * 16 + (iota(shape, 1) & 15) - 1) >> 1) == i


def main_kernel(dims, *refs):
    n_rows, hp, cw, tokens, ni, half_rows = dims
    own_ref, side_ref = refs[0:2]
    tiles = refs[2 : 1 + n_rows]
    rights = refs[1 + n_rows : 2 * n_rows]
    (act_ref, table_ref, pb_ref, mb_ref, qb_ref, vb_ref, ob_ref, hb_ref, rb_ref, fb_ref, lb_ref,
     pw_ref, mw_ref, fw_ref, aw_ref, ow_ref, hw_ref, rw_ref, low_ref,
     q_ref, k_ref, v_ref, da_ref, rows_ref, aux_ref, res_ref, mid_ref, in_ref, x_ref, mem_ref, turn_ref, ms_ref, vel_ref,
     item_ref, keep_ref, send_ref,
     es, ct_s, at_s, mlp_s, ha_s, dh_s, dbm_s, dba_s, ri_s, gd_s, dacc, small, g_s) = refs[2 * n_rows :]
    width = res_ref.shape[1]
    pairs = width // 128
    r = lax.axis_index("row")
    core = lax.axis_index("col") & 1
    shift = int(math.log2(hp))

    es[...] = jnp.zeros_like(es)
    es[r, LEFT : LEFT + 64, :] = own_ref[...]
    for k in range(1, n_rows):
        other = lax.rem(r - k + n_rows, n_rows)
        es[other, LEFT : LEFT + 64, :] = tiles[k - 1][...]
        es[other, LEFT + 64 :, :] = rights[k - 1][...]

    @pl.when(r == 0)
    def _():
        es[r, 0:LEFT, :] = side_ref[0:LEFT, :]

    @pl.when(r > 0)
    def _():
        es[r, LEFT + 64 :, :] = side_ref[...]

    meta = es[r, :, 256:384].astype(F32)
    lane = iota(meta.shape, 1)
    weighted = meta * jnp.where(lane == 0, 256.0, jnp.where(lane == 8, 1.0, 0.0))
    down = iota(meta.shape, 0)
    start = LEFT + r * cw
    tag_prev = jnp.sum(jnp.where(down == start - 1, weighted, 0.0)).astype(jnp.int32)
    tag_last = jnp.sum(jnp.where(down == start + cw - 1, weighted, 0.0)).astype(jnp.int32)
    tag_first = jnp.sum(jnp.where(down == start, weighted, 0.0)).astype(jnp.int32)
    strip_prev = jnp.where(tag_prev == 0, ((tag_first - 1) >> 1) - 1, (tag_prev - 1) >> 1)
    strip_last = (tag_last - 1) >> 1
    base = 2 * (strip_prev + 1)

    pick = one(iota((16, act_ref.shape[0]), 1) == base + iota((16, act_ref.shape[0]), 0))
    own_act = low(mm(pick, act_ref[...]))
    ms_ref[48:, :] = jnp.zeros_like(ms_ref[48:, :])
    for b in range(8):
        cols = slice(b * width, (b + 1) * width)
        if b < 6:
            value = mm(own_act, mw_ref[:, cols]) + line(mb_ref, b * width, width)
        else:
            value = mm(own_act, fw_ref[:, (b - 6) * width : (b - 5) * width]) + line(fb_ref, (b - 6) * width, width)
        p0 = low(value)
        rest = value - p0.astype(F32)
        p1 = low(rest)
        ms_ref[0:16, cols] = p0
        ms_ref[16:32, cols] = p1
        ms_ref[32:48, cols] = low(rest - p1.astype(F32))

    def mod(mem, b, n=1):
        return mm(mem, ms_ref[:, b * width : (b + n) * width])

    fold = lane_fold(16)
    embed = low(t_mm(fold, pw_ref[...]))
    unread = low(t_mm(low_ref[...], fold))
    b_lanes = iota((BLOCK, 128), 1)
    is_b1 = b_lanes >= 64
    half_lanes = (one(b_lanes < 64), one(is_b1))

    lanes = iota((FIRST, 128), 1)
    second_side = lanes >= 64

    def first(tb, carry):
        t0 = pl.multiple_of(tb * FIRST, FIRST)
        rows = pl.ds(t0, FIRST)
        token = t0 + iota((FIRST, 1), 0)
        j = token >> shift
        i = token & (hp - 1)
        spot = iota((FIRST, LEFT + 64 + RIGHT), 1)
        rep0 = one(spot == start + j)
        rep1 = one(spot == start + j + 1)
        x = jnp.zeros((FIRST, 128), F32)
        c = jnp.zeros((FIRST, 128), F32)
        m = jnp.zeros((FIRST, 128), F32)
        for q in range(n_rows):
            here = mm(rep0, es[q])
            beside = mm(rep1, es[q, :, 0:256])
            mask = row_mask(q, i, (FIRST, 128))
            x = x + jnp.where(mask, jnp.where(second_side, here[:, 0:128], beside[:, 0:128]), 0.0)
            c = c + jnp.where(mask, jnp.where(second_side, here[:, 128:256], beside[:, 128:256]), 0.0)
            m = m + jnp.where((q * 8 + (lanes & 7)) == i, here[:, 256:384], 0.0)
        x = low(x)
        m = low(m)
        x_ref[rows, :] = x
        ml = iota((128, 128), 0)
        mc = iota((128, 128), 1)
        kind = ml >> 3
        gather = jnp.where(
            (mc == 0) & (kind == 0), 256.0,
            jnp.where(((mc == 0) & (kind == 1)) | ((mc >= 1) & (mc <= 3) & (kind == mc + 1)), 1.0, 0.0),
        ).astype(BF16)
        cols = mm(m, gather)
        rl = iota((8, 128), 1) >> 3
        rr = iota((8, 128), 0)
        row_pick = jnp.where((rr == 6) & (rl == 0), 256.0, jnp.where((rr == 6) & (rl == 1), 1.0, 0.0)).astype(BF16)
        across = mm_t(row_pick, m)
        rows_ref[:, rows] = across
        tag_row = across[6:7, :].astype(jnp.int32)
        strip_row = (tag_row - 1) >> 1
        turn_ref[:, rows] = one(
            (tag_row - 1 - base == iota((16, FIRST), 0)) & (strip_row > strip_prev) & (strip_row <= strip_last)
        )
        tag = cols[:, 0:1]
        gap = cols[:, 3:4]
        tag_i = tag.astype(jnp.int32)
        strip = (tag_i - 1) >> 1
        owned = (strip > strip_prev) & (strip <= strip_last)
        act = jnp.where(owned, gap, 0.0)
        aux_ref[rows, :] = jnp.where(lanes == 0, tag * gap, jnp.where(lanes == 1, act, 0.0))
        item = tag_i - 1 - base
        mem = one((item == (lanes & 15)) & (lanes < 48) & owned)
        mem_ref[rows, :] = mem
        ct_s[rows, :] = low(c * act)
        p0 = cols[:, 1:2].astype(jnp.int32)
        p1 = cols[:, 2:3].astype(jnp.int32) + POSITIONS
        spot = iota((FIRST, 2 * POSITIONS), 1)
        place = one((spot == p0) | (spot == p1))
        res = (
            mm(x, embed) + line(pb_ref)
            + (mm(place, table_ref[0 : 2 * POSITIONS, :]) + mm(place, table_ref[2 * POSITIONS :, :]))
        )
        res_ref[rows, :] = res
        normed, _ = layer_norm(res)
        ab = mod(mem, 0, 2)
        attn_in = low(normed * (1.0 + ab[:, width:]) + ab[:, :width])
        in_ref[rows, :] = attn_in
        for part, ref in enumerate((q_ref, k_ref, v_ref)):
            value = mm(attn_in, aw_ref[:, part * width : (part + 1) * width])
            if part != 1:
                value = value + line(vb_ref if part else qb_ref)
            value = low(value)
            if part == 0:
                value = value * BF16(1.0 / math.sqrt(width // HEADS))
            for p in range(pairs):
                ref[p, rows, :] = value[:, p * 128 : (p + 1) * 128]
        return carry

    lax.fori_loop(0, tokens // FIRST, first, 0)

    for qb in range(tokens // BLOCK):
        qs = slice(qb * BLOCK, (qb + 1) * BLOCK)
        ks = key_range(qb, hp, tokens)
        q_tag = rows_ref[6:7, qs]
        k_tag = aux_ref[ks, 0:1]
        allowed = k_tag == q_tag
        for p in range(pairs):
            query = q_ref[p, qs, :]
            key = k_ref[p, ks, :]
            value = v_ref[p, ks, :]
            halves = []
            for e in range(2):
                scores = jnp.where(allowed, mm_t(key, query * half_lanes[e]), -1e30)
                top = jnp.max(scores, axis=0, keepdims=True)
                expo = jnp.exp(scores - top)
                total = jnp.sum(expo, axis=0, keepdims=True)
                rows_ref[2 * p + e : 2 * p + e + 1, qs] = top + jnp.log(total)
                halves.append(t_mm(low(expo * (1.0 / total)), value))
            at_s[p, qs, :] = low(jnp.where(is_b1, halves[1], halves[0]))

    dacc[...] = jnp.zeros_like(dacc)
    small[...] = jnp.zeros_like(small)

    def second(tb, carry):
        t0 = pl.multiple_of(tb * SECOND, SECOND)
        rows = pl.ds(t0, SECOND)
        mem = mem_ref[rows, :]

        turned = turn_ref[:, rows]

        def item_sum(b, grad):
            dacc[:, b * width : (b + 1) * width] += mm(turned, low(grad))

        attended = jnp.concatenate([at_s[p, rows, :] for p in range(pairs)], axis=1)
        branch_a = mm(attended, ow_ref[...]) + line(ob_ref)
        gate_a = mod(mem, 2)
        mid = res_ref[rows, :] + gate_a * branch_a
        norm_mid, inv_mid = layer_norm(mid)
        scale_m = 1.0 + mod(mem, 4)
        mlp_in = low(norm_mid * scale_m + mod(mem, 3))
        mlp_s[rows, :] = mlp_in
        hidden = hw_ref.shape[1]
        branch_m = jnp.zeros((SECOND, width), F32)
        for n in range(hidden // width):
            part = slice(n * width, (n + 1) * width)
            pre = mm(mlp_in, hw_ref[:, part]) + line(hb_ref, n * width, width)
            square = pre * pre
            c0 = math.sqrt(2.0 / math.pi)
            t = jnp.tanh(pre * (c0 + (c0 * 0.044715) * square))
            up = 0.5 + 0.5 * t
            act = low(pre * up)
            gd_s[:, part] = up + (0.5 * pre) * (1.0 - t * t) * (c0 + (3.0 * c0 * 0.044715) * square)
            ha_s[rows, part] = act
            branch_m = branch_m + mm(act, rw_ref[part, :])
        branch_m = branch_m + line(rb_ref)
        gate_m = mod(mem, 5)
        norm_out, inv_out = layer_norm(mid + gate_m * branch_m)
        scale_f = 1.0 + mod(mem, 7)
        readout_in = low(norm_out * scale_f + mod(mem, 6))
        ri_s[rows, :] = readout_in
        active = aux_ref[rows, 1:2]
        bias_lanes = mm(low(line(lb_ref) + jnp.zeros((8, 16), F32)), fold)[0:1, :]
        vel_ref[rows, :] = low((mm(readout_in, unread) + bias_lanes) * active)
        d_read = mm_t(ct_s[rows, :], unread)
        item_sum(6, d_read)
        item_sum(7, d_read * norm_out)
        d_out = norm_back(norm_out, inv_out, d_read * scale_f)
        item_sum(5, d_out * branch_m)
        d_bm = low(d_out * gate_m)
        dbm_s[rows, :] = d_bm
        small[16:17, :] += jnp.sum(d_bm.astype(F32), axis=0, keepdims=True)
        d_mlp = jnp.zeros((SECOND, width), F32)
        for n in range(hidden // width):
            part = slice(n * width, (n + 1) * width)
            d_hid = low(mm_t(d_bm, rw_ref[part, :]) * gd_s[:, part])
            dh_s[rows, part] = d_hid
            small[17 + n : 18 + n, :] += jnp.sum(d_hid.astype(F32), axis=0, keepdims=True)
            d_mlp = d_mlp + mm_t(d_hid, hw_ref[:, part])
        item_sum(3, d_mlp)
        item_sum(4, d_mlp * norm_mid)
        d_mid = d_out + norm_back(norm_mid, inv_mid, d_mlp * scale_m)
        mid_ref[rows, :] = d_mid
        item_sum(2, d_mid * branch_a)
        d_ba = low(d_mid * gate_a)
        dba_s[rows, :] = d_ba
        small[21:22, :] += jnp.sum(d_ba.astype(F32), axis=0, keepdims=True)
        d_at = low(mm_t(d_ba, ow_ref[...]))
        for p in range(pairs):
            da_ref[p, rows, :] = d_at[:, p * 128 : (p + 1) * 128]
        return carry

    lax.fori_loop(0, tokens // SECOND, second, 0)
    rows = [dacc[0:ni, b * width : (b + 1) * width] for b in range(2, 8)]
    spot = ((core * 2 * n_rows + plane_spot()) * (lax.axis_size("col") // 4) + line_spot()) * ni
    index = iota((4, width), 0) * width + iota((4, width), 1) - spot
    number = jnp.where((index >= 0) & (index < ni), base + index, 0)
    rows += [(number >> 8).astype(F32), (number & 255).astype(F32)]
    item_ref[...] = low(jnp.concatenate(rows, axis=0))

    g_s[...] = jnp.zeros_like(g_s)
    put = functools.partial(put_rows, g_s, half_rows)
    n_hidden = hw_ref.shape[1] // width
    for n in range(n_hidden):
        part = slice(n * width, (n + 1) * width)
        put(n * width, low(t_mm(ha_s[:, part], dbm_s[...])))
    grad = low(t_mm(mlp_s[...], dh_s[...]))
    for n in range(n_hidden):
        put((n_hidden + n) * width, grad[:, n * width : (n + 1) * width])
    attended = jnp.concatenate([at_s[p] for p in range(pairs)], axis=1)
    put(2 * n_hidden * width, low(t_mm(attended, dba_s[...])))
    ones = jnp.ones((8, tokens), BF16)
    small[0:16, :] = mm(fold, low(t_mm(ct_s[...], ri_s[...])))
    sums = mm(ones, ct_s[...])
    small[22:23, 0:128] = mm_t(jnp.broadcast_to(low(sums[0:1, :]), (8, 128)), lane_fold(128))[0:1, :]
    put((2 * n_hidden + 1) * width, low(small[...]))
    keep_ref[...] = g_s[core]
    send_ref[...] = g_s[1 - core]


def put_rows(g_s, half_rows, row, value):
    count = value.shape[0]
    done = 0
    while done < count:
        side, at = divmod(row + done, half_rows)
        take = min(count - done, half_rows - at)
        g_s[side, at : at + take, :] = value[done : done + take, :]
        done += take


def key_range(qb, hp, tokens):
    first_col = (qb * BLOCK) // hp
    last_col = ((qb + 1) * BLOCK - 1) // hp
    return slice(max(0, first_col - HALO) * hp, min(tokens, (last_col + 1 + HALO) * hp))


def attend_back_kernel(hp, first, q_ref, k_ref, v_ref, da_ref, rows_ref, aux_ref, dq_ref, dk_ref, dv_ref, dk_s, dv_s):
    tokens = q_ref.shape[1]
    b_lanes = iota((BLOCK, 128), 1)
    is_b1 = b_lanes >= 64
    half_lanes = (one(b_lanes < 64), one(is_b1))
    scale = 1.0 / math.sqrt(q_ref.shape[0] * 128 // HEADS)
    dk_s[...] = jnp.zeros_like(dk_s)
    dv_s[...] = jnp.zeros_like(dv_s)
    for qb in range(tokens // BLOCK):
        qs = slice(qb * BLOCK, (qb + 1) * BLOCK)
        ks = key_range(qb, hp, tokens)
        allowed = aux_ref[ks, 0:1] == rows_ref[6:7, qs]
        for n in range(dq_ref.shape[0]):
            p = first + n
            query = q_ref[p, qs, :]
            key = k_ref[p, ks, :]
            value = v_ref[p, ks, :]
            d_at = da_ref[p, qs, :]
            d_key = 0.0
            d_value = 0.0
            halves = []
            for e in range(2):
                q_half = query * half_lanes[e]
                d_half = d_at * half_lanes[e]
                scores = jnp.where(allowed, mm_t(key, q_half), -1e30)
                probs = jnp.exp(scores - rows_ref[2 * p + e : 2 * p + e + 1, qs])
                d_probs = mm_t(value, d_half)
                inner = jnp.sum(probs * d_probs, axis=0, keepdims=True)
                d_scores = low(probs * (d_probs - inner))
                d_value = d_value + mm(low(probs), d_half)
                d_key = d_key + mm(d_scores, q_half)
                halves.append(t_mm(d_scores, key))
            dk_s[n, ks, :] += d_key
            dv_s[n, ks, :] += d_value
            dq_ref[n, qs, :] = low(jnp.where(is_b1, halves[1], halves[0]) * scale)
    dk_ref[...] = low(dk_s[...])
    dv_ref[...] = low(dv_s[...])


def joined(refs, rows):
    return jnp.concatenate(
        [ref[n, rows, :] for kind in range(3) for ref in refs[kind::3] for n in range(ref.shape[0])], axis=1
    )


def weigh_attention(half_rows, in_ref, parts, keep_ref, send_ref, small, g_s):
    tokens, width = in_ref.shape
    core = lax.axis_index("col") & 1
    put = functools.partial(put_rows, g_s, half_rows)
    ones = jnp.ones((8, tokens), BF16)
    g_s[...] = jnp.zeros_like(g_s)
    small[...] = jnp.zeros_like(small)
    whole = joined(parts, slice(None))
    for n in range(3):
        grad = whole[:, n * width : (n + 1) * width]
        put(n * width, low(t_mm(in_ref[...], grad)))
        if n != 1:
            small[n // 2 : n // 2 + 1, :] = mm(ones, grad)[0:1, :]
    put(3 * width, low(small[...]))
    keep_ref[...] = g_s[core]
    send_ref[...] = g_s[1 - core]


def back_kernel(dims, *refs):
    n_rows, hp, cw, tokens, ni, half_rows = dims
    heads, done = refs[:6], refs[6:9]
    (in_ref, res_ref, mid_ref, x_ref, mem_ref, turn_ref, ms_ref, vel_ref, aw_ref, pw_ref, keep_ref, send_ref, item_ref) = refs[9:22]
    mine_refs = refs[22 : 22 + n_rows]
    over_refs = refs[22 + n_rows : 22 + 2 * n_rows]
    *rest, dk_s, dv_s, small, g_s, di_s, dacc, frame = refs[22 + 2 * n_rows :]
    parts = [*done, *rest]
    attend_back_kernel(hp, done[0].shape[0], *heads, *rest, dk_s, dv_s)
    weigh_attention(half_rows, in_ref, parts, keep_ref, send_ref, small, g_s)
    width = res_ref.shape[1]
    r = lax.axis_index("row")
    shift = int(math.log2(hp))

    embed = low(t_mm(lane_fold(16), pw_ref[...]))
    dacc[...] = jnp.zeros_like(dacc)
    frame[...] = jnp.zeros_like(frame)

    def third(tb, carry):
        t0 = pl.multiple_of(tb * THIRD, THIRD)
        rows = pl.ds(t0, THIRD)
        mem = mem_ref[rows, :]
        d_attn = mm_t(joined(parts, rows), aw_ref[...])
        normed, inverse = layer_norm(res_ref[rows, :])
        scale_a = 1.0 + mm(mem, ms_ref[:, width : 2 * width])
        turned = turn_ref[:, rows]
        dacc[:, 0:width] += mm(turned, low(d_attn))
        dacc[:, width : 2 * width] += mm(turned, low(d_attn * normed))
        d_in = low(mid_ref[rows, :] + norm_back(normed, inverse, d_attn * scale_a))
        di_s[rows, :] = d_in
        grad = low(mm_t(d_in, embed))
        both = jnp.concatenate([vel_ref[rows, :], grad], axis=1)
        token = t0 + iota((THIRD, 1), 0)
        j = token >> shift
        i = token & (hp - 1)
        spot = iota((THIRD, 64 + RIGHT), 1)
        rep = jnp.concatenate([one(spot == r * cw + j), one(spot == r * cw + j + 1)], axis=0)
        side = (iota((THIRD, 256), 1) >> 6) & 1
        for q in range(n_rows):
            mask = row_mask(q, i, (THIRD, 256))
            split = jnp.concatenate([both * one(mask & (side == 1)), both * one(mask & (side == 0))], axis=0)
            frame[q] += t_mm(rep, split)
        return carry

    lax.fori_loop(0, tokens // THIRD, third, 0)

    ones = jnp.ones((8, tokens), BF16)
    rows = [dacc[0:ni, 0:width], dacc[0:ni, width : 2 * width]]
    rows += [mm(lane_fold(16), low(t_mm(x_ref[...], di_s[...]))), mm(ones, di_s[...])]
    item_ref[...] = low(jnp.concatenate(rows, axis=0))
    for k in range(n_rows):
        q = lax.rem(r + k, n_rows)
        whole = low(frame[q])
        mine_refs[k][...] = whole[0:64, :]
        over_refs[k][...] = whole[64:, :]


def canvas_kernel(n_rows, *refs):
    mine, over = refs[0:n_rows], refs[n_rows : 2 * n_rows]
    vel_ref, grad_ref = refs[2 * n_rows :]
    total = mine[0][...].astype(F32)
    for ref in mine[1:]:
        total = total + ref[...].astype(F32)
    extra = over[0][...].astype(F32)
    for ref in over[1:]:
        extra = extra + ref[...].astype(F32)
    total = low(total + jnp.concatenate([extra, jnp.zeros((64 - RIGHT, 256), F32)], axis=0))
    for n, ref in enumerate((vel_ref, grad_ref)):
        value = 0.0
        for side in (0, 1):
            pick = one(iota((64, 128), 1) == 2 * iota((64, 128), 0) + side)
            value = value + t_mm(total[:, n * 128 + side * 64 : n * 128 + (side + 1) * 64], pick)
        ref[...] = value.reshape(ref.shape).astype(ref.dtype)


def add_kernel(count, me, *refs):
    outs = refs[len(refs) - count :]
    ins = refs[: len(refs) - count]
    spot = me()
    for m, out in enumerate(outs):
        at = jnp.bitwise_xor(spot, m) if count > 1 else 0
        total = ins[0][at].astype(F32)
        for ref in ins[1:]:
            total = total + ref[at].astype(F32)
        out[...] = low(total)


def plane_spot():
    return lax.axis_index("row") + lax.axis_size("row") * ((lax.axis_index("col") >> 1) & 1)


def line_spot():
    return lax.axis_index("col") >> 2


def send(value, n_rows, n_cols, flip_row=0, flip_col=0):
    route = [
        (i * n_cols + j, (i ^ flip_row) * n_cols + (j ^ flip_col)) for i in range(n_rows) for j in range(n_cols)
    ]
    return lax.ppermute(value, ("row", "col"), route)


def add_up(arrays, count, me, after=()):
    n, w = arrays[0].shape
    ins = [a.reshape(count, n // count, w) for a in arrays]
    return call(
        functools.partial(add_kernel, count, me), [((n // count, w), BF16)] * count, ins, after=after,
        near_in=range(len(ins)), near_out=range(count),
    )


def add_below_kernel(*refs):
    *ins, more, out = refs
    total = ins[0][...].astype(F32)
    for ref in ins[1:]:
        total = total + ref[...].astype(F32)
    out[...] = jnp.concatenate([low(total), more[...]], axis=0)


def add_below(arrays, more, after=()):
    n, w = arrays[0].shape
    ins = [*arrays, more]
    return call(
        add_below_kernel, [((n + more.shape[0], w), BF16)], ins, after=after, near_in=range(len(ins)), near_out=(0,)
    )[0]


def line_kernel(share, *refs):
    *ins, out, rows = refs
    spot = line_spot()
    for m, ref in enumerate(ins):
        rows[jnp.bitwise_xor(spot, m)] = ref[0:share, :].astype(F32)
    more = ins[0].shape[0] - share
    out[0:share, :] = low(jnp.sum(rows[...], axis=0))
    for m, ref in enumerate(ins):
        out[share + m * more : share + (m + 1) * more, :] = ref[share:, :]


def to_plane(parts, n_rows, n_cols):
    return [
        send(parts[m], n_rows, n_cols, flip_row=m % n_rows, flip_col=2 * (m // n_rows)) for m in range(1, 2 * n_rows)
    ]


def to_line(parts, n_rows, n_cols):
    return [send(parts[m], n_rows, n_cols, flip_col=4 * m) for m in range(1, n_cols // 4)]


def stack_kernel(*refs):
    *ins, out = refs
    for n, ref in enumerate(ins):
        out[n] = ref[...]


def stack(arrays, after=()):
    return call(
        stack_kernel, [((len(arrays), *arrays[0].shape), BF16)], arrays, after=after, near_in=range(len(arrays)),
        near_out=(0,),
    )[0]


def for_planes(n_rows, body):
    core = lax.axis_index("col") & 1
    plane = plane_spot()
    for c in range(2):

        def step(m, carry, c=c):
            body(c, m, jnp.bitwise_xor(core, c) * 2 * n_rows + jnp.bitwise_xor(plane, m))
            return carry

        lax.fori_loop(0, 2 * n_rows, step, 0)


def for_parts(n_rows, n_cols, body):
    line = line_spot()

    def inner(c, m, at):
        for n in range(n_cols // 4):
            body(c, m, n, at * (n_cols // 4) + jnp.bitwise_xor(line, n))

    for_planes(n_rows, inner)


def first_out_kernel(mesh_shape, *refs):
    n_rows, n_cols = mesh_shape
    blocks = refs[:2]
    ret_ref, hid_ref, out_ref, read_ref, rb_ref, hb_ref, ob_ref, lb_ref, whole = refs[2:]

    def place(c, m, n, at):
        whole[at] = blocks[c][m, n, 0 : whole.shape[1], :].astype(F32)

    for_parts(n_rows, n_cols, place)
    flat = whole[...].reshape(whole.shape[0] * whole.shape[1], whole.shape[2])
    width = flat.shape[1]
    hidden = ret_ref.shape[0]
    ret_ref[...] = flat[0:hidden]
    for n in range(hidden // width):
        hid_ref[:, n * width : (n + 1) * width] = flat[hidden + n * width : hidden + (n + 1) * width]
    out_ref[...] = flat[2 * hidden : 2 * hidden + width]
    at = 2 * hidden + width
    small = flat[at : at + 24]
    read_ref[...] = small[0:16]
    rb_ref[...] = small[16]
    for n in range(hidden // width):
        hb_ref[n * width : (n + 1) * width] = small[17 + n]
    ob_ref[...] = small[21]
    lb_ref[...] = small[22, 0:16]


def second_out_kernel(mesh_shape, own_ref, other_ref, att_ref, qb_ref, vb_ref, whole):

    def place(c, m, at):
        whole[at] = (own_ref, other_ref)[c][m, 0 : whole.shape[1], :].astype(F32)

    for_planes(mesh_shape[0], place)
    flat = whole[...].reshape(whole.shape[0] * whole.shape[1], whole.shape[2])
    width = flat.shape[1]
    for n in range(3):
        att_ref[:, n * width : (n + 1) * width] = flat[n * width : (n + 1) * width]
    small = flat[3 * width : 3 * width + 8]
    qb_ref[...] = small[0]
    vb_ref[...] = small[1]


def item_condition_kernel(
    mesh_shape, ni, above, own_ref, other_ref, tl_ref, act_ref, mw_ref, fw_ref,
    mod_ref, fin_ref, mb_ref, fb_ref, cond_ref, pick_ref, dev_s, mod_s, ids_s, sem,
):
    n_rows, n_cols = mesh_shape
    width = own_ref.shape[-1]
    items = tl_ref.shape[1]
    ids_s[...] = jnp.zeros_like(ids_s)

    def place(c, m, n, at):
        part = (own_ref, other_ref)[c][m, n, above:, :].astype(F32)
        for b in range(6):
            dev_s[b, at] = part[b * ni : (b + 1) * ni]
        ids_s[...] += part[6 * ni :]

    for_parts(n_rows, n_cols, place)
    ids = ids_s[...]
    count = n_rows * n_cols
    numbers = ids[0:4] * 256.0 + ids[4:8]
    number = jnp.concatenate([numbers[k : k + 1, :] for k in range(-(-count * ni // width))], axis=1)[:, : count * ni]
    pick = one(iota((items, count * ni), 0).astype(F32) == number)
    pick_ref[...] = pick
    ones = jnp.ones((8, items), BF16)
    act = act_ref[...]
    copy = pltpu.make_async_copy(mod_s, mod_ref.at[:, 2 * width :], sem)
    d_cond = jnp.zeros((items, width), F32)
    for b in range(6):
        grad = low(mm(pick, low(dev_s[b].reshape(count * ni, width))))
        total = mm(ones, grad)[0]
        cols = slice(b * width, (b + 1) * width)
        if b < 4:
            mb_ref[cols] = total
            mod_s[:, cols] = t_mm(act, grad)
            d_cond = d_cond + mm_t(grad, mw_ref[:, (b + 2) * width : (b + 3) * width])
            if b == 3:
                copy.start()
        else:
            cols = slice((b - 4) * width, (b - 3) * width)
            fb_ref[cols] = total
            fin_ref[:, cols] = t_mm(act, grad)
            d_cond = d_cond + mm_t(grad, fw_ref[:, cols])
    cond_ref[...] = d_cond
    copy.wait()


def condition_kernel(
    mesh_shape, ni, share, own_ref, other_ref, tl_ref, feat_ref, pre_ref, cond_ref, act_ref, mw_ref, cw_ref,
    part_b_ref, d_cond_ref, pick_ref, _,
    mod_ref, table_ref, clock_ref, time_ref, mb_ref, cb_ref, tb_ref, patch_ref, pb_ref, dev_s, mod_s, table_s, patch_s, sem, table_sem,
):
    n_rows, n_cols = mesh_shape
    width = cw_ref.shape[0]
    items = tl_ref.shape[1]
    count = n_rows * n_cols
    line = n_cols // 4
    more = (own_ref.shape[1] - share) // line

    def place(c, m, n, at):
        part = (own_ref, other_ref)[c][m, share + n * more : share + (n + 1) * more, :].astype(F32)
        for b in range(2):
            dev_s[b, at] = part[b * ni : (b + 1) * ni]
        patch_s[at] = part[2 * ni :]

    for_parts(n_rows, n_cols, place)
    patch = jnp.sum(patch_s[...], axis=0)
    patch_ref[...] = patch[0:16]
    pb_ref[...] = patch[16]
    ones = jnp.ones((8, items), BF16)
    act = act_ref[...]
    d_cond = d_cond_ref[...]
    copy = pltpu.make_async_copy(mod_s, mod_ref.at[:, 0 : 2 * width], sem)
    for b in range(2):
        grad = low(mm(pick_ref[...], low(dev_s[b].reshape(count * ni, width))))
        cols = slice(b * width, (b + 1) * width)
        mb_ref[cols] = mm(ones, grad)[0]
        mod_s[:, cols] = t_mm(act, grad)
        d_cond = d_cond + mm_t(grad, mw_ref[:, cols])
    copy.start()
    mb_ref[2 * width :] = part_b_ref[...]
    cond = cond_ref[...]
    sigma = sigmoid(cond)
    d_cond = low(d_cond * (sigma * (1.0 + cond * (1.0 - sigma))))
    pre = pre_ref[...]
    sigma = sigmoid(pre)
    hidden = low(pre * sigma)
    classes = table_ref.shape[0]
    table_s[...] = mm(one(iota((classes, items), 0) == tl_ref[1:2, :]), d_cond)
    table_copy = pltpu.make_async_copy(table_s, table_ref, table_sem)
    table_copy.start()
    clock_ref[...] = t_mm(hidden, d_cond)
    cb_ref[...] = mm(ones, d_cond)[0]
    d_time = low(mm_t(d_cond, cw_ref[...]) * (sigma * (1.0 + pre * (1.0 - sigma))))
    time_ref[...] = mm(feat_ref[...], d_time)
    tb_ref[...] = mm(ones, d_time)[0]
    copy.wait()
    table_copy.wait()


def local(
    latent, cotangent, item_ids, positions, gap_mask, timesteps, labels, patch_weight, patch_bias, time_weight,
    time_bias, clock_weight, clock_bias, class_table, modulation_weight, modulation_bias, attention_weight, query_bias,
    value_bias, output_weight, output_bias, hidden_weight, hidden_bias, return_weight, return_bias, final_modulation,
    final_offsets, readout_weight, readout_bias,
):
    n_rows, n_cols = lax.axis_size("row"), lax.axis_size("col")
    row_count, col_count = item_ids.shape
    width = patch_weight.shape[1]
    hidden = hidden_weight.shape[1]
    hp = n_rows * row_count
    cw = col_count // n_rows
    tokens = (cw + HALO) * hp
    ni = 2 * (-(-cw // LEAST))
    items = -(-(timesteps.shape[0] + 16) // 32) * 32
    unit = 8 * n_rows * n_cols
    rows_1 = -(-(2 * hidden + width + 128) // unit) * unit
    rows_2 = -(-(3 * width + 128) // unit) * unit
    pairs = width // 128
    near = int(tokens <= 1024)

    tile, first_cols, side_cols = call(
        tile_kernel,
        [((col_count, 384), BF16), ((RIGHT, 384), BF16), ((RIGHT, 384), BF16)],
        [latent, cotangent, item_ids, positions, gap_mask],
        far_in=range(5), near_out=range(3),
    )

    def shift(value, step_row, step_col, wanted):
        route = [
            (i * n_cols + j, (i + step_row) % n_rows * n_cols + j + step_col)
            for i in range(n_rows)
            for j in range(n_cols)
            if 0 <= j + step_col < n_cols and wanted((i + step_row) % n_rows)
        ]
        return lax.ppermute(value, ("row", "col"), route)

    def needs_right(i):
        return (i + 1) * cw + HALO + 1 > col_count

    tiles = [shift(tile, k, 0, lambda i: True) for k in range(1, n_rows)]
    rights = [shift(first_cols, k, -1, needs_right) for k in range(1, n_rows)]
    route = [(j, j + 1) for j in range(n_cols - 1)]
    route += [
        (i * n_cols + j, i * n_cols + j - 1) for i in range(1, n_rows) if needs_right(i) for j in range(1, n_cols)
    ]
    side = lax.ppermute(side_cols, ("row", "col"), route)

    tl, feat, time_pre, condition, cond_act, table = call(
        item_kernel,
        [((8, items), jnp.int32), ((time_weight.shape[0], items), BF16), ((items, width), F32), ((items, width), F32),
         ((items, width), BF16), ((4 * POSITIONS, width), BF16)],
        [timesteps, labels, time_weight, time_bias, clock_weight, clock_bias, class_table],
        us=5,
    )

    dims = (n_rows, hp, cw, tokens, ni, rows_1 // 2)
    heads = ((pairs, tokens, 128), BF16)
    ins = [tile, side, *tiles, *rights, cond_act, table, patch_bias, modulation_bias, query_bias, value_bias, output_bias,
           hidden_bias, return_bias, final_offsets, readout_bias, patch_weight, modulation_weight, final_modulation,
           attention_weight, output_weight, hidden_weight, return_weight, readout_weight.T]
    q, k, v, d_at, rows, aux, res, mid, attn_in, patches, member, turned, spread, spoken, item_main, keep, out = call(
        functools.partial(main_kernel, dims),
        [heads, heads, heads, heads, ((8, tokens), F32), ((tokens, 128), F32), ((tokens, width), F32),
         ((tokens, width), F32), ((tokens, width), BF16), ((tokens, 128), BF16), ((tokens, 128), BF16),
         ((16, tokens), BF16), ((128, 8 * width), BF16), ((tokens, 128), BF16), ((6 * ni + 8, width), BF16),
         ((rows_1 // 2, width), BF16), ((rows_1 // 2, width), BF16)],
        ins,
        [((n_rows, LEFT + 64 + RIGHT, 384), BF16), ((tokens, 128), BF16), ((pairs, tokens, 128), BF16),
         ((tokens, width), BF16), ((tokens, hidden), BF16), ((tokens, hidden), BF16), ((tokens, width), BF16),
         ((tokens, width), BF16), ((tokens, width), BF16), ((SECOND, hidden), F32), ((16, 8 * width), F32),
         ((128, width), F32), ((2, rows_1 // 2, width), BF16)],
        us=30, room=36 if near else 60, near_out=range(17 * near), near_in=range(len(ins) * near),
    )
    shape = (n_rows, n_cols)
    lines = n_cols // 4
    got = send(out, *shape, flip_col=1)

    part = ((1, tokens, 128), BF16)
    total = ((1, tokens, 128), F32)
    d_first = call(
        functools.partial(attend_back_kernel, hp, 0), [part] * 3, [q, k, v, d_at, rows, aux], [total] * 2,
        us=4, room=24 if near else 60, near_in=range(6 * near), near_out=range(3 * near),
    )
    parts = add_up([keep, got], 2 * n_rows, plane_spot, after=[d_first[0]])
    got = to_plane(parts, *shape)
    dims = (n_rows, hp, cw, tokens, ni, rows_2 // 2)
    part = ((pairs - 1, tokens, 128), BF16)
    total = ((pairs - 1, tokens, 128), F32)
    result = call(
        functools.partial(back_kernel, dims),
        [((rows_2 // 2, width), BF16)] * 2 + [((2 * ni + 24, width), BF16)]
        + [((64, 256), BF16)] * n_rows + [((RIGHT, 256), BF16)] * n_rows,
        [q, k, v, d_at, rows, aux, *d_first, attn_in, res, mid, patches, member, turned, spread, spoken,
         attention_weight, patch_weight],
        [part] * 3 + [total] * 2 + [((128, width), F32), ((2, rows_2 // 2, width), BF16)]
        + [((tokens, width), BF16), ((16, 2 * width), F32), ((n_rows, 64 + RIGHT, 256), F32)],
        us=14, after=[parts[0]], room=32 if near else 60, near_in=range(17 * near),
        near_out=range((3 + 2 * n_rows) * near),
    )
    keep_2, out_2, item_back = result[:3]
    got_2 = send(out_2, *shape, flip_col=1)
    mine, over = result[3 : 3 + n_rows], result[3 + n_rows :]
    share_1 = rows_1 // (n_rows * n_cols)
    share_2 = rows_2 // (4 * n_rows)

    parts = add_up([parts[0]] + got, lines, line_spot, after=[item_back])
    got = to_line(parts, *shape)
    parts_2 = add_up([keep_2, got_2], 2 * n_rows, plane_spot, after=[parts[0]])
    got_2 = to_plane(parts_2, *shape)
    mine = [mine[0]] + [shift(mine[k], k, 0, lambda i: True) for k in range(1, n_rows)]
    over = [shift(over[k], k, 1, lambda i: True) for k in range(n_rows)]
    velocity, latent_grad = call(
        functools.partial(canvas_kernel, n_rows), [(latent.shape, BF16), (latent.shape, F32)], [*mine, *over],
        near_in=range(2 * n_rows),
    )
    part = add_below([parts[0]] + got, item_main, after=[velocity])
    part_2 = add_below([parts_2[0]] + got_2, item_back)
    block = stack([part] + to_line([part] * lines, *shape), after=[part_2])
    lists = [part_2] + to_line([part_2] * lines, *shape)
    (block_2,) = call(
        functools.partial(line_kernel, share_2), [((share_2 + lines * item_back.shape[0], width), BF16)], lists,
        [((lines, share_2, width), F32)], near_in=range(lines), near_out=(0,),
    )
    plane = stack([block] + to_plane([block] * (2 * n_rows), *shape), after=[block_2])
    blocks = plane, send(plane, *shape, flip_col=1)
    got_2 = to_plane([block_2] * (2 * n_rows), *shape)
    devices = n_rows * n_cols
    vector = ((width,), F32)
    return_grad, hidden_grad, output_grad, readout_grad, return_b, hidden_b, output_b, readout_b = call(
        functools.partial(first_out_kernel, shape),
        [((hidden, width), F32), ((width, hidden), F32), ((width, width), F32), ((16, width), F32), vector,
         ((hidden,), F32), vector, ((16,), F32)],
        blocks,
        [((devices, share_1, width), F32)],
        us=3, room=32, near_in=range(2),
    )
    part_mod, final_grad, part_b, final_b, d_cond, pick = call(
        functools.partial(item_condition_kernel, shape, ni, share_1),
        [((width, 6 * width), F32), ((width, 2 * width), F32), ((4 * width,), F32), ((2 * width,), F32),
         ((items, width), F32), ((items, devices * ni), BF16)],
        [*blocks, tl, cond_act, modulation_weight, final_modulation],
        [((6, devices, ni, width), F32), ((width, 4 * width), F32), ((8, width), F32)],
        us=5, room=32, near_in=range(6), near_out=(2, 4, 5), hand_out=(0,),
    )
    plane = stack([block_2] + got_2, after=[return_b, d_cond])
    blocks_2 = plane, send(plane, *shape, flip_col=1)

    modulation_grad, table_grad, clock_grad, time_grad, modulation_b, clock_b, time_b, patch_grad, patch_b = call(
        functools.partial(condition_kernel, shape, ni, share_2),
        [((width, 6 * width), F32), (class_table.shape, F32), ((width, width), F32), (time_weight.shape, F32),
         ((6 * width,), F32), vector, vector, ((16, width), F32), vector],
        [*blocks_2, tl, feat, time_pre, condition, cond_act, modulation_weight, clock_weight, part_b, d_cond, pick,
         part_mod],
        [((2, devices, ni, width), F32), ((width, 2 * width), F32), (class_table.shape, F32), ((devices, 24, width), F32)],
        us=5, room=32, near_in=range(12), hand_out=(0, 1), alias=12,
    )
    attention_grad, query_b, value_b = call(
        functools.partial(second_out_kernel, shape),
        [((width, 3 * width), F32), vector, vector],
        blocks_2,
        [((4 * n_rows, share_2, width), F32)],
        near_in=range(2),
    )
    return (
        velocity, latent_grad, patch_grad, patch_b, time_grad, time_b, clock_grad, clock_b, table_grad, modulation_grad,
        modulation_b, attention_grad, query_b, value_b, output_grad, output_b, hidden_grad, hidden_b, return_grad,
        return_b, final_grad, final_b, readout_grad.T, readout_b,
    )


def solution(mesh):
    canvas, grid = P(None, "row", "col"), P("row", "col")
    return jax.shard_map(
        local,
        mesh=mesh,
        in_specs=(canvas, canvas, grid, canvas, grid) + (P(),) * 24,
        out_specs=(canvas, canvas) + (P(),) * 22,
        check_vma=False,
    )
```

```python
import functools
import math

import jax
import jax.numpy as jnp
from jax import lax
from jax.experimental import pallas as pl
from jax.experimental.pallas import tpu as pltpu
from jax.sharding import PartitionSpec as P

HEADS = 6
HALO = 16
LEAST = 8
BLOCK = 256
FIRST, SECOND, THIRD = 384, 256, 384
LEFT = 16
RIGHT = 32
POSITIONS = 128
F32 = jnp.float32
BF16 = jnp.bfloat16
FLOPS_US = 1_150_000_000
BYTES_US = 3_700_000


def iota(shape, dim):
    return lax.broadcasted_iota(jnp.int32, shape, dim)


def mm(a, b):
    return jnp.dot(a, b, preferred_element_type=F32)


def mm_t(a, b):
    return lax.dot_general(a, b, (((1,), (1,)), ((), ())), preferred_element_type=F32)


def t_mm(a, b):
    return lax.dot_general(a, b, (((0,), (0,)), ((), ())), preferred_element_type=F32)


def low(v):
    return v.astype(BF16)


def one(cond):
    return jnp.where(cond, 1.0, 0.0).astype(BF16)


def sigmoid(v):
    return 1.0 / (1.0 + jnp.exp(-v))


def layer_norm(v):
    center = v - jnp.mean(v, axis=-1, keepdims=True)
    inverse = lax.rsqrt(jnp.mean(center * center, axis=-1, keepdims=True) + 1e-06)
    return center * inverse, inverse


def norm_back(normed, inverse, grad):
    mean_grad = jnp.mean(grad, axis=-1, keepdims=True)
    mean_cross = jnp.mean(grad * normed, axis=-1, keepdims=True)
    return inverse * (grad - mean_grad - normed * mean_cross)


def call(
    body, outs, ins, scratch=(), near_in=(), near_out=(), far_in=(), hand_out=(), alias=None, after=(), us=2, room=16
):
    spec = pl.BlockSpec(memory_space=pltpu.VMEM)
    away = pl.BlockSpec(memory_space=pl.ANY)
    used = len(ins)

    def run(*refs):
        body(*refs[:used], *refs[used + len(after) :])

    ins = [
        pltpu.with_memory_space_constraint(a, pltpu.VMEM if n in near_in else pltpu.HBM)
        if n in near_in or n in far_in else a
        for n, a in enumerate(ins)
    ]
    return pl.pallas_call(
        run,
        out_shape=[
            (pltpu.VMEM if n in near_out else jax.ShapeDtypeStruct)(shape, dtype)
            for n, (shape, dtype) in enumerate(outs)
        ],
        in_specs=[away if n == alias else spec for n in range(used)] + [away] * len(after),
        out_specs=[away if n in hand_out else spec for n in range(len(outs))],
        scratch_shapes=[pltpu.VMEM(shape, dtype) for shape, dtype in scratch]
        + [pltpu.SemaphoreType.DMA(())] * len(hand_out),
        input_output_aliases={} if alias is None else {alias: 0},
        compiler_params=pltpu.CompilerParams(vmem_limit_bytes=room * 1024 * 1024),
        cost_estimate=pl.CostEstimate(flops=us * FLOPS_US, bytes_accessed=us * BYTES_US, transcendentals=0),
    )(*ins, *after)


def line(ref, start=0, count=None):
    count = ref.shape[0] if count is None else count
    return ref[start : start + count].astype(F32).reshape(1, count)


def lane_fold(rows):
    lane = iota((rows, 128), 1)
    feature = 8 * (1 - (lane & 1)) + 4 * (1 - (lane >> 6)) + ((lane >> 4) & 3)
    return one(iota((rows, 128), 0) == feature)


def tile_kernel(lat_ref, cot_ref, ids_ref, pos_ref, gap_ref, tile_ref, first_ref, side_ref):
    cols = ids_ref.shape[1]
    pieces = []
    for ref in (lat_ref, cot_ref):
        flat = ref[...].reshape(64, 2 * cols)
        for side in (0, 1):
            pick = one(iota((cols, 2 * cols), 1) == 2 * iota((cols, 2 * cols), 0) + side)
            pieces.append(mm_t(pick, flat))
    tag = ids_ref[...] + 1
    meta = jnp.concatenate(
        [tag >> 8, tag & 255, pos_ref[0], pos_ref[1], gap_ref[...], jnp.zeros((88, cols), jnp.int32)], axis=0
    ).astype(F32)
    pieces.append(mm_t(one(iota((cols, cols), 0) == iota((cols, cols), 1)), low(meta)))
    tile = low(jnp.concatenate(pieces, axis=1))
    tile_ref[...] = tile
    first_ref[...] = tile[:RIGHT]
    side_ref[...] = tile[:RIGHT]

    @pl.when(lax.axis_index("row") == 0)
    def _():
        side_ref[0:LEFT, :] = tile[cols - LEFT :]


def item_kernel(
    steps_ref, labels_ref, tw_ref, tb_ref, cw_ref, cb_ref, ct_ref, tl_ref, feat_ref, pre_ref, cond_ref, act_ref, table_ref
):
    items = tl_ref.shape[1]
    count = steps_ref.shape[0]
    tl_ref[...] = jnp.zeros_like(tl_ref)
    tl_ref[0:1, 0:count] = steps_ref[...].reshape(1, count)
    tl_ref[1:2, 0:count] = labels_ref[...].reshape(1, count)
    half = tw_ref.shape[0] // 2
    steps = tl_ref[0:1, :].astype(F32)
    freq = jnp.exp(iota((half, 1), 0).astype(F32) * (-math.log(10000.0) / half))
    angle = freq * steps
    feat_ref[0:half, :] = low(jnp.cos(angle))
    feat_ref[half:, :] = low(jnp.sin(angle))
    pre = t_mm(feat_ref[...], tw_ref[...]) + line(tb_ref)
    pre_ref[...] = pre
    hidden = low(pre * sigmoid(pre))
    classes = ct_ref.shape[0]
    pick = one(iota((classes, items), 0) == tl_ref[1:2, :])
    cond = mm(hidden, cw_ref[...]) + line(cb_ref) + t_mm(pick, ct_ref[...])
    cond_ref[...] = cond
    act_ref[...] = low(cond * sigmoid(cond))
    width = table_ref.shape[1]
    quarter = width // 4
    shape = (2 * POSITIONS, width)
    lane = iota(shape, 1)
    row = iota(shape, 0)
    second = lane >= 2 * quarter
    within = jnp.where(second, lane - 2 * quarter, lane)
    cosine = within >= quarter
    index = jnp.where(cosine, within - quarter, within)
    omega = jnp.exp(index.astype(F32) * (-math.log(10000.0) / quarter))
    angle = (row & (POSITIONS - 1)).astype(F32) * omega
    value = jnp.where(cosine, jnp.cos(angle), jnp.sin(angle))
    value = jnp.where(jnp.where(second, 1, 0) == jnp.where(row >= POSITIONS, 1, 0), value, 0.0)
    high = low(value)
    table_ref[0 : 2 * POSITIONS, :] = high
    table_ref[2 * POSITIONS :, :] = low(value - high.astype(F32))


def row_mask(q, i, shape):
    return ((q * 16 + (iota(shape, 1) & 15) - 1) >> 1) == i


def main_kernel(dims, *refs):
    n_rows, hp, cw, tokens, ni, half_rows = dims
    own_ref, side_ref = refs[0:2]
    tiles = refs[2 : 1 + n_rows]
    rights = refs[1 + n_rows : 2 * n_rows]
    (act_ref, table_ref, pb_ref, mb_ref, qb_ref, vb_ref, ob_ref, hb_ref, rb_ref, fb_ref, lb_ref,
     pw_ref, mw_ref, fw_ref, aw_ref, ow_ref, hw_ref, rw_ref, low_ref,
     q_ref, k_ref, v_ref, da_ref, rows_ref, aux_ref, res_ref, mid_ref, in_ref, x_ref, mem_ref, turn_ref, ms_ref, vel_ref,
     item_ref, keep_ref, send_ref,
     es, ct_s, at_s, mlp_s, ha_s, dh_s, dbm_s, dba_s, ri_s, gd_s, dacc, small, g_s) = refs[2 * n_rows :]
    width = res_ref.shape[1]
    pairs = width // 128
    r = lax.axis_index("row")
    core = lax.axis_index("col") & 1
    shift = int(math.log2(hp))

    es[...] = jnp.zeros_like(es)
    es[r, LEFT : LEFT + 64, :] = own_ref[...]
    for k in range(1, n_rows):
        other = lax.rem(r - k + n_rows, n_rows)
        es[other, LEFT : LEFT + 64, :] = tiles[k - 1][...]
        es[other, LEFT + 64 :, :] = rights[k - 1][...]

    @pl.when(r == 0)
    def _():
        es[r, 0:LEFT, :] = side_ref[0:LEFT, :]

    @pl.when(r > 0)
    def _():
        es[r, LEFT + 64 :, :] = side_ref[...]

    meta = es[r, :, 256:384].astype(F32)
    lane = iota(meta.shape, 1)
    weighted = meta * jnp.where(lane == 0, 256.0, jnp.where(lane == 8, 1.0, 0.0))
    down = iota(meta.shape, 0)
    start = LEFT + r * cw
    tag_prev = jnp.sum(jnp.where(down == start - 1, weighted, 0.0)).astype(jnp.int32)
    tag_last = jnp.sum(jnp.where(down == start + cw - 1, weighted, 0.0)).astype(jnp.int32)
    tag_first = jnp.sum(jnp.where(down == start, weighted, 0.0)).astype(jnp.int32)
    strip_prev = jnp.where(tag_prev == 0, ((tag_first - 1) >> 1) - 1, (tag_prev - 1) >> 1)
    strip_last = (tag_last - 1) >> 1
    base = 2 * (strip_prev + 1)

    pick = one(iota((16, act_ref.shape[0]), 1) == base + iota((16, act_ref.shape[0]), 0))
    own_act = low(mm(pick, act_ref[...]))
    ms_ref[48:, :] = jnp.zeros_like(ms_ref[48:, :])
    for b in range(8):
        cols = slice(b * width, (b + 1) * width)
        if b < 6:
            value = mm(own_act, mw_ref[:, cols]) + line(mb_ref, b * width, width)
        else:
            value = mm(own_act, fw_ref[:, (b - 6) * width : (b - 5) * width]) + line(fb_ref, (b - 6) * width, width)
        p0 = low(value)
        rest = value - p0.astype(F32)
        p1 = low(rest)
        ms_ref[0:16, cols] = p0
        ms_ref[16:32, cols] = p1
        ms_ref[32:48, cols] = low(rest - p1.astype(F32))

    def mod(mem, b, n=1):
        return mm(mem, ms_ref[:, b * width : (b + n) * width])

    fold = lane_fold(16)
    embed = low(t_mm(fold, pw_ref[...]))
    unread = low(t_mm(low_ref[...], fold))
    b_lanes = iota((BLOCK, 128), 1)
    is_b1 = b_lanes >= 64
    half_lanes = (one(b_lanes < 64), one(is_b1))

    lanes = iota((FIRST, 128), 1)
    second_side = lanes >= 64

    def first(tb, carry):
        t0 = pl.multiple_of(tb * FIRST, FIRST)
        rows = pl.ds(t0, FIRST)
        token = t0 + iota((FIRST, 1), 0)
        j = token >> shift
        i = token & (hp - 1)
        spot = iota((FIRST, LEFT + 64 + RIGHT), 1)
        rep0 = one(spot == start + j)
        rep1 = one(spot == start + j + 1)
        x = jnp.zeros((FIRST, 128), F32)
        c = jnp.zeros((FIRST, 128), F32)
        m = jnp.zeros((FIRST, 128), F32)
        for q in range(n_rows):
            here = mm(rep0, es[q])
            beside = mm(rep1, es[q, :, 0:256])
            mask = row_mask(q, i, (FIRST, 128))
            x = x + jnp.where(mask, jnp.where(second_side, here[:, 0:128], beside[:, 0:128]), 0.0)
            c = c + jnp.where(mask, jnp.where(second_side, here[:, 128:256], beside[:, 128:256]), 0.0)
            m = m + jnp.where((q * 8 + (lanes & 7)) == i, here[:, 256:384], 0.0)
        x = low(x)
        m = low(m)
        x_ref[rows, :] = x
        ml = iota((128, 128), 0)
        mc = iota((128, 128), 1)
        kind = ml >> 3
        gather = jnp.where(
            (mc == 0) & (kind == 0), 256.0,
            jnp.where(((mc == 0) & (kind == 1)) | ((mc >= 1) & (mc <= 3) & (kind == mc + 1)), 1.0, 0.0),
        ).astype(BF16)
        cols = mm(m, gather)
        rl = iota((8, 128), 1) >> 3
        rr = iota((8, 128), 0)
        row_pick = jnp.where((rr == 6) & (rl == 0), 256.0, jnp.where((rr == 6) & (rl == 1), 1.0, 0.0)).astype(BF16)
        across = mm_t(row_pick, m)
        rows_ref[:, rows] = across
        tag_row = across[6:7, :].astype(jnp.int32)
        strip_row = (tag_row - 1) >> 1
        turn_ref[:, rows] = one(
            (tag_row - 1 - base == iota((16, FIRST), 0)) & (strip_row > strip_prev) & (strip_row <= strip_last)
        )
        tag = cols[:, 0:1]
        gap = cols[:, 3:4]
        tag_i = tag.astype(jnp.int32)
        strip = (tag_i - 1) >> 1
        owned = (strip > strip_prev) & (strip <= strip_last)
        act = jnp.where(owned, gap, 0.0)
        aux_ref[rows, :] = jnp.where(lanes == 0, tag * gap, jnp.where(lanes == 1, act, 0.0))
        item = tag_i - 1 - base
        mem = one((item == (lanes & 15)) & (lanes < 48) & owned)
        mem_ref[rows, :] = mem
        ct_s[rows, :] = low(c * act)
        p0 = cols[:, 1:2].astype(jnp.int32)
        p1 = cols[:, 2:3].astype(jnp.int32) + POSITIONS
        spot = iota((FIRST, 2 * POSITIONS), 1)
        place = one((spot == p0) | (spot == p1))
        res = (
            mm(x, embed) + line(pb_ref)
            + (mm(place, table_ref[0 : 2 * POSITIONS, :]) + mm(place, table_ref[2 * POSITIONS :, :]))
        )
        res_ref[rows, :] = res
        normed, _ = layer_norm(res)
        ab = mod(mem, 0, 2)
        attn_in = low(normed * (1.0 + ab[:, width:]) + ab[:, :width])
        in_ref[rows, :] = attn_in
        for part, ref in enumerate((q_ref, k_ref, v_ref)):
            value = mm(attn_in, aw_ref[:, part * width : (part + 1) * width])
            if part != 1:
                value = value + line(vb_ref if part else qb_ref)
            value = low(value)
            if part == 0:
                value = value * BF16(1.0 / math.sqrt(width // HEADS))
            for p in range(pairs):
                ref[p, rows, :] = value[:, p * 128 : (p + 1) * 128]
        return carry

    lax.fori_loop(0, tokens // FIRST, first, 0)

    for qb in range(tokens // BLOCK):
        qs = slice(qb * BLOCK, (qb + 1) * BLOCK)
        ks = key_range(qb, hp, tokens)
        q_tag = rows_ref[6:7, qs]
        k_tag = aux_ref[ks, 0:1]
        allowed = k_tag == q_tag
        for p in range(pairs):
            query = q_ref[p, qs, :]
            key = k_ref[p, ks, :]
            value = v_ref[p, ks, :]
            halves = []
            for e in range(2):
                scores = jnp.where(allowed, mm_t(key, query * half_lanes[e]), -1e30)
                top = jnp.max(scores, axis=0, keepdims=True)
                expo = jnp.exp(scores - top)
                total = jnp.sum(expo, axis=0, keepdims=True)
                rows_ref[2 * p + e : 2 * p + e + 1, qs] = top + jnp.log(total)
                halves.append(t_mm(low(expo * (1.0 / total)), value))
            at_s[p, qs, :] = low(jnp.where(is_b1, halves[1], halves[0]))

    dacc[...] = jnp.zeros_like(dacc)
    small[...] = jnp.zeros_like(small)

    def second(tb, carry):
        t0 = pl.multiple_of(tb * SECOND, SECOND)
        rows = pl.ds(t0, SECOND)
        mem = mem_ref[rows, :]

        turned = turn_ref[:, rows]

        def item_sum(b, grad):
            dacc[:, b * width : (b + 1) * width] += mm(turned, low(grad))

        attended = jnp.concatenate([at_s[p, rows, :] for p in range(pairs)], axis=1)
        branch_a = mm(attended, ow_ref[...]) + line(ob_ref)
        gate_a = mod(mem, 2)
        mid = res_ref[rows, :] + gate_a * branch_a
        norm_mid, inv_mid = layer_norm(mid)
        scale_m = 1.0 + mod(mem, 4)
        mlp_in = low(norm_mid * scale_m + mod(mem, 3))
        mlp_s[rows, :] = mlp_in
        hidden = hw_ref.shape[1]
        branch_m = jnp.zeros((SECOND, width), F32)
        for n in range(hidden // width):
            part = slice(n * width, (n + 1) * width)
            pre = mm(mlp_in, hw_ref[:, part]) + line(hb_ref, n * width, width)
            square = pre * pre
            c0 = math.sqrt(2.0 / math.pi)
            t = jnp.tanh(pre * (c0 + (c0 * 0.044715) * square))
            up = 0.5 + 0.5 * t
            act = low(pre * up)
            gd_s[:, part] = up + (0.5 * pre) * (1.0 - t * t) * (c0 + (3.0 * c0 * 0.044715) * square)
            ha_s[rows, part] = act
            branch_m = branch_m + mm(act, rw_ref[part, :])
        branch_m = branch_m + line(rb_ref)
        gate_m = mod(mem, 5)
        norm_out, inv_out = layer_norm(mid + gate_m * branch_m)
        scale_f = 1.0 + mod(mem, 7)
        readout_in = low(norm_out * scale_f + mod(mem, 6))
        ri_s[rows, :] = readout_in
        active = aux_ref[rows, 1:2]
        bias_lanes = mm(low(line(lb_ref) + jnp.zeros((8, 16), F32)), fold)[0:1, :]
        vel_ref[rows, :] = low((mm(readout_in, unread) + bias_lanes) * active)
        d_read = mm_t(ct_s[rows, :], unread)
        item_sum(6, d_read)
        item_sum(7, d_read * norm_out)
        d_out = norm_back(norm_out, inv_out, d_read * scale_f)
        item_sum(5, d_out * branch_m)
        d_bm = low(d_out * gate_m)
        dbm_s[rows, :] = d_bm
        small[16:17, :] += jnp.sum(d_bm.astype(F32), axis=0, keepdims=True)
        d_mlp = jnp.zeros((SECOND, width), F32)
        for n in range(hidden // width):
            part = slice(n * width, (n + 1) * width)
            d_hid = low(mm_t(d_bm, rw_ref[part, :]) * gd_s[:, part])
            dh_s[rows, part] = d_hid
            small[17 + n : 18 + n, :] += jnp.sum(d_hid.astype(F32), axis=0, keepdims=True)
            d_mlp = d_mlp + mm_t(d_hid, hw_ref[:, part])
        item_sum(3, d_mlp)
        item_sum(4, d_mlp * norm_mid)
        d_mid = d_out + norm_back(norm_mid, inv_mid, d_mlp * scale_m)
        mid_ref[rows, :] = d_mid
        item_sum(2, d_mid * branch_a)
        d_ba = low(d_mid * gate_a)
        dba_s[rows, :] = d_ba
        small[21:22, :] += jnp.sum(d_ba.astype(F32), axis=0, keepdims=True)
        d_at = low(mm_t(d_ba, ow_ref[...]))
        for p in range(pairs):
            da_ref[p, rows, :] = d_at[:, p * 128 : (p + 1) * 128]
        return carry

    lax.fori_loop(0, tokens // SECOND, second, 0)
    rows = [dacc[0:ni, b * width : (b + 1) * width] for b in range(2, 8)]
    spot = ((core * 2 * n_rows + plane_spot()) * (lax.axis_size("col") // 4) + line_spot()) * ni
    index = iota((4, width), 0) * width + iota((4, width), 1) - spot
    number = jnp.where((index >= 0) & (index < ni), base + index, 0)
    rows += [(number >> 8).astype(F32), (number & 255).astype(F32)]
    item_ref[...] = low(jnp.concatenate(rows, axis=0))

    g_s[...] = jnp.zeros_like(g_s)
    put = functools.partial(put_rows, g_s, half_rows)
    n_hidden = hw_ref.shape[1] // width
    for n in range(n_hidden):
        part = slice(n * width, (n + 1) * width)
        put(n * width, low(t_mm(ha_s[:, part], dbm_s[...])))
    grad = low(t_mm(mlp_s[...], dh_s[...]))
    for n in range(n_hidden):
        put((n_hidden + n) * width, grad[:, n * width : (n + 1) * width])
    attended = jnp.concatenate([at_s[p] for p in range(pairs)], axis=1)
    put(2 * n_hidden * width, low(t_mm(attended, dba_s[...])))
    ones = jnp.ones((8, tokens), BF16)
    small[0:16, :] = mm(fold, low(t_mm(ct_s[...], ri_s[...])))
    sums = mm(ones, ct_s[...])
    small[22:23, 0:128] = mm_t(jnp.broadcast_to(low(sums[0:1, :]), (8, 128)), lane_fold(128))[0:1, :]
    put((2 * n_hidden + 1) * width, low(small[...]))
    keep_ref[...] = g_s[core]
    send_ref[...] = g_s[1 - core]


def put_rows(g_s, half_rows, row, value):
    count = value.shape[0]
    done = 0
    while done < count:
        side, at = divmod(row + done, half_rows)
        take = min(count - done, half_rows - at)
        g_s[side, at : at + take, :] = value[done : done + take, :]
        done += take


def key_range(qb, hp, tokens):
    first_col = (qb * BLOCK) // hp
    last_col = ((qb + 1) * BLOCK - 1) // hp
    return slice(max(0, first_col - HALO) * hp, min(tokens, (last_col + 1 + HALO) * hp))


def attend_back_kernel(hp, first, q_ref, k_ref, v_ref, da_ref, rows_ref, aux_ref, dq_ref, dk_ref, dv_ref, dk_s, dv_s):
    tokens = q_ref.shape[1]
    b_lanes = iota((BLOCK, 128), 1)
    is_b1 = b_lanes >= 64
    half_lanes = (one(b_lanes < 64), one(is_b1))
    scale = 1.0 / math.sqrt(q_ref.shape[0] * 128 // HEADS)
    dk_s[...] = jnp.zeros_like(dk_s)
    dv_s[...] = jnp.zeros_like(dv_s)
    for qb in range(tokens // BLOCK):
        qs = slice(qb * BLOCK, (qb + 1) * BLOCK)
        ks = key_range(qb, hp, tokens)
        allowed = aux_ref[ks, 0:1] == rows_ref[6:7, qs]
        for n in range(dq_ref.shape[0]):
            p = first + n
            query = q_ref[p, qs, :]
            key = k_ref[p, ks, :]
            value = v_ref[p, ks, :]
            d_at = da_ref[p, qs, :]
            d_key = 0.0
            d_value = 0.0
            halves = []
            for e in range(2):
                q_half = query * half_lanes[e]
                d_half = d_at * half_lanes[e]
                scores = jnp.where(allowed, mm_t(key, q_half), -1e30)
                probs = jnp.exp(scores - rows_ref[2 * p + e : 2 * p + e + 1, qs])
                d_probs = mm_t(value, d_half)
                inner = jnp.sum(probs * d_probs, axis=0, keepdims=True)
                d_scores = low(probs * (d_probs - inner))
                d_value = d_value + mm(low(probs), d_half)
                d_key = d_key + mm(d_scores, q_half)
                halves.append(t_mm(d_scores, key))
            dk_s[n, ks, :] += d_key
            dv_s[n, ks, :] += d_value
            dq_ref[n, qs, :] = low(jnp.where(is_b1, halves[1], halves[0]) * scale)
    dk_ref[...] = low(dk_s[...])
    dv_ref[...] = low(dv_s[...])


def joined(refs, rows):
    return jnp.concatenate(
        [ref[n, rows, :] for kind in range(3) for ref in refs[kind::3] for n in range(ref.shape[0])], axis=1
    )


def weigh_attention(half_rows, in_ref, parts, keep_ref, send_ref, small, g_s):
    tokens, width = in_ref.shape
    core = lax.axis_index("col") & 1
    put = functools.partial(put_rows, g_s, half_rows)
    ones = jnp.ones((8, tokens), BF16)
    g_s[...] = jnp.zeros_like(g_s)
    small[...] = jnp.zeros_like(small)
    whole = joined(parts, slice(None))
    for n in range(3):
        grad = whole[:, n * width : (n + 1) * width]
        put(n * width, low(t_mm(in_ref[...], grad)))
        if n != 1:
            small[n // 2 : n // 2 + 1, :] = mm(ones, grad)[0:1, :]
    put(3 * width, low(small[...]))
    keep_ref[...] = g_s[core]
    send_ref[...] = g_s[1 - core]


def back_kernel(dims, *refs):
    n_rows, hp, cw, tokens, ni, half_rows = dims
    heads, done = refs[:6], refs[6:9]
    (in_ref, res_ref, mid_ref, x_ref, mem_ref, turn_ref, ms_ref, vel_ref, more_ref, aw_ref, pw_ref, keep_ref, send_ref,
     item_ref) = refs[9:23]
    frame_refs = refs[23 : 23 + n_rows]
    *rest, dk_s, dv_s, small, g_s, di_s, dacc, frame = refs[23 + n_rows :]
    parts = [*done, *rest]
    attend_back_kernel(hp, done[0].shape[0], *heads, *rest, dk_s, dv_s)
    weigh_attention(half_rows, in_ref, parts, keep_ref, send_ref, small, g_s)
    width = res_ref.shape[1]
    r = lax.axis_index("row")
    shift = int(math.log2(hp))

    embed = low(t_mm(lane_fold(16), pw_ref[...]))
    dacc[...] = jnp.zeros_like(dacc)
    frame[...] = jnp.zeros_like(frame)

    def third(tb, carry):
        t0 = pl.multiple_of(tb * THIRD, THIRD)
        rows = pl.ds(t0, THIRD)
        mem = mem_ref[rows, :]
        d_attn = mm_t(joined(parts, rows), aw_ref[...])
        normed, inverse = layer_norm(res_ref[rows, :])
        scale_a = 1.0 + mm(mem, ms_ref[:, width : 2 * width])
        turned = turn_ref[:, rows]
        dacc[:, 0:width] += mm(turned, low(d_attn))
        dacc[:, width : 2 * width] += mm(turned, low(d_attn * normed))
        d_in = low(mid_ref[rows, :] + norm_back(normed, inverse, d_attn * scale_a))
        di_s[rows, :] = d_in
        grad = low(mm_t(d_in, embed))
        both = jnp.concatenate([vel_ref[rows, :], grad], axis=1)
        token = t0 + iota((THIRD, 1), 0)
        j = token >> shift
        i = token & (hp - 1)
        spot = iota((THIRD, 64 + RIGHT), 1)
        rep = jnp.concatenate([one(spot == r * cw + j), one(spot == r * cw + j + 1)], axis=0)
        side = (iota((THIRD, 256), 1) >> 6) & 1
        for q in range(n_rows):
            mask = row_mask(q, i, (THIRD, 256))
            split = jnp.concatenate([both * one(mask & (side == 1)), both * one(mask & (side == 0))], axis=0)
            frame[q] += t_mm(rep, split)
        return carry

    lax.fori_loop(0, tokens // THIRD, third, 0)

    ones = jnp.ones((8, tokens), BF16)
    rows = [dacc[0:ni, 0:width], dacc[0:ni, width : 2 * width]]
    rows += [more_ref[...].astype(F32), mm(lane_fold(16), low(t_mm(x_ref[...], di_s[...]))), mm(ones, di_s[...])]
    item_ref[...] = low(jnp.concatenate(rows, axis=0))
    for k in range(n_rows):
        q = lax.rem(r + k, n_rows)
        frame_refs[k][...] = low(frame[q])


def frame_kernel(*refs):
    *ins, mine_ref, over_ref = refs
    total = ins[0][...].astype(F32)
    for ref in ins[1:]:
        total = total + ref[...].astype(F32)
    mine_ref[...] = low(total[0:64])
    over_ref[...] = low(total[64:])


def canvas_kernel(mine_ref, over_ref, vel_ref, grad_ref):
    extra = jnp.concatenate([over_ref[...].astype(F32), jnp.zeros((64 - RIGHT, 256), F32)], axis=0)
    total = low(mine_ref[...].astype(F32) + extra)
    for n, ref in enumerate((vel_ref, grad_ref)):
        value = 0.0
        for side in (0, 1):
            pick = one(iota((64, 128), 1) == 2 * iota((64, 128), 0) + side)
            value = value + t_mm(total[:, n * 128 + side * 64 : n * 128 + (side + 1) * 64], pick)
        ref[...] = value.reshape(ref.shape).astype(ref.dtype)


def add_kernel(count, me, *refs):
    outs = refs[len(refs) - count :]
    ins = refs[: len(refs) - count]
    spot = me()
    for m, out in enumerate(outs):
        at = jnp.bitwise_xor(spot, m) if count > 1 else 0
        total = ins[0][at].astype(F32)
        for ref in ins[1:]:
            total = total + ref[at].astype(F32)
        out[...] = low(total)


def plane_spot():
    return lax.axis_index("row") + lax.axis_size("row") * ((lax.axis_index("col") >> 1) & 1)


def line_spot():
    return lax.axis_index("col") >> 2


def send(value, n_rows, n_cols, flip_row=0, flip_col=0):
    route = [
        (i * n_cols + j, (i ^ flip_row) * n_cols + (j ^ flip_col)) for i in range(n_rows) for j in range(n_cols)
    ]
    return lax.ppermute(value, ("row", "col"), route)


def add_up(arrays, count, me, after=()):
    n, w = arrays[0].shape
    ins = [a.reshape(count, n // count, w) for a in arrays]
    return call(
        functools.partial(add_kernel, count, me), [((n // count, w), BF16)] * count, ins, after=after,
        near_in=range(len(ins)), near_out=range(count),
    )


def add_with_kernel(count, me, *refs):
    outs = refs[len(refs) - count :]
    *ins, more = refs[: len(refs) - count]
    spot = me()
    for m, out in enumerate(outs):
        at = jnp.bitwise_xor(spot, m)
        total = ins[0][at].astype(F32)
        for ref in ins[1:]:
            total = total + ref[at].astype(F32)
        out[0 : total.shape[0], :] = low(total)
        if m:
            out[total.shape[0] :, :] = more[...]


def add_tops_kernel(*refs):
    *ins, out = refs
    total = ins[0][...].astype(F32)
    for ref in ins[1:]:
        total = total + ref[0 : out.shape[0], :].astype(F32)
    out[...] = low(total)


def list_ends_kernel(*refs):
    own_ref, *ins, out = refs
    out[0] = own_ref[...]
    for m, ref in enumerate(ins):
        out[m + 1] = ref[ref.shape[0] - own_ref.shape[0] :, :]


def add_below_kernel(*refs):
    *ins, first, out = refs
    total = ins[0][...].astype(F32)
    for ref in ins[1:]:
        total = total + ref[...].astype(F32)
    out[0 : first.shape[0], :] = first[...]
    out[first.shape[0] :, :] = low(total)


def line_kernel(share, *refs):
    *ins, out, rows = refs
    spot = line_spot()
    for m, ref in enumerate(ins):
        out[m * share : (m + 1) * share, :] = ref[0:share, :]
        rows[jnp.bitwise_xor(spot, m)] = ref[share:, :].astype(F32)
    out[len(ins) * share :, :] = low(jnp.sum(rows[...], axis=0))


def copy_kernel(in_ref, out_ref):
    out_ref[...] = in_ref[...]


def to_plane(parts, n_rows, n_cols):
    return [
        send(parts[m], n_rows, n_cols, flip_row=m % n_rows, flip_col=2 * (m // n_rows)) for m in range(1, 2 * n_rows)
    ]


def to_line(parts, n_rows, n_cols):
    return [send(parts[m], n_rows, n_cols, flip_col=4 * m) for m in range(1, n_cols // 4)]


def stack_kernel(*refs):
    *ins, out = refs
    for n, ref in enumerate(ins):
        out[n] = ref[...]


def stack(arrays, after=()):
    return call(
        stack_kernel, [((len(arrays), *arrays[0].shape), BF16)], arrays, after=after, near_in=range(len(arrays)),
        near_out=(0,),
    )[0]


def for_planes(n_rows, body):
    core = lax.axis_index("col") & 1
    plane = plane_spot()
    for c in range(2):

        def step(m, carry, c=c):
            body(c, m, jnp.bitwise_xor(core, c) * 2 * n_rows + jnp.bitwise_xor(plane, m))
            return carry

        lax.fori_loop(0, 2 * n_rows, step, 0)


def for_parts(n_rows, n_cols, body):
    line = line_spot()

    def inner(c, m, at):
        for n in range(n_cols // 4):
            body(c, m, n, at * (n_cols // 4) + jnp.bitwise_xor(line, n))

    for_planes(n_rows, inner)


def weights_kernel(mesh_shape, *refs):
    n_rows, n_cols = mesh_shape
    blocks = refs[:2]
    ret_ref, hid_ref, out_ref, read_ref, rb_ref, hb_ref, ob_ref, lb_ref, att_ref, qb_ref, vb_ref, first, second = refs[2:]
    share = first.shape[1]

    def place(c, m, n, at):
        first[at] = blocks[c][m, n * share : (n + 1) * share, :].astype(F32)

    for_parts(n_rows, n_cols, place)

    def place_second(c, m, at):
        second[at] = blocks[c][m, n_cols // 4 * share :, :].astype(F32)

    for_planes(n_rows, place_second)
    flat = first[...].reshape(first.shape[0] * share, first.shape[2])
    width = flat.shape[1]
    hidden = ret_ref.shape[0]
    ret_ref[...] = flat[0:hidden]
    for n in range(hidden // width):
        hid_ref[:, n * width : (n + 1) * width] = flat[hidden + n * width : hidden + (n + 1) * width]
    out_ref[...] = flat[2 * hidden : 2 * hidden + width]
    at = 2 * hidden + width
    small = flat[at : at + 24]
    read_ref[...] = small[0:16]
    rb_ref[...] = small[16]
    for n in range(hidden // width):
        hb_ref[n * width : (n + 1) * width] = small[17 + n]
    ob_ref[...] = small[21]
    lb_ref[...] = small[22, 0:16]
    flat = second[...].reshape(second.shape[0] * second.shape[1], width)
    for n in range(3):
        att_ref[:, n * width : (n + 1) * width] = flat[n * width : (n + 1) * width]
    small = flat[3 * width : 3 * width + 8]
    qb_ref[...] = small[0]
    vb_ref[...] = small[1]


def condition_kernel(
    mesh_shape, ni, own_ref, other_ref, tl_ref, feat_ref, pre_ref, cond_ref, act_ref, mw_ref, fw_ref, cw_ref,
    mod_ref, fin_ref, table_ref, clock_ref, time_ref, mb_ref, fb_ref, cb_ref, tb_ref, patch_ref, pb_ref,
    dev_s, patch_s, ids_s,
):
    n_rows, n_cols = mesh_shape
    width = cw_ref.shape[0]
    items = tl_ref.shape[1]
    count = n_rows * n_cols
    ids_s[...] = jnp.zeros_like(ids_s)

    def place(c, m, n, at):
        part = (own_ref, other_ref)[c][m, n].astype(F32)
        for b in range(8):
            dev_s[b, at] = part[b * ni : (b + 1) * ni]
        ids_s[...] += part[8 * ni : 8 * ni + 8]
        patch_s[at] = part[8 * ni + 8 :]

    for_parts(n_rows, n_cols, place)
    patch = jnp.sum(patch_s[...], axis=0)
    patch_ref[...] = patch[0:16]
    pb_ref[...] = patch[16]
    ids = ids_s[...]
    numbers = ids[0:4] * 256.0 + ids[4:8]
    number = jnp.concatenate([numbers[k : k + 1, :] for k in range(-(-count * ni // width))], axis=1)[:, : count * ni]
    pick = one(iota((items, count * ni), 0).astype(F32) == number)
    ones = jnp.ones((8, items), BF16)
    act = act_ref[...]
    d_cond = jnp.zeros((items, width), F32)
    for b in range(8):
        grad = low(mm(pick, low(dev_s[b].reshape(count * ni, width))))
        total = mm(ones, grad)[0]
        if b < 6:
            cols = slice(b * width, (b + 1) * width)
            mb_ref[cols] = total
            mod_ref[:, cols] = t_mm(act, grad)
            d_cond = d_cond + mm_t(grad, mw_ref[:, cols])
        else:
            cols = slice((b - 6) * width, (b - 5) * width)
            fb_ref[cols] = total
            fin_ref[:, cols] = t_mm(act, grad)
            d_cond = d_cond + mm_t(grad, fw_ref[:, cols])
    cond = cond_ref[...]
    sigma = sigmoid(cond)
    d_cond = low(d_cond * (sigma * (1.0 + cond * (1.0 - sigma))))
    pre = pre_ref[...]
    sigma = sigmoid(pre)
    hidden = low(pre * sigma)
    classes = table_ref.shape[0]
    table_ref[...] = mm(one(iota((classes, items), 0) == tl_ref[1:2, :]), d_cond)
    clock_ref[...] = t_mm(hidden, d_cond)
    cb_ref[...] = mm(ones, d_cond)[0]
    d_time = low(mm_t(d_cond, cw_ref[...]) * (sigma * (1.0 + pre * (1.0 - sigma))))
    time_ref[...] = mm(feat_ref[...], d_time)
    tb_ref[...] = mm(ones, d_time)[0]


def local(
    latent, cotangent, item_ids, positions, gap_mask, timesteps, labels, patch_weight, patch_bias, time_weight,
    time_bias, clock_weight, clock_bias, class_table, modulation_weight, modulation_bias, attention_weight, query_bias,
    value_bias, output_weight, output_bias, hidden_weight, hidden_bias, return_weight, return_bias, final_modulation,
    final_offsets, readout_weight, readout_bias,
):
    n_rows, n_cols = lax.axis_size("row"), lax.axis_size("col")
    row_count, col_count = item_ids.shape
    width = patch_weight.shape[1]
    hidden = hidden_weight.shape[1]
    hp = n_rows * row_count
    cw = col_count // n_rows
    tokens = (cw + HALO) * hp
    ni = 2 * (-(-cw // LEAST))
    items = -(-(timesteps.shape[0] + 16) // 32) * 32
    unit = 8 * n_rows * n_cols
    rows_1 = -(-(2 * hidden + width + 128) // unit) * unit
    rows_2 = -(-(3 * width + 128) // unit) * unit
    pairs = width // 128
    near = int(tokens <= 1024)

    tile, first_cols, side_cols = call(
        tile_kernel,
        [((col_count, 384), BF16), ((RIGHT, 384), BF16), ((RIGHT, 384), BF16)],
        [latent, cotangent, item_ids, positions, gap_mask],
        far_in=range(5), near_out=range(3),
    )

    def shift(value, step_row, step_col, wanted):
        route = [
            (i * n_cols + j, (i + step_row) % n_rows * n_cols + j + step_col)
            for i in range(n_rows)
            for j in range(n_cols)
            if 0 <= j + step_col < n_cols and wanted((i + step_row) % n_rows)
        ]
        return lax.ppermute(value, ("row", "col"), route)

    def needs_right(i):
        return (i + 1) * cw + HALO + 1 > col_count

    tiles = [shift(tile, k, 0, lambda i: True) for k in range(1, n_rows)]
    rights = [shift(first_cols, k, -1, needs_right) for k in range(1, n_rows)]
    route = [(j, j + 1) for j in range(n_cols - 1)]
    route += [
        (i * n_cols + j, i * n_cols + j - 1) for i in range(1, n_rows) if needs_right(i) for j in range(1, n_cols)
    ]
    side = lax.ppermute(side_cols, ("row", "col"), route)

    tl, feat, time_pre, condition, cond_act, table = call(
        item_kernel,
        [((8, items), jnp.int32), ((time_weight.shape[0], items), BF16), ((items, width), F32), ((items, width), F32),
         ((items, width), BF16), ((4 * POSITIONS, width), BF16)],
        [timesteps, labels, time_weight, time_bias, clock_weight, clock_bias, class_table],
        us=5,
    )

    dims = (n_rows, hp, cw, tokens, ni, rows_1 // 2)
    heads = ((pairs, tokens, 128), BF16)
    ins = [tile, side, *tiles, *rights, cond_act, table, patch_bias, modulation_bias, query_bias, value_bias, output_bias,
           hidden_bias, return_bias, final_offsets, readout_bias, patch_weight, modulation_weight, final_modulation,
           attention_weight, output_weight, hidden_weight, return_weight, readout_weight.T]
    q, k, v, d_at, rows, aux, res, mid, attn_in, patches, member, turned, spread, spoken, item_main, keep, out = call(
        functools.partial(main_kernel, dims),
        [heads, heads, heads, heads, ((8, tokens), F32), ((tokens, 128), F32), ((tokens, width), F32),
         ((tokens, width), F32), ((tokens, width), BF16), ((tokens, 128), BF16), ((tokens, 128), BF16),
         ((16, tokens), BF16), ((128, 8 * width), BF16), ((tokens, 128), BF16), ((6 * ni + 8, width), BF16),
         ((rows_1 // 2, width), BF16), ((rows_1 // 2, width), BF16)],
        ins,
        [((n_rows, LEFT + 64 + RIGHT, 384), BF16), ((tokens, 128), BF16), ((pairs, tokens, 128), BF16),
         ((tokens, width), BF16), ((tokens, hidden), BF16), ((tokens, hidden), BF16), ((tokens, width), BF16),
         ((tokens, width), BF16), ((tokens, width), BF16), ((SECOND, hidden), F32), ((16, 8 * width), F32),
         ((128, width), F32), ((2, rows_1 // 2, width), BF16)],
        us=30, room=36 if near else 60, near_out=range(17 * near), near_in=range(len(ins) * near),
    )
    shape = (n_rows, n_cols)
    lines = n_cols // 4
    got = send(out, *shape, flip_col=1)

    part = ((1, tokens, 128), BF16)
    total = ((1, tokens, 128), F32)
    d_first = call(
        functools.partial(attend_back_kernel, hp, 0), [part] * 3, [q, k, v, d_at, rows, aux], [total] * 2,
        us=4, room=24 if near else 60, near_in=range(6 * near), near_out=range(3 * near),
    )
    parts = add_up([keep, got], 2 * n_rows, plane_spot, after=[d_first[0]])
    got = to_plane(parts, *shape)
    dims = (n_rows, hp, cw, tokens, ni, rows_2 // 2)
    part = ((pairs - 1, tokens, 128), BF16)
    total = ((pairs - 1, tokens, 128), F32)
    result = call(
        functools.partial(back_kernel, dims),
        [((rows_2 // 2, width), BF16)] * 2 + [((8 * ni + 32, width), BF16)]
        + [((64 + RIGHT, 256), BF16)] * n_rows,
        [q, k, v, d_at, rows, aux, *d_first, attn_in, res, mid, patches, member, turned, spread, spoken,
         item_main, attention_weight, patch_weight],
        [part] * 3 + [total] * 2 + [((128, width), F32), ((2, rows_2 // 2, width), BF16)]
        + [((tokens, width), BF16), ((16, 2 * width), F32), ((n_rows, 64 + RIGHT, 256), F32)],
        us=14, after=[parts[0]], room=32 if near else 60, near_in=range(18 * near),
        near_out=range((3 + n_rows) * near),
    )
    keep_2, out_2, items_own = result[:3]
    got_2 = send(out_2, *shape, flip_col=1)
    frames = result[3:]
    share_1 = rows_1 // (n_rows * n_cols)
    share_2 = rows_2 // (4 * n_rows)

    count = items_own.shape[0]
    ins = [a.reshape(lines, share_1, width) for a in (parts[0], *got)]
    parts = call(
        functools.partial(add_with_kernel, lines, line_spot),
        [((share_1 + (count if m else 0), width), BF16) for m in range(lines)], [*ins, items_own],
        near_in=range(len(ins) + 1), near_out=range(lines),
    )
    got = to_line(parts, *shape)
    parts_2 = add_up([keep_2, got_2], 2 * n_rows, plane_spot, after=[parts[0]])
    got_2 = to_plane(parts_2, *shape)
    (part,) = call(
        add_tops_kernel, [((share_1, width), BF16)], [parts[0], *got], near_in=range(lines), near_out=(0,),
        after=[parts_2[0]],
    )
    ins = [parts_2[0], *got_2, part]
    (both,) = call(
        add_below_kernel, [((share_1 + share_2, width), BF16)], ins, near_in=range(len(ins)), near_out=(0,),
    )
    got_both = to_line([both] * lines, *shape)
    (block_items,) = call(
        list_ends_kernel, [((lines, count, width), BF16)], [items_own, *got], near_in=range(lines), near_out=(0,),
        after=[both],
    )
    plane_items = to_plane([block_items] * (2 * n_rows), *shape)

    frames = [
        call(copy_kernel, [(a.shape, BF16)], [a], near_in=(0,), near_out=(0,), after=[both])[0] if k else a
        for k, a in enumerate(frames)
    ]
    frames = [frames[0]] + [shift(frames[k], k, 0, lambda i: True) for k in range(1, n_rows)]
    mine, over = call(
        frame_kernel, [((64, 256), BF16), ((RIGHT, 256), BF16)], frames, near_in=range(n_rows), near_out=(0, 1),
    )
    velocity, latent_grad = call(
        canvas_kernel, [(latent.shape, BF16), (latent.shape, F32)], [mine, shift(over, 0, 1, lambda i: True)],
        near_in=(0, 1),
    )
    (block,) = call(
        functools.partial(line_kernel, share_1), [((lines * share_1 + share_2, width), BF16)], [both, *got_both],
        [((lines, share_2, width), F32)], near_in=range(lines), near_out=(0,), after=[velocity],
    )
    plane_block = to_plane([block] * (2 * n_rows), *shape)
    blocks_items = stack([block_items] + plane_items, after=[block])
    blocks_items = blocks_items, send(blocks_items, *shape, flip_col=1)
    devices = n_rows * n_cols
    vector = ((width,), F32)
    (modulation_grad, final_grad, table_grad, clock_grad, time_grad, modulation_b, final_b, clock_b, time_b, patch_grad,
     patch_b) = call(
        functools.partial(condition_kernel, shape, ni),
        [((width, 6 * width), F32), ((width, 2 * width), F32), (class_table.shape, F32), ((width, width), F32),
         (time_weight.shape, F32), ((6 * width,), F32), ((2 * width,), F32), vector, vector, ((16, width), F32), vector],
        [*blocks_items, tl, feat, time_pre, condition, cond_act, modulation_weight, final_modulation, clock_weight],
        [((8, devices, ni, width), F32), ((devices, 24, width), F32), ((8, width), F32)],
        us=8, room=40, near_in=range(2),
    )
    plane = stack([block] + plane_block, after=[patch_b])
    (return_grad, hidden_grad, output_grad, readout_grad, return_b, hidden_b, output_b, readout_b, attention_grad, query_b,
     value_b) = call(
        functools.partial(weights_kernel, shape),
        [((hidden, width), F32), ((width, hidden), F32), ((width, width), F32), ((16, width), F32), vector,
         ((hidden,), F32), vector, ((16,), F32), ((width, 3 * width), F32), vector, vector],
        [plane, send(plane, *shape, flip_col=1)],
        [((devices, share_1, width), F32), ((4 * n_rows, share_2, width), F32)],
        us=4, room=36, near_in=range(2),
    )
    return (
        velocity, latent_grad, patch_grad, patch_b, time_grad, time_b, clock_grad, clock_b, table_grad, modulation_grad,
        modulation_b, attention_grad, query_b, value_b, output_grad, output_b, hidden_grad, hidden_b, return_grad,
        return_b, final_grad, final_b, readout_grad.T, readout_b,
    )


def solution(mesh):
    canvas, grid = P(None, "row", "col"), P("row", "col")
    return jax.shard_map(
        local,
        mesh=mesh,
        in_specs=(canvas, canvas, grid, canvas, grid) + (P(),) * 24,
        out_specs=(canvas, canvas) + (P(),) * 22,
        check_vma=False,
    )
```

```python
import functools
import math

import jax
import jax.numpy as jnp
from jax import lax
from jax.experimental import pallas as pl
from jax.experimental.pallas import tpu as pltpu
from jax.sharding import PartitionSpec as P

HEADS = 6
HALO = 16
LEAST = 8
BLOCK = 256
FIRST, SECOND, THIRD = 384, 256, 384
LEFT = 16
RIGHT = 32
POSITIONS = 128
F32 = jnp.float32
BF16 = jnp.bfloat16
FLOPS_US = 1_150_000_000
BYTES_US = 3_700_000


def iota(shape, dim):
    return lax.broadcasted_iota(jnp.int32, shape, dim)


def mm(a, b):
    return jnp.dot(a, b, preferred_element_type=F32)


def mm_t(a, b):
    return lax.dot_general(a, b, (((1,), (1,)), ((), ())), preferred_element_type=F32)


def t_mm(a, b):
    return lax.dot_general(a, b, (((0,), (0,)), ((), ())), preferred_element_type=F32)


def low(v):
    return v.astype(BF16)


def one(cond):
    return jnp.where(cond, 1.0, 0.0).astype(BF16)


def sigmoid(v):
    return 1.0 / (1.0 + jnp.exp(-v))


def layer_norm(v):
    center = v - jnp.mean(v, axis=-1, keepdims=True)
    inverse = lax.rsqrt(jnp.mean(center * center, axis=-1, keepdims=True) + 1e-06)
    return center * inverse, inverse


def norm_back(normed, inverse, grad):
    mean_grad = jnp.mean(grad, axis=-1, keepdims=True)
    mean_cross = jnp.mean(grad * normed, axis=-1, keepdims=True)
    return inverse * (grad - mean_grad - normed * mean_cross)


def call(
    body, outs, ins, scratch=(), near_in=(), near_out=(), far_in=(), hand_out=(), alias=None, after=(), us=2, room=16
):
    spec = pl.BlockSpec(memory_space=pltpu.VMEM)
    away = pl.BlockSpec(memory_space=pl.ANY)
    used = len(ins)

    def run(*refs):
        body(*refs[:used], *refs[used + len(after) :])

    ins = [
        pltpu.with_memory_space_constraint(a, pltpu.VMEM if n in near_in else pltpu.HBM)
        if n in near_in or n in far_in else a
        for n, a in enumerate(ins)
    ]
    return pl.pallas_call(
        run,
        out_shape=[
            (pltpu.VMEM if n in near_out else jax.ShapeDtypeStruct)(shape, dtype)
            for n, (shape, dtype) in enumerate(outs)
        ],
        in_specs=[away if n == alias else spec for n in range(used)] + [away] * len(after),
        out_specs=[away if n in hand_out else spec for n in range(len(outs))],
        scratch_shapes=[pltpu.VMEM(shape, dtype) for shape, dtype in scratch]
        + [pltpu.SemaphoreType.DMA(())] * len(hand_out),
        input_output_aliases={} if alias is None else {alias: 0},
        compiler_params=pltpu.CompilerParams(vmem_limit_bytes=room * 1024 * 1024),
        cost_estimate=pl.CostEstimate(flops=us * FLOPS_US, bytes_accessed=us * BYTES_US, transcendentals=0),
    )(*ins, *after)


def line(ref, start=0, count=None):
    count = ref.shape[0] if count is None else count
    return ref[start : start + count].astype(F32).reshape(1, count)


def lane_fold(rows):
    lane = iota((rows, 128), 1)
    feature = 8 * (1 - (lane & 1)) + 4 * (1 - (lane >> 6)) + ((lane >> 4) & 3)
    return one(iota((rows, 128), 0) == feature)


def tile_kernel(lat_ref, cot_ref, ids_ref, pos_ref, gap_ref, tile_ref, first_ref, side_ref):
    cols = ids_ref.shape[1]
    pieces = []
    for ref in (lat_ref, cot_ref):
        flat = ref[...].reshape(64, 2 * cols)
        for side in (0, 1):
            pick = one(iota((cols, 2 * cols), 1) == 2 * iota((cols, 2 * cols), 0) + side)
            pieces.append(mm_t(pick, flat))
    tag = ids_ref[...] + 1
    meta = jnp.concatenate(
        [tag >> 8, tag & 255, pos_ref[0], pos_ref[1], gap_ref[...], jnp.zeros((88, cols), jnp.int32)], axis=0
    ).astype(F32)
    pieces.append(mm_t(one(iota((cols, cols), 0) == iota((cols, cols), 1)), low(meta)))
    tile = low(jnp.concatenate(pieces, axis=1))
    tile_ref[...] = tile
    first_ref[...] = tile[:RIGHT]
    side_ref[...] = tile[:RIGHT]

    @pl.when(lax.axis_index("row") == 0)
    def _():
        side_ref[0:LEFT, :] = tile[cols - LEFT :]


def item_kernel(
    steps_ref, labels_ref, tw_ref, tb_ref, cw_ref, cb_ref, ct_ref, tl_ref, feat_ref, pre_ref, cond_ref, act_ref, table_ref
):
    items = tl_ref.shape[1]
    count = steps_ref.shape[0]
    tl_ref[...] = jnp.zeros_like(tl_ref)
    tl_ref[0:1, 0:count] = steps_ref[...].reshape(1, count)
    tl_ref[1:2, 0:count] = labels_ref[...].reshape(1, count)
    half = tw_ref.shape[0] // 2
    steps = tl_ref[0:1, :].astype(F32)
    freq = jnp.exp(iota((half, 1), 0).astype(F32) * (-math.log(10000.0) / half))
    angle = freq * steps
    feat_ref[0:half, :] = low(jnp.cos(angle))
    feat_ref[half:, :] = low(jnp.sin(angle))
    pre = t_mm(feat_ref[...], tw_ref[...]) + line(tb_ref)
    pre_ref[...] = pre
    hidden = low(pre * sigmoid(pre))
    classes = ct_ref.shape[0]
    pick = one(iota((classes, items), 0) == tl_ref[1:2, :])
    cond = mm(hidden, cw_ref[...]) + line(cb_ref) + t_mm(pick, ct_ref[...])
    cond_ref[...] = cond
    act_ref[...] = low(cond * sigmoid(cond))
    width = table_ref.shape[1]
    quarter = width // 4
    shape = (2 * POSITIONS, width)
    lane = iota(shape, 1)
    row = iota(shape, 0)
    second = lane >= 2 * quarter
    within = jnp.where(second, lane - 2 * quarter, lane)
    cosine = within >= quarter
    index = jnp.where(cosine, within - quarter, within)
    omega = jnp.exp(index.astype(F32) * (-math.log(10000.0) / quarter))
    angle = (row & (POSITIONS - 1)).astype(F32) * omega
    value = jnp.where(cosine, jnp.cos(angle), jnp.sin(angle))
    value = jnp.where(jnp.where(second, 1, 0) == jnp.where(row >= POSITIONS, 1, 0), value, 0.0)
    high = low(value)
    table_ref[0 : 2 * POSITIONS, :] = high
    table_ref[2 * POSITIONS :, :] = low(value - high.astype(F32))


def row_mask(q, i, shape):
    return ((q * 16 + (iota(shape, 1) & 15) - 1) >> 1) == i


def main_kernel(dims, *refs):
    n_rows, hp, cw, tokens, ni, half_rows = dims
    own_ref, side_ref = refs[0:2]
    tiles = refs[2 : 1 + n_rows]
    rights = refs[1 + n_rows : 2 * n_rows]
    (act_ref, table_ref, pb_ref, mb_ref, qb_ref, vb_ref, ob_ref, hb_ref, rb_ref, fb_ref, lb_ref,
     pw_ref, mw_ref, fw_ref, aw_ref, ow_ref, hw_ref, rw_ref, low_ref,
     q_ref, k_ref, v_ref, da_ref, rows_ref, aux_ref, res_ref, mid_ref, in_ref, x_ref, mem_ref, turn_ref, ms_ref, vel_ref,
     item_ref, keep_ref, send_ref,
     es, ct_s, at_s, mlp_s, ha_s, dh_s, dbm_s, dba_s, ri_s, gd_s, dacc, small, g_s) = refs[2 * n_rows :]
    width = res_ref.shape[1]
    pairs = width // 128
    r = lax.axis_index("row")
    core = lax.axis_index("col") & 1
    shift = int(math.log2(hp))

    es[...] = jnp.zeros_like(es)
    es[r, LEFT : LEFT + 64, :] = own_ref[...]
    for k in range(1, n_rows):
        other = lax.rem(r - k + n_rows, n_rows)
        es[other, LEFT : LEFT + 64, :] = tiles[k - 1][...]
        es[other, LEFT + 64 :, :] = rights[k - 1][...]

    @pl.when(r == 0)
    def _():
        es[r, 0:LEFT, :] = side_ref[0:LEFT, :]

    @pl.when(r > 0)
    def _():
        es[r, LEFT + 64 :, :] = side_ref[...]

    meta = es[r, :, 256:384].astype(F32)
    lane = iota(meta.shape, 1)
    weighted = meta * jnp.where(lane == 0, 256.0, jnp.where(lane == 8, 1.0, 0.0))
    down = iota(meta.shape, 0)
    start = LEFT + r * cw
    tag_prev = jnp.sum(jnp.where(down == start - 1, weighted, 0.0)).astype(jnp.int32)
    tag_last = jnp.sum(jnp.where(down == start + cw - 1, weighted, 0.0)).astype(jnp.int32)
    tag_first = jnp.sum(jnp.where(down == start, weighted, 0.0)).astype(jnp.int32)
    strip_prev = jnp.where(tag_prev == 0, ((tag_first - 1) >> 1) - 1, (tag_prev - 1) >> 1)
    strip_last = (tag_last - 1) >> 1
    base = 2 * (strip_prev + 1)

    pick = one(iota((16, act_ref.shape[0]), 1) == base + iota((16, act_ref.shape[0]), 0))
    own_act = low(mm(pick, act_ref[...]))
    ms_ref[48:, :] = jnp.zeros_like(ms_ref[48:, :])
    for b in range(8):
        cols = slice(b * width, (b + 1) * width)
        if b < 6:
            value = mm(own_act, mw_ref[:, cols]) + line(mb_ref, b * width, width)
        else:
            value = mm(own_act, fw_ref[:, (b - 6) * width : (b - 5) * width]) + line(fb_ref, (b - 6) * width, width)
        p0 = low(value)
        rest = value - p0.astype(F32)
        p1 = low(rest)
        ms_ref[0:16, cols] = p0
        ms_ref[16:32, cols] = p1
        ms_ref[32:48, cols] = low(rest - p1.astype(F32))

    def mod(mem, b, n=1):
        return mm(mem, ms_ref[:, b * width : (b + n) * width])

    fold = lane_fold(16)
    embed = low(t_mm(fold, pw_ref[...]))
    unread = low(t_mm(low_ref[...], fold))
    b_lanes = iota((BLOCK, 128), 1)
    is_b1 = b_lanes >= 64
    half_lanes = (one(b_lanes < 64), one(is_b1))

    lanes = iota((FIRST, 128), 1)
    second_side = lanes >= 64

    def first(tb, carry):
        t0 = pl.multiple_of(tb * FIRST, FIRST)
        rows = pl.ds(t0, FIRST)
        token = t0 + iota((FIRST, 1), 0)
        j = token >> shift
        i = token & (hp - 1)
        spot = iota((FIRST, LEFT + 64 + RIGHT), 1)
        rep0 = one(spot == start + j)
        rep1 = one(spot == start + j + 1)
        x = jnp.zeros((FIRST, 128), F32)
        c = jnp.zeros((FIRST, 128), F32)
        m = jnp.zeros((FIRST, 128), F32)
        for q in range(n_rows):
            here = mm(rep0, es[q])
            beside = mm(rep1, es[q, :, 0:256])
            mask = row_mask(q, i, (FIRST, 128))
            x = x + jnp.where(mask, jnp.where(second_side, here[:, 0:128], beside[:, 0:128]), 0.0)
            c = c + jnp.where(mask, jnp.where(second_side, here[:, 128:256], beside[:, 128:256]), 0.0)
            m = m + jnp.where((q * 8 + (lanes & 7)) == i, here[:, 256:384], 0.0)
        x = low(x)
        m = low(m)
        x_ref[rows, :] = x
        ml = iota((128, 128), 0)
        mc = iota((128, 128), 1)
        kind = ml >> 3
        gather = jnp.where(
            (mc == 0) & (kind == 0), 256.0,
            jnp.where(((mc == 0) & (kind == 1)) | ((mc >= 1) & (mc <= 3) & (kind == mc + 1)), 1.0, 0.0),
        ).astype(BF16)
        cols = mm(m, gather)
        rl = iota((8, 128), 1) >> 3
        rr = iota((8, 128), 0)
        row_pick = jnp.where((rr == 6) & (rl == 0), 256.0, jnp.where((rr == 6) & (rl == 1), 1.0, 0.0)).astype(BF16)
        across = mm_t(row_pick, m)
        rows_ref[:, rows] = across
        tag_row = across[6:7, :].astype(jnp.int32)
        strip_row = (tag_row - 1) >> 1
        turn_ref[:, rows] = one(
            (tag_row - 1 - base == iota((16, FIRST), 0)) & (strip_row > strip_prev) & (strip_row <= strip_last)
        )
        tag = cols[:, 0:1]
        gap = cols[:, 3:4]
        tag_i = tag.astype(jnp.int32)
        strip = (tag_i - 1) >> 1
        owned = (strip > strip_prev) & (strip <= strip_last)
        act = jnp.where(owned, gap, 0.0)
        aux_ref[rows, :] = jnp.where(lanes == 0, tag * gap, jnp.where(lanes == 1, act, 0.0))
        item = tag_i - 1 - base
        mem = one((item == (lanes & 15)) & (lanes < 48) & owned)
        mem_ref[rows, :] = mem
        ct_s[rows, :] = low(c * act)
        p0 = cols[:, 1:2].astype(jnp.int32)
        p1 = cols[:, 2:3].astype(jnp.int32) + POSITIONS
        spot = iota((FIRST, 2 * POSITIONS), 1)
        place = one((spot == p0) | (spot == p1))
        res = (
            mm(x, embed) + line(pb_ref)
            + (mm(place, table_ref[0 : 2 * POSITIONS, :]) + mm(place, table_ref[2 * POSITIONS :, :]))
        )
        res_ref[rows, :] = res
        normed, _ = layer_norm(res)
        ab = mod(mem, 0, 2)
        attn_in = low(normed * (1.0 + ab[:, width:]) + ab[:, :width])
        in_ref[rows, :] = attn_in
        for part, ref in enumerate((q_ref, k_ref, v_ref)):
            value = mm(attn_in, aw_ref[:, part * width : (part + 1) * width])
            if part != 1:
                value = value + line(vb_ref if part else qb_ref)
            value = low(value)
            if part == 0:
                value = value * BF16(1.0 / math.sqrt(width // HEADS))
            for p in range(pairs):
                ref[p, rows, :] = value[:, p * 128 : (p + 1) * 128]
        return carry

    lax.fori_loop(0, tokens // FIRST, first, 0)

    for qb in range(tokens // BLOCK):
        qs = slice(qb * BLOCK, (qb + 1) * BLOCK)
        ks = key_range(qb, hp, tokens)
        q_tag = rows_ref[6:7, qs]
        k_tag = aux_ref[ks, 0:1]
        allowed = k_tag == q_tag
        for p in range(pairs):
            query = q_ref[p, qs, :]
            key = k_ref[p, ks, :]
            value = v_ref[p, ks, :]
            halves = []
            for e in range(2):
                scores = jnp.where(allowed, mm_t(key, query * half_lanes[e]), -1e30)
                top = jnp.max(scores, axis=0, keepdims=True)
                expo = jnp.exp(scores - top)
                total = jnp.sum(expo, axis=0, keepdims=True)
                rows_ref[2 * p + e : 2 * p + e + 1, qs] = top + jnp.log(total)
                halves.append(t_mm(low(expo * (1.0 / total)), value))
            at_s[p, qs, :] = low(jnp.where(is_b1, halves[1], halves[0]))

    dacc[...] = jnp.zeros_like(dacc)
    small[...] = jnp.zeros_like(small)

    def second(tb, carry):
        t0 = pl.multiple_of(tb * SECOND, SECOND)
        rows = pl.ds(t0, SECOND)
        mem = mem_ref[rows, :]

        turned = turn_ref[:, rows]

        def item_sum(b, grad):
            dacc[:, b * width : (b + 1) * width] += mm(turned, low(grad))

        attended = jnp.concatenate([at_s[p, rows, :] for p in range(pairs)], axis=1)
        branch_a = mm(attended, ow_ref[...]) + line(ob_ref)
        gate_a = mod(mem, 2)
        mid = res_ref[rows, :] + gate_a * branch_a
        norm_mid, inv_mid = layer_norm(mid)
        scale_m = 1.0 + mod(mem, 4)
        mlp_in = low(norm_mid * scale_m + mod(mem, 3))
        mlp_s[rows, :] = mlp_in
        hidden = hw_ref.shape[1]
        branch_m = jnp.zeros((SECOND, width), F32)
        for n in range(hidden // width):
            part = slice(n * width, (n + 1) * width)
            pre = mm(mlp_in, hw_ref[:, part]) + line(hb_ref, n * width, width)
            square = pre * pre
            c0 = math.sqrt(2.0 / math.pi)
            t = jnp.tanh(pre * (c0 + (c0 * 0.044715) * square))
            up = 0.5 + 0.5 * t
            act = low(pre * up)
            gd_s[:, part] = up + (0.5 * pre) * (1.0 - t * t) * (c0 + (3.0 * c0 * 0.044715) * square)
            ha_s[rows, part] = act
            branch_m = branch_m + mm(act, rw_ref[part, :])
        branch_m = branch_m + line(rb_ref)
        gate_m = mod(mem, 5)
        norm_out, inv_out = layer_norm(mid + gate_m * branch_m)
        scale_f = 1.0 + mod(mem, 7)
        readout_in = low(norm_out * scale_f + mod(mem, 6))
        ri_s[rows, :] = readout_in
        active = aux_ref[rows, 1:2]
        bias_lanes = mm(low(line(lb_ref) + jnp.zeros((8, 16), F32)), fold)[0:1, :]
        vel_ref[rows, :] = low((mm(readout_in, unread) + bias_lanes) * active)
        d_read = mm_t(ct_s[rows, :], unread)
        item_sum(6, d_read)
        item_sum(7, d_read * norm_out)
        d_out = norm_back(norm_out, inv_out, d_read * scale_f)
        item_sum(5, d_out * branch_m)
        d_bm = low(d_out * gate_m)
        dbm_s[rows, :] = d_bm
        small[16:17, :] += jnp.sum(d_bm.astype(F32), axis=0, keepdims=True)
        d_mlp = jnp.zeros((SECOND, width), F32)
        for n in range(hidden // width):
            part = slice(n * width, (n + 1) * width)
            d_hid = low(mm_t(d_bm, rw_ref[part, :]) * gd_s[:, part])
            dh_s[rows, part] = d_hid
            small[17 + n : 18 + n, :] += jnp.sum(d_hid.astype(F32), axis=0, keepdims=True)
            d_mlp = d_mlp + mm_t(d_hid, hw_ref[:, part])
        item_sum(3, d_mlp)
        item_sum(4, d_mlp * norm_mid)
        d_mid = d_out + norm_back(norm_mid, inv_mid, d_mlp * scale_m)
        mid_ref[rows, :] = d_mid
        item_sum(2, d_mid * branch_a)
        d_ba = low(d_mid * gate_a)
        dba_s[rows, :] = d_ba
        small[21:22, :] += jnp.sum(d_ba.astype(F32), axis=0, keepdims=True)
        d_at = low(mm_t(d_ba, ow_ref[...]))
        for p in range(pairs):
            da_ref[p, rows, :] = d_at[:, p * 128 : (p + 1) * 128]
        return carry

    lax.fori_loop(0, tokens // SECOND, second, 0)
    rows = [dacc[0:ni, b * width : (b + 1) * width] for b in range(2, 8)]
    spot = ((core * 2 * n_rows + plane_spot()) * (lax.axis_size("col") // 4) + line_spot()) * ni
    index = iota((4, width), 0) * width + iota((4, width), 1) - spot
    number = jnp.where((index >= 0) & (index < ni), base + index, 0)
    rows += [(number >> 8).astype(F32), (number & 255).astype(F32)]
    item_ref[...] = low(jnp.concatenate(rows, axis=0))

    g_s[...] = jnp.zeros_like(g_s)
    put = functools.partial(put_rows, g_s, half_rows)
    n_hidden = hw_ref.shape[1] // width
    for n in range(n_hidden):
        part = slice(n * width, (n + 1) * width)
        put(n * width, low(t_mm(ha_s[:, part], dbm_s[...])))
    grad = low(t_mm(mlp_s[...], dh_s[...]))
    for n in range(n_hidden):
        put((n_hidden + n) * width, grad[:, n * width : (n + 1) * width])
    attended = jnp.concatenate([at_s[p] for p in range(pairs)], axis=1)
    put(2 * n_hidden * width, low(t_mm(attended, dba_s[...])))
    ones = jnp.ones((8, tokens), BF16)
    small[0:16, :] = mm(fold, low(t_mm(ct_s[...], ri_s[...])))
    sums = mm(ones, ct_s[...])
    small[22:23, 0:128] = mm_t(jnp.broadcast_to(low(sums[0:1, :]), (8, 128)), lane_fold(128))[0:1, :]
    put((2 * n_hidden + 1) * width, low(small[...]))
    keep_ref[...] = g_s[core]
    send_ref[...] = g_s[1 - core]


def put_rows(g_s, half_rows, row, value):
    count = value.shape[0]
    done = 0
    while done < count:
        side, at = divmod(row + done, half_rows)
        take = min(count - done, half_rows - at)
        g_s[side, at : at + take, :] = value[done : done + take, :]
        done += take


def key_range(qb, hp, tokens):
    first_col = (qb * BLOCK) // hp
    last_col = ((qb + 1) * BLOCK - 1) // hp
    return slice(max(0, first_col - HALO) * hp, min(tokens, (last_col + 1 + HALO) * hp))


def attend_back_kernel(hp, first, q_ref, k_ref, v_ref, da_ref, rows_ref, aux_ref, dq_ref, dk_ref, dv_ref, dk_s, dv_s):
    tokens = q_ref.shape[1]
    b_lanes = iota((BLOCK, 128), 1)
    is_b1 = b_lanes >= 64
    half_lanes = (one(b_lanes < 64), one(is_b1))
    scale = 1.0 / math.sqrt(q_ref.shape[0] * 128 // HEADS)
    dk_s[...] = jnp.zeros_like(dk_s)
    dv_s[...] = jnp.zeros_like(dv_s)
    for qb in range(tokens // BLOCK):
        qs = slice(qb * BLOCK, (qb + 1) * BLOCK)
        ks = key_range(qb, hp, tokens)
        allowed = aux_ref[ks, 0:1] == rows_ref[6:7, qs]
        for n in range(dq_ref.shape[0]):
            p = first + n
            query = q_ref[p, qs, :]
            key = k_ref[p, ks, :]
            value = v_ref[p, ks, :]
            d_at = da_ref[p, qs, :]
            d_key = 0.0
            d_value = 0.0
            halves = []
            for e in range(2):
                q_half = query * half_lanes[e]
                d_half = d_at * half_lanes[e]
                scores = jnp.where(allowed, mm_t(key, q_half), -1e30)
                probs = jnp.exp(scores - rows_ref[2 * p + e : 2 * p + e + 1, qs])
                d_probs = mm_t(value, d_half)
                inner = jnp.sum(probs * d_probs, axis=0, keepdims=True)
                d_scores = low(probs * (d_probs - inner))
                d_value = d_value + mm(low(probs), d_half)
                d_key = d_key + mm(d_scores, q_half)
                halves.append(t_mm(d_scores, key))
            dk_s[n, ks, :] += d_key
            dv_s[n, ks, :] += d_value
            dq_ref[n, qs, :] = low(jnp.where(is_b1, halves[1], halves[0]) * scale)
    dk_ref[...] = low(dk_s[...])
    dv_ref[...] = low(dv_s[...])


def joined(refs, rows):
    return jnp.concatenate(
        [ref[n, rows, :] for kind in range(3) for ref in refs[kind::3] for n in range(ref.shape[0])], axis=1
    )


def weigh_attention(half_rows, in_ref, parts, patch, keep_ref, send_ref, small, g_s):
    tokens, width = in_ref.shape
    core = lax.axis_index("col") & 1
    put = functools.partial(put_rows, g_s, half_rows)
    ones = jnp.ones((8, tokens), BF16)
    g_s[...] = jnp.zeros_like(g_s)
    small[...] = jnp.zeros_like(small)
    small[0 : patch.shape[0], :] = patch
    whole = joined(parts, slice(None))
    for n in range(3):
        grad = whole[:, n * width : (n + 1) * width]
        put(n * width, low(t_mm(in_ref[...], grad)))
        if n != 1:
            small[17 + n // 2 : 18 + n // 2, :] = mm(ones, grad)[0:1, :]
    put(3 * width, low(small[...]))
    keep_ref[...] = g_s[core]
    send_ref[...] = g_s[1 - core]


def back_kernel(dims, *refs):
    n_rows, hp, cw, tokens, ni, half_rows = dims
    heads, done = refs[:6], refs[6:9]
    (in_ref, res_ref, mid_ref, x_ref, mem_ref, turn_ref, ms_ref, vel_ref, more_ref, aw_ref, pw_ref, keep_ref, send_ref,
     item_ref) = refs[9:23]
    frame_refs = refs[23 : 23 + n_rows]
    *rest, dk_s, dv_s, small, g_s, di_s, dacc, frame = refs[23 + n_rows :]
    parts = [*done, *rest]
    attend_back_kernel(hp, done[0].shape[0], *heads, *rest, dk_s, dv_s)
    width = res_ref.shape[1]
    r = lax.axis_index("row")
    shift = int(math.log2(hp))

    embed = low(t_mm(lane_fold(16), pw_ref[...]))
    dacc[...] = jnp.zeros_like(dacc)
    frame[...] = jnp.zeros_like(frame)

    def third(tb, carry):
        t0 = pl.multiple_of(tb * THIRD, THIRD)
        rows = pl.ds(t0, THIRD)
        mem = mem_ref[rows, :]
        d_attn = mm_t(joined(parts, rows), aw_ref[...])
        normed, inverse = layer_norm(res_ref[rows, :])
        scale_a = 1.0 + mm(mem, ms_ref[:, width : 2 * width])
        turned = turn_ref[:, rows]
        dacc[:, 0:width] += mm(turned, low(d_attn))
        dacc[:, width : 2 * width] += mm(turned, low(d_attn * normed))
        d_in = low(mid_ref[rows, :] + norm_back(normed, inverse, d_attn * scale_a))
        di_s[rows, :] = d_in
        grad = low(mm_t(d_in, embed))
        both = jnp.concatenate([vel_ref[rows, :], grad], axis=1)
        token = t0 + iota((THIRD, 1), 0)
        j = token >> shift
        i = token & (hp - 1)
        spot = iota((THIRD, 64 + RIGHT), 1)
        rep = jnp.concatenate([one(spot == r * cw + j), one(spot == r * cw + j + 1)], axis=0)
        side = (iota((THIRD, 256), 1) >> 6) & 1
        for q in range(n_rows):
            mask = row_mask(q, i, (THIRD, 256))
            split = jnp.concatenate([both * one(mask & (side == 1)), both * one(mask & (side == 0))], axis=0)
            frame[q] += t_mm(rep, split)
        return carry

    lax.fori_loop(0, tokens // THIRD, third, 0)

    ones = jnp.ones((8, tokens), BF16)
    rows = [dacc[0:ni, 0:width], dacc[0:ni, width : 2 * width]]
    rows += [more_ref[...].astype(F32)]
    item_ref[...] = low(jnp.concatenate(rows, axis=0))
    patch = jnp.concatenate([mm(lane_fold(16), low(t_mm(x_ref[...], di_s[...]))), mm(ones, di_s[...])[0:1, :]], axis=0)
    weigh_attention(half_rows, in_ref, parts, patch, keep_ref, send_ref, small, g_s)
    for k in range(n_rows):
        q = lax.rem(r + k, n_rows)
        frame_refs[k][...] = low(frame[q])


def frame_kernel(*refs):
    *ins, mine_ref, over_ref = refs
    total = ins[0][...].astype(F32)
    for ref in ins[1:]:
        total = total + ref[...].astype(F32)
    mine_ref[...] = low(total[0:64])
    over_ref[...] = low(total[64:])


def canvas_kernel(mine_ref, over_ref, vel_ref, grad_ref):
    extra = jnp.concatenate([over_ref[...].astype(F32), jnp.zeros((64 - RIGHT, 256), F32)], axis=0)
    total = low(mine_ref[...].astype(F32) + extra)
    for n, ref in enumerate((vel_ref, grad_ref)):
        value = 0.0
        for side in (0, 1):
            pick = one(iota((64, 128), 1) == 2 * iota((64, 128), 0) + side)
            value = value + t_mm(total[:, n * 128 + side * 64 : n * 128 + (side + 1) * 64], pick)
        ref[...] = value.reshape(ref.shape).astype(ref.dtype)


def add_kernel(count, me, *refs):
    outs = refs[len(refs) - count :]
    ins = refs[: len(refs) - count]
    spot = me()
    for m, out in enumerate(outs):
        at = jnp.bitwise_xor(spot, m) if count > 1 else 0
        total = ins[0][at].astype(F32)
        for ref in ins[1:]:
            total = total + ref[at].astype(F32)
        out[...] = low(total)


def plane_spot():
    return lax.axis_index("row") + lax.axis_size("row") * ((lax.axis_index("col") >> 1) & 1)


def line_spot():
    return lax.axis_index("col") >> 2


def send(value, n_rows, n_cols, flip_row=0, flip_col=0):
    route = [
        (i * n_cols + j, (i ^ flip_row) * n_cols + (j ^ flip_col)) for i in range(n_rows) for j in range(n_cols)
    ]
    return lax.ppermute(value, ("row", "col"), route)


def add_up(arrays, count, me, after=()):
    n, w = arrays[0].shape
    ins = [a.reshape(count, n // count, w) for a in arrays]
    return call(
        functools.partial(add_kernel, count, me), [((n // count, w), BF16)] * count, ins, after=after,
        near_in=range(len(ins)), near_out=range(count),
    )


def add_with_kernel(count, me, *refs):
    outs = refs[len(refs) - count :]
    *ins, more = refs[: len(refs) - count]
    spot = me()
    for m, out in enumerate(outs):
        at = jnp.bitwise_xor(spot, m)
        total = ins[0][at].astype(F32)
        for ref in ins[1:]:
            total = total + ref[at].astype(F32)
        out[0 : total.shape[0], :] = low(total)
        if m:
            out[total.shape[0] :, :] = more[...]


def add_tops_kernel(*refs):
    *ins, out = refs
    total = ins[0][...].astype(F32)
    for ref in ins[1:]:
        total = total + ref[0 : out.shape[0], :].astype(F32)
    out[...] = low(total)


def list_ends_kernel(*refs):
    own_ref, *ins, out = refs
    out[0] = own_ref[...]
    for m, ref in enumerate(ins):
        out[m + 1] = ref[ref.shape[0] - own_ref.shape[0] :, :]


def add_below_kernel(*refs):
    *ins, first, out = refs
    total = ins[0][...].astype(F32)
    for ref in ins[1:]:
        total = total + ref[...].astype(F32)
    out[0 : first.shape[0], :] = first[...]
    out[first.shape[0] :, :] = low(total)


def line_kernel(share, *refs):
    *ins, out, rows = refs
    spot = line_spot()
    for m, ref in enumerate(ins):
        out[m * share : (m + 1) * share, :] = ref[0:share, :]
        rows[jnp.bitwise_xor(spot, m)] = ref[share:, :].astype(F32)
    out[len(ins) * share :, :] = low(jnp.sum(rows[...], axis=0))


def copy_kernel(in_ref, out_ref):
    out_ref[...] = in_ref[...]


def to_plane(parts, n_rows, n_cols):
    return [
        send(parts[m], n_rows, n_cols, flip_row=m % n_rows, flip_col=2 * (m // n_rows)) for m in range(1, 2 * n_rows)
    ]


def to_line(parts, n_rows, n_cols):
    return [send(parts[m], n_rows, n_cols, flip_col=4 * m) for m in range(1, n_cols // 4)]


def stack_kernel(*refs):
    *ins, out = refs
    for n, ref in enumerate(ins):
        out[n] = ref[...]


def stack(arrays, after=()):
    return call(
        stack_kernel, [((len(arrays), *arrays[0].shape), BF16)], arrays, after=after, near_in=range(len(arrays)),
        near_out=(0,),
    )[0]


def for_planes(n_rows, body):
    core = lax.axis_index("col") & 1
    plane = plane_spot()
    for c in range(2):

        def step(m, carry, c=c):
            body(c, m, jnp.bitwise_xor(core, c) * 2 * n_rows + jnp.bitwise_xor(plane, m))
            return carry

        lax.fori_loop(0, 2 * n_rows, step, 0)


def for_parts(n_rows, n_cols, body):
    line = line_spot()

    def inner(c, m, at):
        for n in range(n_cols // 4):
            body(c, m, n, at * (n_cols // 4) + jnp.bitwise_xor(line, n))

    for_planes(n_rows, inner)


def weights_kernel(mesh_shape, *refs):
    n_rows, n_cols = mesh_shape
    blocks = refs[: 4 * n_rows]
    (ret_ref, hid_ref, out_ref, read_ref, rb_ref, hb_ref, ob_ref, lb_ref, att_ref, patch_ref, pb_ref, qb_ref, vb_ref,
     first, second) = refs[4 * n_rows :]
    share = first.shape[1]
    core = lax.axis_index("col") & 1
    plane, line = plane_spot(), line_spot()
    lines = n_cols // 4
    for n, ref in enumerate(blocks):
        c, m = divmod(n, 2 * n_rows)
        at = jnp.bitwise_xor(core, c) * 2 * n_rows + jnp.bitwise_xor(plane, m)
        for k in range(lines):
            first[at * lines + jnp.bitwise_xor(line, k)] = ref[k * share : (k + 1) * share, :].astype(F32)
        second[at] = ref[lines * share :, :].astype(F32)
    flat = first[...].reshape(first.shape[0] * share, first.shape[2])
    width = flat.shape[1]
    hidden = ret_ref.shape[0]
    ret_ref[...] = flat[0:hidden]
    for n in range(hidden // width):
        hid_ref[:, n * width : (n + 1) * width] = flat[hidden + n * width : hidden + (n + 1) * width]
    out_ref[...] = flat[2 * hidden : 2 * hidden + width]
    at = 2 * hidden + width
    small = flat[at : at + 24]
    read_ref[...] = small[0:16]
    rb_ref[...] = small[16]
    for n in range(hidden // width):
        hb_ref[n * width : (n + 1) * width] = small[17 + n]
    ob_ref[...] = small[21]
    lb_ref[...] = small[22, 0:16]
    flat = second[...].reshape(second.shape[0] * second.shape[1], width)
    for n in range(3):
        att_ref[:, n * width : (n + 1) * width] = flat[n * width : (n + 1) * width]
    small = flat[3 * width : 3 * width + 24]
    patch_ref[...] = small[0:16]
    pb_ref[...] = small[16]
    qb_ref[...] = small[17]
    vb_ref[...] = small[18]


def condition_kernel(
    mesh_shape, ni, own_ref, other_ref, tl_ref, feat_ref, pre_ref, cond_ref, act_ref, mw_ref, fw_ref, cw_ref,
    mod_ref, fin_ref, table_ref, clock_ref, time_ref, mb_ref, fb_ref, cb_ref, tb_ref,
    dev_s, ids_s,
):
    n_rows, n_cols = mesh_shape
    width = cw_ref.shape[0]
    items = tl_ref.shape[1]
    count = n_rows * n_cols
    ids_s[...] = jnp.zeros_like(ids_s)

    def place(c, m, n, at):
        part = (own_ref, other_ref)[c][m, n].astype(F32)
        for b in range(8):
            dev_s[b, at] = part[b * ni : (b + 1) * ni]
        ids_s[...] += part[8 * ni :]

    for_parts(n_rows, n_cols, place)
    ids = ids_s[...]
    numbers = ids[0:4] * 256.0 + ids[4:8]
    number = jnp.concatenate([numbers[k : k + 1, :] for k in range(-(-count * ni // width))], axis=1)[:, : count * ni]
    pick = one(iota((items, count * ni), 0).astype(F32) == number)
    ones = jnp.ones((8, items), BF16)
    act = act_ref[...]
    d_cond = jnp.zeros((items, width), F32)
    for b in range(8):
        grad = low(mm(pick, low(dev_s[b].reshape(count * ni, width))))
        total = mm(ones, grad)[0]
        if b < 6:
            cols = slice(b * width, (b + 1) * width)
            mb_ref[cols] = total
            mod_ref[:, cols] = t_mm(act, grad)
            d_cond = d_cond + mm_t(grad, mw_ref[:, cols])
        else:
            cols = slice((b - 6) * width, (b - 5) * width)
            fb_ref[cols] = total
            fin_ref[:, cols] = t_mm(act, grad)
            d_cond = d_cond + mm_t(grad, fw_ref[:, cols])
    cond = cond_ref[...]
    sigma = sigmoid(cond)
    d_cond = low(d_cond * (sigma * (1.0 + cond * (1.0 - sigma))))
    pre = pre_ref[...]
    sigma = sigmoid(pre)
    hidden = low(pre * sigma)
    classes = table_ref.shape[0]
    table_ref[...] = mm(one(iota((classes, items), 0) == tl_ref[1:2, :]), d_cond)
    clock_ref[...] = t_mm(hidden, d_cond)
    cb_ref[...] = mm(ones, d_cond)[0]
    d_time = low(mm_t(d_cond, cw_ref[...]) * (sigma * (1.0 + pre * (1.0 - sigma))))
    time_ref[...] = mm(feat_ref[...], d_time)
    tb_ref[...] = mm(ones, d_time)[0]


def local(
    latent, cotangent, item_ids, positions, gap_mask, timesteps, labels, patch_weight, patch_bias, time_weight,
    time_bias, clock_weight, clock_bias, class_table, modulation_weight, modulation_bias, attention_weight, query_bias,
    value_bias, output_weight, output_bias, hidden_weight, hidden_bias, return_weight, return_bias, final_modulation,
    final_offsets, readout_weight, readout_bias,
):
    n_rows, n_cols = lax.axis_size("row"), lax.axis_size("col")
    row_count, col_count = item_ids.shape
    width = patch_weight.shape[1]
    hidden = hidden_weight.shape[1]
    hp = n_rows * row_count
    cw = col_count // n_rows
    tokens = (cw + HALO) * hp
    ni = 2 * (-(-cw // LEAST))
    items = -(-(timesteps.shape[0] + 16) // 32) * 32
    unit = 8 * n_rows * n_cols
    rows_1 = -(-(2 * hidden + width + 128) // unit) * unit
    rows_2 = -(-(3 * width + 128) // unit) * unit
    pairs = width // 128
    near = int(tokens <= 1024)

    tile, first_cols, side_cols = call(
        tile_kernel,
        [((col_count, 384), BF16), ((RIGHT, 384), BF16), ((RIGHT, 384), BF16)],
        [latent, cotangent, item_ids, positions, gap_mask],
        far_in=range(5), near_out=range(3),
    )

    def shift(value, step_row, step_col, wanted):
        route = [
            (i * n_cols + j, (i + step_row) % n_rows * n_cols + j + step_col)
            for i in range(n_rows)
            for j in range(n_cols)
            if 0 <= j + step_col < n_cols and wanted((i + step_row) % n_rows)
        ]
        return lax.ppermute(value, ("row", "col"), route)

    def needs_right(i):
        return (i + 1) * cw + HALO + 1 > col_count

    tiles = [shift(tile, k, 0, lambda i: True) for k in range(1, n_rows)]
    rights = [shift(first_cols, k, -1, needs_right) for k in range(1, n_rows)]
    route = [(j, j + 1) for j in range(n_cols - 1)]
    route += [
        (i * n_cols + j, i * n_cols + j - 1) for i in range(1, n_rows) if needs_right(i) for j in range(1, n_cols)
    ]
    side = lax.ppermute(side_cols, ("row", "col"), route)

    tl, feat, time_pre, condition, cond_act, table = call(
        item_kernel,
        [((8, items), jnp.int32), ((time_weight.shape[0], items), BF16), ((items, width), F32), ((items, width), F32),
         ((items, width), BF16), ((4 * POSITIONS, width), BF16)],
        [timesteps, labels, time_weight, time_bias, clock_weight, clock_bias, class_table],
        us=5,
    )

    dims = (n_rows, hp, cw, tokens, ni, rows_1 // 2)
    heads = ((pairs, tokens, 128), BF16)
    ins = [tile, side, *tiles, *rights, cond_act, table, patch_bias, modulation_bias, query_bias, value_bias, output_bias,
           hidden_bias, return_bias, final_offsets, readout_bias, patch_weight, modulation_weight, final_modulation,
           attention_weight, output_weight, hidden_weight, return_weight, readout_weight.T]
    q, k, v, d_at, rows, aux, res, mid, attn_in, patches, member, turned, spread, spoken, item_main, keep, out = call(
        functools.partial(main_kernel, dims),
        [heads, heads, heads, heads, ((8, tokens), F32), ((tokens, 128), F32), ((tokens, width), F32),
         ((tokens, width), F32), ((tokens, width), BF16), ((tokens, 128), BF16), ((tokens, 128), BF16),
         ((16, tokens), BF16), ((128, 8 * width), BF16), ((tokens, 128), BF16), ((6 * ni + 8, width), BF16),
         ((rows_1 // 2, width), BF16), ((rows_1 // 2, width), BF16)],
        ins,
        [((n_rows, LEFT + 64 + RIGHT, 384), BF16), ((tokens, 128), BF16), ((pairs, tokens, 128), BF16),
         ((tokens, width), BF16), ((tokens, hidden), BF16), ((tokens, hidden), BF16), ((tokens, width), BF16),
         ((tokens, width), BF16), ((tokens, width), BF16), ((SECOND, hidden), F32), ((16, 8 * width), F32),
         ((128, width), F32), ((2, rows_1 // 2, width), BF16)],
        us=30, room=36 if near else 60, near_out=range(17 * near), near_in=range(len(ins) * near),
    )
    shape = (n_rows, n_cols)
    lines = n_cols // 4
    got = send(out, *shape, flip_col=1)

    part = ((1, tokens, 128), BF16)
    total = ((1, tokens, 128), F32)
    d_first = call(
        functools.partial(attend_back_kernel, hp, 0), [part] * 3, [q, k, v, d_at, rows, aux], [total] * 2,
        us=4, room=24 if near else 60, near_in=range(6 * near), near_out=range(3 * near),
    )
    parts = add_up([keep, got], 2 * n_rows, plane_spot, after=[d_first[0]])
    got = to_plane(parts, *shape)
    dims = (n_rows, hp, cw, tokens, ni, rows_2 // 2)
    part = ((pairs - 1, tokens, 128), BF16)
    total = ((pairs - 1, tokens, 128), F32)
    result = call(
        functools.partial(back_kernel, dims),
        [((rows_2 // 2, width), BF16)] * 2 + [((8 * ni + 8, width), BF16)]
        + [((64 + RIGHT, 256), BF16)] * n_rows,
        [q, k, v, d_at, rows, aux, *d_first, attn_in, res, mid, patches, member, turned, spread, spoken,
         item_main, attention_weight, patch_weight],
        [part] * 3 + [total] * 2 + [((128, width), F32), ((2, rows_2 // 2, width), BF16)]
        + [((tokens, width), BF16), ((16, 2 * width), F32), ((n_rows, 64 + RIGHT, 256), F32)],
        us=14, after=[parts[0]], room=32 if near else 60, near_in=range(18 * near),
        near_out=range((3 + n_rows) * near),
    )
    keep_2, out_2, items_own = result[:3]
    got_2 = send(out_2, *shape, flip_col=1)
    frames = result[3:]
    share_1 = rows_1 // (n_rows * n_cols)
    share_2 = rows_2 // (4 * n_rows)

    count = items_own.shape[0]
    ins = [a.reshape(lines, share_1, width) for a in (parts[0], *got)]
    parts = call(
        functools.partial(add_with_kernel, lines, line_spot),
        [((share_1 + (count if m else 0), width), BF16) for m in range(lines)], [*ins, items_own],
        near_in=range(len(ins) + 1), near_out=range(lines),
    )
    got = to_line(parts, *shape)
    parts_2 = add_up([keep_2, got_2], 2 * n_rows, plane_spot, after=[parts[0]])
    got_2 = to_plane(parts_2, *shape)
    (part,) = call(
        add_tops_kernel, [((share_1, width), BF16)], [parts[0], *got], near_in=range(lines), near_out=(0,),
        after=[parts_2[0]],
    )
    ins = [parts_2[0], *got_2, part]
    (both,) = call(
        add_below_kernel, [((share_1 + share_2, width), BF16)], ins, near_in=range(len(ins)), near_out=(0,),
    )
    got_both = to_line([both] * lines, *shape)
    (block_items,) = call(
        list_ends_kernel, [((lines, count, width), BF16)], [items_own, *got], near_in=range(lines), near_out=(0,),
        after=[both],
    )
    plane_items = to_plane([block_items] * (2 * n_rows), *shape)

    frames = [
        call(copy_kernel, [(a.shape, BF16)], [a], near_in=(0,), near_out=(0,), after=[both])[0] if k else a
        for k, a in enumerate(frames)
    ]
    frames = [frames[0]] + [shift(frames[k], k, 0, lambda i: True) for k in range(1, n_rows)]
    mine, over = call(
        frame_kernel, [((64, 256), BF16), ((RIGHT, 256), BF16)], frames, near_in=range(n_rows), near_out=(0, 1),
    )
    velocity, latent_grad = call(
        canvas_kernel, [(latent.shape, BF16), (latent.shape, F32)], [mine, shift(over, 0, 1, lambda i: True)],
        near_in=(0, 1),
    )
    (block,) = call(
        functools.partial(line_kernel, share_1), [((lines * share_1 + share_2, width), BF16)], [both, *got_both],
        [((lines, share_2, width), F32)], near_in=range(lines), near_out=(0,), after=[velocity],
    )
    plane_block = to_plane([block] * (2 * n_rows), *shape)
    blocks_items = stack([block_items] + plane_items, after=[block])
    blocks_items = blocks_items, send(blocks_items, *shape, flip_col=1)
    devices = n_rows * n_cols
    vector = ((width,), F32)
    modulation_grad, final_grad, table_grad, clock_grad, time_grad, modulation_b, final_b, clock_b, time_b = call(
        functools.partial(condition_kernel, shape, ni),
        [((width, 6 * width), F32), ((width, 2 * width), F32), (class_table.shape, F32), ((width, width), F32),
         (time_weight.shape, F32), ((6 * width,), F32), ((2 * width,), F32), vector, vector],
        [*blocks_items, tl, feat, time_pre, condition, cond_act, modulation_weight, final_modulation, clock_weight],
        [((8, devices, ni, width), F32), ((8, width), F32)],
        us=8, room=40, near_in=range(2),
    )
    blocks = [block] + [
        call(copy_kernel, [(a.shape, BF16)], [a], near_in=(0,), near_out=(0,), after=[time_b])[0] for a in plane_block
    ]
    blocks += [send(b, *shape, flip_col=1) for b in blocks]
    (return_grad, hidden_grad, output_grad, readout_grad, return_b, hidden_b, output_b, readout_b, attention_grad, patch_grad,
     patch_b, query_b, value_b) = call(
        functools.partial(weights_kernel, shape),
        [((hidden, width), F32), ((width, hidden), F32), ((width, width), F32), ((16, width), F32), vector,
         ((hidden,), F32), vector, ((16,), F32), ((width, 3 * width), F32), ((16, width), F32), vector, vector, vector],
        blocks,
        [((devices, share_1, width), F32), ((4 * n_rows, share_2, width), F32)],
        us=4, room=36, near_in=range(len(blocks)), after=[time_b],
    )
    return (
        velocity, latent_grad, patch_grad, patch_b, time_grad, time_b, clock_grad, clock_b, table_grad, modulation_grad,
        modulation_b, attention_grad, query_b, value_b, output_grad, output_b, hidden_grad, hidden_b, return_grad,
        return_b, final_grad, final_b, readout_grad.T, readout_b,
    )


def solution(mesh):
    canvas, grid = P(None, "row", "col"), P("row", "col")
    return jax.shard_map(
        local,
        mesh=mesh,
        in_specs=(canvas, canvas, grid, canvas, grid) + (P(),) * 24,
        out_specs=(canvas, canvas) + (P(),) * 22,
        check_vma=False,
    )
```

```python
import functools
import math

import jax
import jax.numpy as jnp
from jax import lax
from jax.experimental import pallas as pl
from jax.experimental.pallas import tpu as pltpu
from jax.sharding import PartitionSpec as P

HEADS = 6
HALO = 16
LEAST = 8
BLOCK = 256
FIRST, SECOND, THIRD = 384, 256, 384
LEFT = 16
RIGHT = 32
POSITIONS = 128
F32 = jnp.float32
BF16 = jnp.bfloat16
FLOPS_US = 1_150_000_000
BYTES_US = 3_700_000


def iota(shape, dim):
    return lax.broadcasted_iota(jnp.int32, shape, dim)


def mm(a, b):
    return jnp.dot(a, b, preferred_element_type=F32)


def mm_t(a, b):
    return lax.dot_general(a, b, (((1,), (1,)), ((), ())), preferred_element_type=F32)


def t_mm(a, b):
    return lax.dot_general(a, b, (((0,), (0,)), ((), ())), preferred_element_type=F32)


def low(v):
    return v.astype(BF16)


def one(cond):
    return jnp.where(cond, 1.0, 0.0).astype(BF16)


def sigmoid(v):
    return 1.0 / (1.0 + jnp.exp(-v))


def layer_norm(v):
    center = v - jnp.mean(v, axis=-1, keepdims=True)
    inverse = lax.rsqrt(jnp.mean(center * center, axis=-1, keepdims=True) + 1e-06)
    return center * inverse, inverse


def norm_back(normed, inverse, grad):
    mean_grad = jnp.mean(grad, axis=-1, keepdims=True)
    mean_cross = jnp.mean(grad * normed, axis=-1, keepdims=True)
    return inverse * (grad - mean_grad - normed * mean_cross)


def call(
    body, outs, ins, scratch=(), near_in=(), near_out=(), far_in=(), hand_out=(), alias=None, after=(), us=2, room=16
):
    spec = pl.BlockSpec(memory_space=pltpu.VMEM)
    away = pl.BlockSpec(memory_space=pl.ANY)
    used = len(ins)

    def run(*refs):
        body(*refs[:used], *refs[used + len(after) :])

    ins = [
        pltpu.with_memory_space_constraint(a, pltpu.VMEM if n in near_in else pltpu.HBM)
        if n in near_in or n in far_in else a
        for n, a in enumerate(ins)
    ]
    return pl.pallas_call(
        run,
        out_shape=[
            (pltpu.VMEM if n in near_out else jax.ShapeDtypeStruct)(shape, dtype)
            for n, (shape, dtype) in enumerate(outs)
        ],
        in_specs=[away if n == alias else spec for n in range(used)] + [away] * len(after),
        out_specs=[away if n in hand_out else spec for n in range(len(outs))],
        scratch_shapes=[pltpu.VMEM(shape, dtype) for shape, dtype in scratch]
        + [pltpu.SemaphoreType.DMA(())] * len(hand_out),
        input_output_aliases={} if alias is None else {alias: 0},
        compiler_params=pltpu.CompilerParams(vmem_limit_bytes=room * 1024 * 1024),
        cost_estimate=pl.CostEstimate(flops=us * FLOPS_US, bytes_accessed=us * BYTES_US, transcendentals=0),
    )(*ins, *after)


def line(ref, start=0, count=None):
    count = ref.shape[0] if count is None else count
    return ref[start : start + count].astype(F32).reshape(1, count)


def lane_fold(rows):
    lane = iota((rows, 128), 1)
    feature = 8 * (1 - (lane & 1)) + 4 * (1 - (lane >> 6)) + ((lane >> 4) & 3)
    return one(iota((rows, 128), 0) == feature)


def tile_kernel(lat_ref, cot_ref, ids_ref, pos_ref, gap_ref, tile_ref, first_ref, side_ref):
    cols = ids_ref.shape[1]
    pieces = []
    for ref in (lat_ref, cot_ref):
        flat = ref[...].reshape(64, 2 * cols)
        for side in (0, 1):
            pick = one(iota((cols, 2 * cols), 1) == 2 * iota((cols, 2 * cols), 0) + side)
            pieces.append(mm_t(pick, flat))
    tag = ids_ref[...] + 1
    meta = jnp.concatenate(
        [tag >> 8, tag & 255, pos_ref[0], pos_ref[1], gap_ref[...], jnp.zeros((88, cols), jnp.int32)], axis=0
    ).astype(F32)
    pieces.append(mm_t(one(iota((cols, cols), 0) == iota((cols, cols), 1)), low(meta)))
    tile = low(jnp.concatenate(pieces, axis=1))
    tile_ref[...] = tile
    first_ref[...] = tile[:RIGHT]
    side_ref[...] = tile[:RIGHT]

    @pl.when(lax.axis_index("row") == 0)
    def _():
        side_ref[0:LEFT, :] = tile[cols - LEFT :]


def item_kernel(
    steps_ref, labels_ref, tw_ref, tb_ref, cw_ref, cb_ref, ct_ref, tl_ref, feat_ref, pre_ref, cond_ref, act_ref, table_ref
):
    items = tl_ref.shape[1]
    count = steps_ref.shape[0]
    tl_ref[...] = jnp.zeros_like(tl_ref)
    tl_ref[0:1, 0:count] = steps_ref[...].reshape(1, count)
    tl_ref[1:2, 0:count] = labels_ref[...].reshape(1, count)
    half = tw_ref.shape[0] // 2
    steps = tl_ref[0:1, :].astype(F32)
    freq = jnp.exp(iota((half, 1), 0).astype(F32) * (-math.log(10000.0) / half))
    angle = freq * steps
    feat_ref[0:half, :] = low(jnp.cos(angle))
    feat_ref[half:, :] = low(jnp.sin(angle))
    pre = t_mm(feat_ref[...], tw_ref[...]) + line(tb_ref)
    pre_ref[...] = pre
    hidden = low(pre * sigmoid(pre))
    classes = ct_ref.shape[0]
    pick = one(iota((classes, items), 0) == tl_ref[1:2, :])
    cond = mm(hidden, cw_ref[...]) + line(cb_ref) + t_mm(pick, ct_ref[...])
    cond_ref[...] = cond
    act_ref[...] = low(cond * sigmoid(cond))
    width = table_ref.shape[1]
    quarter = width // 4
    shape = (2 * POSITIONS, width)
    lane = iota(shape, 1)
    row = iota(shape, 0)
    second = lane >= 2 * quarter
    within = jnp.where(second, lane - 2 * quarter, lane)
    cosine = within >= quarter
    index = jnp.where(cosine, within - quarter, within)
    omega = jnp.exp(index.astype(F32) * (-math.log(10000.0) / quarter))
    angle = (row & (POSITIONS - 1)).astype(F32) * omega
    value = jnp.where(cosine, jnp.cos(angle), jnp.sin(angle))
    value = jnp.where(jnp.where(second, 1, 0) == jnp.where(row >= POSITIONS, 1, 0), value, 0.0)
    high = low(value)
    table_ref[0 : 2 * POSITIONS, :] = high
    table_ref[2 * POSITIONS :, :] = low(value - high.astype(F32))


def row_mask(q, i, shape):
    return ((q * 16 + (iota(shape, 1) & 15) - 1) >> 1) == i


def main_kernel(dims, *refs):
    n_rows, hp, cw, tokens, ni, half_rows = dims
    own_ref, side_ref = refs[0:2]
    tiles = refs[2 : 1 + n_rows]
    rights = refs[1 + n_rows : 2 * n_rows]
    (act_ref, table_ref, pb_ref, mb_ref, qb_ref, vb_ref, ob_ref, hb_ref, rb_ref, fb_ref, lb_ref,
     pw_ref, mw_ref, fw_ref, aw_ref, ow_ref, hw_ref, rw_ref, low_ref,
     q_ref, k_ref, v_ref, da_ref, rows_ref, aux_ref, res_ref, mid_ref, in_ref, x_ref, mem_ref, turn_ref, ms_ref, vel_ref,
     item_ref, keep_ref, send_ref,
     es, ct_s, at_s, mlp_s, ha_s, dh_s, dbm_s, dba_s, ri_s, gd_s, dacc, small, g_s) = refs[2 * n_rows :]
    width = res_ref.shape[1]
    pairs = width // 128
    r = lax.axis_index("row")
    core = lax.axis_index("col") & 1
    shift = int(math.log2(hp))

    es[...] = jnp.zeros_like(es)
    es[r, LEFT : LEFT + 64, :] = own_ref[...]
    for k in range(1, n_rows):
        other = lax.rem(r - k + n_rows, n_rows)
        es[other, LEFT : LEFT + 64, :] = tiles[k - 1][...]
        es[other, LEFT + 64 :, :] = rights[k - 1][...]

    @pl.when(r == 0)
    def _():
        es[r, 0:LEFT, :] = side_ref[0:LEFT, :]

    @pl.when(r > 0)
    def _():
        es[r, LEFT + 64 :, :] = side_ref[...]

    meta = es[r, :, 256:384].astype(F32)
    lane = iota(meta.shape, 1)
    weighted = meta * jnp.where(lane == 0, 256.0, jnp.where(lane == 8, 1.0, 0.0))
    down = iota(meta.shape, 0)
    start = LEFT + r * cw
    tag_prev = jnp.sum(jnp.where(down == start - 1, weighted, 0.0)).astype(jnp.int32)
    tag_last = jnp.sum(jnp.where(down == start + cw - 1, weighted, 0.0)).astype(jnp.int32)
    tag_first = jnp.sum(jnp.where(down == start, weighted, 0.0)).astype(jnp.int32)
    strip_prev = jnp.where(tag_prev == 0, ((tag_first - 1) >> 1) - 1, (tag_prev - 1) >> 1)
    strip_last = (tag_last - 1) >> 1
    base = 2 * (strip_prev + 1)

    pick = one(iota((16, act_ref.shape[0]), 1) == base + iota((16, act_ref.shape[0]), 0))
    own_act = low(mm(pick, act_ref[...]))
    ms_ref[48:, :] = jnp.zeros_like(ms_ref[48:, :])
    for b in range(8):
        cols = slice(b * width, (b + 1) * width)
        if b < 6:
            value = mm(own_act, mw_ref[:, cols]) + line(mb_ref, b * width, width)
        else:
            value = mm(own_act, fw_ref[:, (b - 6) * width : (b - 5) * width]) + line(fb_ref, (b - 6) * width, width)
        p0 = low(value)
        rest = value - p0.astype(F32)
        p1 = low(rest)
        ms_ref[0:16, cols] = p0
        ms_ref[16:32, cols] = p1
        ms_ref[32:48, cols] = low(rest - p1.astype(F32))

    def mod(mem, b, n=1):
        return mm(mem, ms_ref[:, b * width : (b + n) * width])

    fold = lane_fold(16)
    embed = low(t_mm(fold, pw_ref[...]))
    unread = low(t_mm(low_ref[...], fold))
    b_lanes = iota((BLOCK, 128), 1)
    is_b1 = b_lanes >= 64
    half_lanes = (one(b_lanes < 64), one(is_b1))

    lanes = iota((FIRST, 128), 1)
    second_side = lanes >= 64

    def first(tb, carry):
        t0 = pl.multiple_of(tb * FIRST, FIRST)
        rows = pl.ds(t0, FIRST)
        token = t0 + iota((FIRST, 1), 0)
        j = token >> shift
        i = token & (hp - 1)
        spot = iota((FIRST, LEFT + 64 + RIGHT), 1)
        rep0 = one(spot == start + j)
        rep1 = one(spot == start + j + 1)
        x = jnp.zeros((FIRST, 128), F32)
        c = jnp.zeros((FIRST, 128), F32)
        m = jnp.zeros((FIRST, 128), F32)
        for q in range(n_rows):
            here = mm(rep0, es[q])
            beside = mm(rep1, es[q, :, 0:256])
            mask = row_mask(q, i, (FIRST, 128))
            x = x + jnp.where(mask, jnp.where(second_side, here[:, 0:128], beside[:, 0:128]), 0.0)
            c = c + jnp.where(mask, jnp.where(second_side, here[:, 128:256], beside[:, 128:256]), 0.0)
            m = m + jnp.where((q * 8 + (lanes & 7)) == i, here[:, 256:384], 0.0)
        x = low(x)
        m = low(m)
        x_ref[rows, :] = x
        ml = iota((128, 128), 0)
        mc = iota((128, 128), 1)
        kind = ml >> 3
        gather = jnp.where(
            (mc == 0) & (kind == 0), 256.0,
            jnp.where(((mc == 0) & (kind == 1)) | ((mc >= 1) & (mc <= 3) & (kind == mc + 1)), 1.0, 0.0),
        ).astype(BF16)
        cols = mm(m, gather)
        rl = iota((8, 128), 1) >> 3
        rr = iota((8, 128), 0)
        row_pick = jnp.where((rr == 6) & (rl == 0), 256.0, jnp.where((rr == 6) & (rl == 1), 1.0, 0.0)).astype(BF16)
        across = mm_t(row_pick, m)
        rows_ref[:, rows] = across
        tag_row = across[6:7, :].astype(jnp.int32)
        strip_row = (tag_row - 1) >> 1
        turn_ref[:, rows] = one(
            (tag_row - 1 - base == iota((16, FIRST), 0)) & (strip_row > strip_prev) & (strip_row <= strip_last)
        )
        tag = cols[:, 0:1]
        gap = cols[:, 3:4]
        tag_i = tag.astype(jnp.int32)
        strip = (tag_i - 1) >> 1
        owned = (strip > strip_prev) & (strip <= strip_last)
        act = jnp.where(owned, gap, 0.0)
        aux_ref[rows, :] = jnp.where(lanes == 0, tag * gap, jnp.where(lanes == 1, act, 0.0))
        item = tag_i - 1 - base
        mem = one((item == (lanes & 15)) & (lanes < 48) & owned)
        mem_ref[rows, :] = mem
        ct_s[rows, :] = low(c * act)
        p0 = cols[:, 1:2].astype(jnp.int32)
        p1 = cols[:, 2:3].astype(jnp.int32) + POSITIONS
        spot = iota((FIRST, 2 * POSITIONS), 1)
        place = one((spot == p0) | (spot == p1))
        res = (
            mm(x, embed) + line(pb_ref)
            + (mm(place, table_ref[0 : 2 * POSITIONS, :]) + mm(place, table_ref[2 * POSITIONS :, :]))
        )
        res_ref[rows, :] = res
        normed, _ = layer_norm(res)
        ab = mod(mem, 0, 2)
        attn_in = low(normed * (1.0 + ab[:, width:]) + ab[:, :width])
        in_ref[rows, :] = attn_in
        for part, ref in enumerate((q_ref, k_ref, v_ref)):
            value = mm(attn_in, aw_ref[:, part * width : (part + 1) * width])
            if part != 1:
                value = value + line(vb_ref if part else qb_ref)
            value = low(value)
            if part == 0:
                value = value * BF16(1.0 / math.sqrt(width // HEADS))
            for p in range(pairs):
                ref[p, rows, :] = value[:, p * 128 : (p + 1) * 128]
        return carry

    lax.fori_loop(0, tokens // FIRST, first, 0)

    for qb in range(tokens // BLOCK):
        qs = slice(qb * BLOCK, (qb + 1) * BLOCK)
        ks = key_range(qb, hp, tokens)
        q_tag = rows_ref[6:7, qs]
        k_tag = aux_ref[ks, 0:1]
        allowed = k_tag == q_tag
        for p in range(pairs):
            query = q_ref[p, qs, :]
            key = k_ref[p, ks, :]
            value = v_ref[p, ks, :]
            halves = []
            for e in range(2):
                scores = jnp.where(allowed, mm_t(key, query * half_lanes[e]), -1e30)
                top = jnp.max(scores, axis=0, keepdims=True)
                expo = jnp.exp(scores - top)
                total = jnp.sum(expo, axis=0, keepdims=True)
                rows_ref[2 * p + e : 2 * p + e + 1, qs] = top + jnp.log(total)
                halves.append(t_mm(low(expo * (1.0 / total)), value))
            at_s[p, qs, :] = low(jnp.where(is_b1, halves[1], halves[0]))

    dacc[...] = jnp.zeros_like(dacc)
    small[...] = jnp.zeros_like(small)

    def second(tb, carry):
        t0 = pl.multiple_of(tb * SECOND, SECOND)
        rows = pl.ds(t0, SECOND)
        mem = mem_ref[rows, :]

        turned = turn_ref[:, rows]

        def item_sum(b, grad):
            dacc[:, b * width : (b + 1) * width] += mm(turned, low(grad))

        attended = jnp.concatenate([at_s[p, rows, :] for p in range(pairs)], axis=1)
        branch_a = mm(attended, ow_ref[...]) + line(ob_ref)
        gate_a = mod(mem, 2)
        mid = res_ref[rows, :] + gate_a * branch_a
        norm_mid, inv_mid = layer_norm(mid)
        scale_m = 1.0 + mod(mem, 4)
        mlp_in = low(norm_mid * scale_m + mod(mem, 3))
        mlp_s[rows, :] = mlp_in
        hidden = hw_ref.shape[1]
        branch_m = jnp.zeros((SECOND, width), F32)
        for n in range(hidden // width):
            part = slice(n * width, (n + 1) * width)
            pre = mm(mlp_in, hw_ref[:, part]) + line(hb_ref, n * width, width)
            square = pre * pre
            c0 = math.sqrt(2.0 / math.pi)
            t = jnp.tanh(pre * (c0 + (c0 * 0.044715) * square))
            up = 0.5 + 0.5 * t
            act = low(pre * up)
            gd_s[:, part] = up + (0.5 * pre) * (1.0 - t * t) * (c0 + (3.0 * c0 * 0.044715) * square)
            ha_s[rows, part] = act
            branch_m = branch_m + mm(act, rw_ref[part, :])
        branch_m = branch_m + line(rb_ref)
        gate_m = mod(mem, 5)
        norm_out, inv_out = layer_norm(mid + gate_m * branch_m)
        scale_f = 1.0 + mod(mem, 7)
        readout_in = low(norm_out * scale_f + mod(mem, 6))
        ri_s[rows, :] = readout_in
        active = aux_ref[rows, 1:2]
        bias_lanes = mm(low(line(lb_ref) + jnp.zeros((8, 16), F32)), fold)[0:1, :]
        vel_ref[rows, :] = low((mm(readout_in, unread) + bias_lanes) * active)
        d_read = mm_t(ct_s[rows, :], unread)
        item_sum(6, d_read)
        item_sum(7, d_read * norm_out)
        d_out = norm_back(norm_out, inv_out, d_read * scale_f)
        item_sum(5, d_out * branch_m)
        d_bm = low(d_out * gate_m)
        dbm_s[rows, :] = d_bm
        small[16:17, :] += jnp.sum(d_bm.astype(F32), axis=0, keepdims=True)
        d_mlp = jnp.zeros((SECOND, width), F32)
        for n in range(hidden // width):
            part = slice(n * width, (n + 1) * width)
            d_hid = low(mm_t(d_bm, rw_ref[part, :]) * gd_s[:, part])
            dh_s[rows, part] = d_hid
            small[17 + n : 18 + n, :] += jnp.sum(d_hid.astype(F32), axis=0, keepdims=True)
            d_mlp = d_mlp + mm_t(d_hid, hw_ref[:, part])
        item_sum(3, d_mlp)
        item_sum(4, d_mlp * norm_mid)
        d_mid = d_out + norm_back(norm_mid, inv_mid, d_mlp * scale_m)
        mid_ref[rows, :] = d_mid
        item_sum(2, d_mid * branch_a)
        d_ba = low(d_mid * gate_a)
        dba_s[rows, :] = d_ba
        small[21:22, :] += jnp.sum(d_ba.astype(F32), axis=0, keepdims=True)
        d_at = low(mm_t(d_ba, ow_ref[...]))
        for p in range(pairs):
            da_ref[p, rows, :] = d_at[:, p * 128 : (p + 1) * 128]
        return carry

    lax.fori_loop(0, tokens // SECOND, second, 0, unroll=True)
    rows = [dacc[0:ni, b * width : (b + 1) * width] for b in range(2, 8)]
    spot = ((core * 2 * n_rows + plane_spot()) * (lax.axis_size("col") // 4) + line_spot()) * ni
    index = iota((4, width), 0) * width + iota((4, width), 1) - spot
    number = jnp.where((index >= 0) & (index < ni), base + index, 0)
    rows += [(number >> 8).astype(F32), (number & 255).astype(F32)]
    item_ref[...] = low(jnp.concatenate(rows, axis=0))

    g_s[...] = jnp.zeros_like(g_s)
    put = functools.partial(put_rows, g_s, half_rows)
    n_hidden = hw_ref.shape[1] // width
    for n in range(n_hidden):
        part = slice(n * width, (n + 1) * width)
        put(n * width, low(t_mm(ha_s[:, part], dbm_s[...])))
    grad = low(t_mm(mlp_s[...], dh_s[...]))
    for n in range(n_hidden):
        put((n_hidden + n) * width, grad[:, n * width : (n + 1) * width])
    attended = jnp.concatenate([at_s[p] for p in range(pairs)], axis=1)
    put(2 * n_hidden * width, low(t_mm(attended, dba_s[...])))
    ones = jnp.ones((8, tokens), BF16)
    small[0:16, :] = mm(fold, low(t_mm(ct_s[...], ri_s[...])))
    sums = mm(ones, ct_s[...])
    small[22:23, 0:128] = mm_t(jnp.broadcast_to(low(sums[0:1, :]), (8, 128)), lane_fold(128))[0:1, :]
    put((2 * n_hidden + 1) * width, low(small[...]))
    keep_ref[...] = g_s[core]
    send_ref[...] = g_s[1 - core]


def put_rows(g_s, half_rows, row, value):
    count = value.shape[0]
    done = 0
    while done < count:
        side, at = divmod(row + done, half_rows)
        take = min(count - done, half_rows - at)
        g_s[side, at : at + take, :] = value[done : done + take, :]
        done += take


def key_range(qb, hp, tokens):
    first_col = (qb * BLOCK) // hp
    last_col = ((qb + 1) * BLOCK - 1) // hp
    return slice(max(0, first_col - HALO) * hp, min(tokens, (last_col + 1 + HALO) * hp))


def attend_back_kernel(hp, first, q_ref, k_ref, v_ref, da_ref, rows_ref, aux_ref, dq_ref, dk_ref, dv_ref, dk_s, dv_s):
    tokens = q_ref.shape[1]
    b_lanes = iota((BLOCK, 128), 1)
    is_b1 = b_lanes >= 64
    half_lanes = (one(b_lanes < 64), one(is_b1))
    scale = 1.0 / math.sqrt(q_ref.shape[0] * 128 // HEADS)
    dk_s[...] = jnp.zeros_like(dk_s)
    dv_s[...] = jnp.zeros_like(dv_s)
    for qb in range(tokens // BLOCK):
        qs = slice(qb * BLOCK, (qb + 1) * BLOCK)
        ks = key_range(qb, hp, tokens)
        allowed = aux_ref[ks, 0:1] == rows_ref[6:7, qs]
        for n in range(dq_ref.shape[0]):
            p = first + n
            query = q_ref[p, qs, :]
            key = k_ref[p, ks, :]
            value = v_ref[p, ks, :]
            d_at = da_ref[p, qs, :]
            d_key = 0.0
            d_value = 0.0
            halves = []
            for e in range(2):
                q_half = query * half_lanes[e]
                d_half = d_at * half_lanes[e]
                scores = jnp.where(allowed, mm_t(key, q_half), -1e30)
                probs = jnp.exp(scores - rows_ref[2 * p + e : 2 * p + e + 1, qs])
                d_probs = mm_t(value, d_half)
                inner = jnp.sum(probs * d_probs, axis=0, keepdims=True)
                d_scores = low(probs * (d_probs - inner))
                d_value = d_value + mm(low(probs), d_half)
                d_key = d_key + mm(d_scores, q_half)
                halves.append(t_mm(d_scores, key))
            dk_s[n, ks, :] += d_key
            dv_s[n, ks, :] += d_value
            dq_ref[n, qs, :] = low(jnp.where(is_b1, halves[1], halves[0]) * scale)
    dk_ref[...] = low(dk_s[...])
    dv_ref[...] = low(dv_s[...])


def joined(refs, rows):
    return jnp.concatenate(
        [ref[n, rows, :] for kind in range(3) for ref in refs[kind::3] for n in range(ref.shape[0])], axis=1
    )


def weigh_attention(half_rows, in_ref, parts, patch, keep_ref, send_ref, small, g_s):
    tokens, width = in_ref.shape
    core = lax.axis_index("col") & 1
    put = functools.partial(put_rows, g_s, half_rows)
    ones = jnp.ones((8, tokens), BF16)
    g_s[...] = jnp.zeros_like(g_s)
    small[...] = jnp.zeros_like(small)
    small[0 : patch.shape[0], :] = patch
    whole = joined(parts, slice(None))
    for n in range(3):
        grad = whole[:, n * width : (n + 1) * width]
        put(n * width, low(t_mm(in_ref[...], grad)))
        if n != 1:
            small[17 + n // 2 : 18 + n // 2, :] = mm(ones, grad)[0:1, :]
    put(3 * width, low(small[...]))
    keep_ref[...] = g_s[core]
    send_ref[...] = g_s[1 - core]


def back_kernel(dims, *refs):
    n_rows, hp, cw, tokens, ni, half_rows = dims
    heads, done = refs[:6], refs[6:9]
    (in_ref, res_ref, mid_ref, x_ref, mem_ref, turn_ref, ms_ref, vel_ref, more_ref, aw_ref, pw_ref, keep_ref, send_ref,
     item_ref) = refs[9:23]
    frame_refs = refs[23 : 23 + n_rows]
    *rest, dk_s, dv_s, small, g_s, di_s, dacc, frame = refs[23 + n_rows :]
    parts = [*done, *rest]
    attend_back_kernel(hp, done[0].shape[0], *heads, *rest, dk_s, dv_s)
    width = res_ref.shape[1]
    r = lax.axis_index("row")
    shift = int(math.log2(hp))

    embed = low(t_mm(lane_fold(16), pw_ref[...]))
    dacc[...] = jnp.zeros_like(dacc)
    frame[...] = jnp.zeros_like(frame)

    def third(tb, carry):
        t0 = pl.multiple_of(tb * THIRD, THIRD)
        rows = pl.ds(t0, THIRD)
        mem = mem_ref[rows, :]
        d_attn = mm_t(joined(parts, rows), aw_ref[...])
        normed, inverse = layer_norm(res_ref[rows, :])
        scale_a = 1.0 + mm(mem, ms_ref[:, width : 2 * width])
        turned = turn_ref[:, rows]
        dacc[:, 0:width] += mm(turned, low(d_attn))
        dacc[:, width : 2 * width] += mm(turned, low(d_attn * normed))
        d_in = low(mid_ref[rows, :] + norm_back(normed, inverse, d_attn * scale_a))
        di_s[rows, :] = d_in
        grad = low(mm_t(d_in, embed))
        both = jnp.concatenate([vel_ref[rows, :], grad], axis=1)
        token = t0 + iota((THIRD, 1), 0)
        j = token >> shift
        i = token & (hp - 1)
        spot = iota((THIRD, 64 + RIGHT), 1)
        rep = jnp.concatenate([one(spot == r * cw + j), one(spot == r * cw + j + 1)], axis=0)
        side = (iota((THIRD, 256), 1) >> 6) & 1
        for q in range(n_rows):
            mask = row_mask(q, i, (THIRD, 256))
            split = jnp.concatenate([both * one(mask & (side == 1)), both * one(mask & (side == 0))], axis=0)
            frame[q] += t_mm(rep, split)
        return carry

    lax.fori_loop(0, tokens // THIRD, third, 0)

    ones = jnp.ones((8, tokens), BF16)
    rows = [dacc[0:ni, 0:width], dacc[0:ni, width : 2 * width]]
    rows += [more_ref[...].astype(F32)]
    item_ref[...] = low(jnp.concatenate(rows, axis=0))
    patch = jnp.concatenate([mm(lane_fold(16), low(t_mm(x_ref[...], di_s[...]))), mm(ones, di_s[...])[0:1, :]], axis=0)
    weigh_attention(half_rows, in_ref, parts, patch, keep_ref, send_ref, small, g_s)
    for k in range(n_rows):
        q = lax.rem(r + k, n_rows)
        frame_refs[k][...] = low(frame[q])


def frame_kernel(*refs):
    *ins, mine_ref, over_ref = refs
    total = ins[0][...].astype(F32)
    for ref in ins[1:]:
        total = total + ref[...].astype(F32)
    mine_ref[...] = low(total[0:64])
    over_ref[...] = low(total[64:])


def canvas_kernel(mine_ref, over_ref, vel_ref, grad_ref):
    extra = jnp.concatenate([over_ref[...].astype(F32), jnp.zeros((64 - RIGHT, 256), F32)], axis=0)
    total = low(mine_ref[...].astype(F32) + extra)
    for n, ref in enumerate((vel_ref, grad_ref)):
        value = 0.0
        for side in (0, 1):
            pick = one(iota((64, 128), 1) == 2 * iota((64, 128), 0) + side)
            value = value + t_mm(total[:, n * 128 + side * 64 : n * 128 + (side + 1) * 64], pick)
        ref[...] = value.reshape(ref.shape).astype(ref.dtype)


def add_kernel(count, me, *refs):
    outs = refs[len(refs) - count :]
    ins = refs[: len(refs) - count]
    spot = me()
    for m, out in enumerate(outs):
        at = jnp.bitwise_xor(spot, m) if count > 1 else 0
        total = ins[0][at].astype(F32)
        for ref in ins[1:]:
            total = total + ref[at].astype(F32)
        out[...] = low(total)


def plane_spot():
    return lax.axis_index("row") + lax.axis_size("row") * ((lax.axis_index("col") >> 1) & 1)


def line_spot():
    return lax.axis_index("col") >> 2


def send(value, n_rows, n_cols, flip_row=0, flip_col=0):
    route = [
        (i * n_cols + j, (i ^ flip_row) * n_cols + (j ^ flip_col)) for i in range(n_rows) for j in range(n_cols)
    ]
    return lax.ppermute(value, ("row", "col"), route)


def add_up(arrays, count, me, after=()):
    n, w = arrays[0].shape
    ins = [a.reshape(count, n // count, w) for a in arrays]
    return call(
        functools.partial(add_kernel, count, me), [((n // count, w), BF16)] * count, ins, after=after,
        near_in=range(len(ins)), near_out=range(count),
    )


def add_with_kernel(count, me, *refs):
    outs = refs[len(refs) - count :]
    *ins, more = refs[: len(refs) - count]
    spot = me()
    for m, out in enumerate(outs):
        at = jnp.bitwise_xor(spot, m)
        total = ins[0][at].astype(F32)
        for ref in ins[1:]:
            total = total + ref[at].astype(F32)
        out[0 : total.shape[0], :] = low(total)
        if m:
            out[total.shape[0] :, :] = more[...]


def add_tops_kernel(*refs):
    *ins, out = refs
    total = ins[0][...].astype(F32)
    for ref in ins[1:]:
        total = total + ref[0 : out.shape[0], :].astype(F32)
    out[...] = low(total)


def list_ends_kernel(*refs):
    own_ref, *ins, out = refs
    out[0] = own_ref[...]
    for m, ref in enumerate(ins):
        out[m + 1] = ref[ref.shape[0] - own_ref.shape[0] :, :]


def add_below_kernel(*refs):
    *ins, first, out = refs
    total = ins[0][...].astype(F32)
    for ref in ins[1:]:
        total = total + ref[...].astype(F32)
    out[0 : first.shape[0], :] = first[...]
    out[first.shape[0] :, :] = low(total)


def line_kernel(share, *refs):
    *ins, out, rows = refs
    spot = line_spot()
    for m, ref in enumerate(ins):
        out[m * share : (m + 1) * share, :] = ref[0:share, :]
        rows[jnp.bitwise_xor(spot, m)] = ref[share:, :].astype(F32)
    out[len(ins) * share :, :] = low(jnp.sum(rows[...], axis=0))


def copy_kernel(in_ref, out_ref):
    out_ref[...] = in_ref[...]


def to_plane(parts, n_rows, n_cols):
    return [
        send(parts[m], n_rows, n_cols, flip_row=m % n_rows, flip_col=2 * (m // n_rows)) for m in range(1, 2 * n_rows)
    ]


def to_line(parts, n_rows, n_cols):
    return [send(parts[m], n_rows, n_cols, flip_col=4 * m) for m in range(1, n_cols // 4)]


def stack_kernel(*refs):
    *ins, out = refs
    for n, ref in enumerate(ins):
        out[n] = ref[...]


def stack(arrays, after=()):
    return call(
        stack_kernel, [((len(arrays), *arrays[0].shape), BF16)], arrays, after=after, near_in=range(len(arrays)),
        near_out=(0,),
    )[0]


def for_planes(n_rows, body):
    core = lax.axis_index("col") & 1
    plane = plane_spot()
    for c in range(2):

        def step(m, carry, c=c):
            body(c, m, jnp.bitwise_xor(core, c) * 2 * n_rows + jnp.bitwise_xor(plane, m))
            return carry

        lax.fori_loop(0, 2 * n_rows, step, 0)


def for_parts(n_rows, n_cols, body):
    line = line_spot()

    def inner(c, m, at):
        for n in range(n_cols // 4):
            body(c, m, n, at * (n_cols // 4) + jnp.bitwise_xor(line, n))

    for_planes(n_rows, inner)


def weights_kernel(mesh_shape, *refs):
    n_rows, n_cols = mesh_shape
    blocks = refs[: 4 * n_rows]
    (ret_ref, hid_ref, out_ref, read_ref, rb_ref, hb_ref, ob_ref, lb_ref, att_ref, patch_ref, pb_ref, qb_ref, vb_ref,
     first, second) = refs[4 * n_rows :]
    share = first.shape[1]
    core = lax.axis_index("col") & 1
    plane, line = plane_spot(), line_spot()
    lines = n_cols // 4
    for n, ref in enumerate(blocks):
        c, m = divmod(n, 2 * n_rows)
        at = jnp.bitwise_xor(core, c) * 2 * n_rows + jnp.bitwise_xor(plane, m)
        for k in range(lines):
            first[at * lines + jnp.bitwise_xor(line, k)] = ref[k * share : (k + 1) * share, :].astype(F32)
        second[at] = ref[lines * share :, :].astype(F32)
    flat = first[...].reshape(first.shape[0] * share, first.shape[2])
    width = flat.shape[1]
    hidden = ret_ref.shape[0]
    ret_ref[...] = flat[0:hidden]
    for n in range(hidden // width):
        hid_ref[:, n * width : (n + 1) * width] = flat[hidden + n * width : hidden + (n + 1) * width]
    out_ref[...] = flat[2 * hidden : 2 * hidden + width]
    at = 2 * hidden + width
    small = flat[at : at + 24]
    read_ref[...] = small[0:16]
    rb_ref[...] = small[16]
    for n in range(hidden // width):
        hb_ref[n * width : (n + 1) * width] = small[17 + n]
    ob_ref[...] = small[21]
    lb_ref[...] = small[22, 0:16]
    flat = second[...].reshape(second.shape[0] * second.shape[1], width)
    for n in range(3):
        att_ref[:, n * width : (n + 1) * width] = flat[n * width : (n + 1) * width]
    small = flat[3 * width : 3 * width + 24]
    patch_ref[...] = small[0:16]
    pb_ref[...] = small[16]
    qb_ref[...] = small[17]
    vb_ref[...] = small[18]


def condition_kernel(
    mesh_shape, ni, own_ref, other_ref, tl_ref, feat_ref, pre_ref, cond_ref, act_ref, mw_ref, fw_ref, cw_ref,
    mod_ref, fin_ref, table_ref, clock_ref, time_ref, mb_ref, fb_ref, cb_ref, tb_ref,
    dev_s, ids_s,
):
    n_rows, n_cols = mesh_shape
    width = cw_ref.shape[0]
    items = tl_ref.shape[1]
    count = n_rows * n_cols
    ids_s[...] = jnp.zeros_like(ids_s)

    def place(c, m, n, at):
        part = (own_ref, other_ref)[c][m, n].astype(F32)
        for b in range(8):
            dev_s[b, at] = part[b * ni : (b + 1) * ni]
        ids_s[...] += part[8 * ni :]

    for_parts(n_rows, n_cols, place)
    ids = ids_s[...]
    numbers = ids[0:4] * 256.0 + ids[4:8]
    number = jnp.concatenate([numbers[k : k + 1, :] for k in range(-(-count * ni // width))], axis=1)[:, : count * ni]
    pick = one(iota((items, count * ni), 0).astype(F32) == number)
    ones = jnp.ones((8, items), BF16)
    act = act_ref[...]
    d_cond = jnp.zeros((items, width), F32)
    for b in range(8):
        grad = low(mm(pick, low(dev_s[b].reshape(count * ni, width))))
        total = mm(ones, grad)[0]
        if b < 6:
            cols = slice(b * width, (b + 1) * width)
            mb_ref[cols] = total
            mod_ref[:, cols] = t_mm(act, grad)
            d_cond = d_cond + mm_t(grad, mw_ref[:, cols])
        else:
            cols = slice((b - 6) * width, (b - 5) * width)
            fb_ref[cols] = total
            fin_ref[:, cols] = t_mm(act, grad)
            d_cond = d_cond + mm_t(grad, fw_ref[:, cols])
    cond = cond_ref[...]
    sigma = sigmoid(cond)
    d_cond = low(d_cond * (sigma * (1.0 + cond * (1.0 - sigma))))
    pre = pre_ref[...]
    sigma = sigmoid(pre)
    hidden = low(pre * sigma)
    classes = table_ref.shape[0]
    table_ref[...] = mm(one(iota((classes, items), 0) == tl_ref[1:2, :]), d_cond)
    clock_ref[...] = t_mm(hidden, d_cond)
    cb_ref[...] = mm(ones, d_cond)[0]
    d_time = low(mm_t(d_cond, cw_ref[...]) * (sigma * (1.0 + pre * (1.0 - sigma))))
    time_ref[...] = mm(feat_ref[...], d_time)
    tb_ref[...] = mm(ones, d_time)[0]


def local(
    latent, cotangent, item_ids, positions, gap_mask, timesteps, labels, patch_weight, patch_bias, time_weight,
    time_bias, clock_weight, clock_bias, class_table, modulation_weight, modulation_bias, attention_weight, query_bias,
    value_bias, output_weight, output_bias, hidden_weight, hidden_bias, return_weight, return_bias, final_modulation,
    final_offsets, readout_weight, readout_bias,
):
    n_rows, n_cols = lax.axis_size("row"), lax.axis_size("col")
    row_count, col_count = item_ids.shape
    width = patch_weight.shape[1]
    hidden = hidden_weight.shape[1]
    hp = n_rows * row_count
    cw = col_count // n_rows
    tokens = (cw + HALO) * hp
    ni = 2 * (-(-cw // LEAST))
    items = -(-(timesteps.shape[0] + 16) // 32) * 32
    unit = 8 * n_rows * n_cols
    rows_1 = -(-(2 * hidden + width + 128) // unit) * unit
    rows_2 = -(-(3 * width + 128) // unit) * unit
    pairs = width // 128
    near = int(tokens <= 1024)

    tile, first_cols, side_cols = call(
        tile_kernel,
        [((col_count, 384), BF16), ((RIGHT, 384), BF16), ((RIGHT, 384), BF16)],
        [latent, cotangent, item_ids, positions, gap_mask],
        far_in=range(5), near_out=range(3),
    )

    def shift(value, step_row, step_col, wanted):
        route = [
            (i * n_cols + j, (i + step_row) % n_rows * n_cols + j + step_col)
            for i in range(n_rows)
            for j in range(n_cols)
            if 0 <= j + step_col < n_cols and wanted((i + step_row) % n_rows)
        ]
        return lax.ppermute(value, ("row", "col"), route)

    def needs_right(i):
        return (i + 1) * cw + HALO + 1 > col_count

    tiles = [shift(tile, k, 0, lambda i: True) for k in range(1, n_rows)]
    rights = [shift(first_cols, k, -1, needs_right) for k in range(1, n_rows)]
    route = [(j, j + 1) for j in range(n_cols - 1)]
    route += [
        (i * n_cols + j, i * n_cols + j - 1) for i in range(1, n_rows) if needs_right(i) for j in range(1, n_cols)
    ]
    side = lax.ppermute(side_cols, ("row", "col"), route)

    tl, feat, time_pre, condition, cond_act, table = call(
        item_kernel,
        [((8, items), jnp.int32), ((time_weight.shape[0], items), BF16), ((items, width), F32), ((items, width), F32),
         ((items, width), BF16), ((4 * POSITIONS, width), BF16)],
        [timesteps, labels, time_weight, time_bias, clock_weight, clock_bias, class_table],
        us=5,
    )

    dims = (n_rows, hp, cw, tokens, ni, rows_1 // 2)
    heads = ((pairs, tokens, 128), BF16)
    ins = [tile, side, *tiles, *rights, cond_act, table, patch_bias, modulation_bias, query_bias, value_bias, output_bias,
           hidden_bias, return_bias, final_offsets, readout_bias, patch_weight, modulation_weight, final_modulation,
           attention_weight, output_weight, hidden_weight, return_weight, readout_weight.T]
    q, k, v, d_at, rows, aux, res, mid, attn_in, patches, member, turned, spread, spoken, item_main, keep, out = call(
        functools.partial(main_kernel, dims),
        [heads, heads, heads, heads, ((8, tokens), F32), ((tokens, 128), F32), ((tokens, width), F32),
         ((tokens, width), F32), ((tokens, width), BF16), ((tokens, 128), BF16), ((tokens, 128), BF16),
         ((16, tokens), BF16), ((128, 8 * width), BF16), ((tokens, 128), BF16), ((6 * ni + 8, width), BF16),
         ((rows_1 // 2, width), BF16), ((rows_1 // 2, width), BF16)],
        ins,
        [((n_rows, LEFT + 64 + RIGHT, 384), BF16), ((tokens, 128), BF16), ((pairs, tokens, 128), BF16),
         ((tokens, width), BF16), ((tokens, hidden), BF16), ((tokens, hidden), BF16), ((tokens, width), BF16),
         ((tokens, width), BF16), ((tokens, width), BF16), ((SECOND, hidden), F32), ((16, 8 * width), F32),
         ((128, width), F32), ((2, rows_1 // 2, width), BF16)],
        us=30, room=36 if near else 60, near_out=range(17 * near), near_in=range(len(ins) * near),
    )
    shape = (n_rows, n_cols)
    lines = n_cols // 4
    got = send(out, *shape, flip_col=1)

    part = ((1, tokens, 128), BF16)
    total = ((1, tokens, 128), F32)
    d_first = call(
        functools.partial(attend_back_kernel, hp, 0), [part] * 3, [q, k, v, d_at, rows, aux], [total] * 2,
        us=4, room=24 if near else 60, near_in=range(6 * near), near_out=range(3 * near),
    )
    parts = add_up([keep, got], 2 * n_rows, plane_spot, after=[d_first[0]])
    got = to_plane(parts, *shape)
    dims = (n_rows, hp, cw, tokens, ni, rows_2 // 2)
    part = ((pairs - 1, tokens, 128), BF16)
    total = ((pairs - 1, tokens, 128), F32)
    result = call(
        functools.partial(back_kernel, dims),
        [((rows_2 // 2, width), BF16)] * 2 + [((8 * ni + 8, width), BF16)]
        + [((64 + RIGHT, 256), BF16)] * n_rows,
        [q, k, v, d_at, rows, aux, *d_first, attn_in, res, mid, patches, member, turned, spread, spoken,
         item_main, attention_weight, patch_weight],
        [part] * 3 + [total] * 2 + [((128, width), F32), ((2, rows_2 // 2, width), BF16)]
        + [((tokens, width), BF16), ((16, 2 * width), F32), ((n_rows, 64 + RIGHT, 256), F32)],
        us=14, after=[parts[0]], room=32 if near else 60, near_in=range(18 * near),
        near_out=range((3 + n_rows) * near),
    )
    keep_2, out_2, items_own = result[:3]
    got_2 = send(out_2, *shape, flip_col=1)
    frames = result[3:]
    share_1 = rows_1 // (n_rows * n_cols)
    share_2 = rows_2 // (4 * n_rows)

    count = items_own.shape[0]
    ins = [a.reshape(lines, share_1, width) for a in (parts[0], *got)]
    parts = call(
        functools.partial(add_with_kernel, lines, line_spot),
        [((share_1 + (count if m else 0), width), BF16) for m in range(lines)], [*ins, items_own],
        near_in=range(len(ins) + 1), near_out=range(lines),
    )
    got = to_line(parts, *shape)
    parts_2 = add_up([keep_2, got_2], 2 * n_rows, plane_spot, after=[parts[0]])
    got_2 = to_plane(parts_2, *shape)
    (part,) = call(
        add_tops_kernel, [((share_1, width), BF16)], [parts[0], *got], near_in=range(lines), near_out=(0,),
        after=[parts_2[0]],
    )
    ins = [parts_2[0], *got_2, part]
    (both,) = call(
        add_below_kernel, [((share_1 + share_2, width), BF16)], ins, near_in=range(len(ins)), near_out=(0,),
    )
    got_both = to_line([both] * lines, *shape)
    (block_items,) = call(
        list_ends_kernel, [((lines, count, width), BF16)], [items_own, *got], near_in=range(lines), near_out=(0,),
        after=[both],
    )
    plane_items = to_plane([block_items] * (2 * n_rows), *shape)

    frames = [
        call(copy_kernel, [(a.shape, BF16)], [a], near_in=(0,), near_out=(0,), after=[both])[0] if k else a
        for k, a in enumerate(frames)
    ]
    frames = [frames[0]] + [shift(frames[k], k, 0, lambda i: True) for k in range(1, n_rows)]
    mine, over = call(
        frame_kernel, [((64, 256), BF16), ((RIGHT, 256), BF16)], frames, near_in=range(n_rows), near_out=(0, 1),
    )
    velocity, latent_grad = call(
        canvas_kernel, [(latent.shape, BF16), (latent.shape, F32)], [mine, shift(over, 0, 1, lambda i: True)],
        near_in=(0, 1),
    )
    (block,) = call(
        functools.partial(line_kernel, share_1), [((lines * share_1 + share_2, width), BF16)], [both, *got_both],
        [((lines, share_2, width), F32)], near_in=range(lines), near_out=(0,), after=[velocity],
    )
    plane_block = to_plane([block] * (2 * n_rows), *shape)
    blocks_items = stack([block_items] + plane_items, after=[block])
    blocks_items = blocks_items, send(blocks_items, *shape, flip_col=1)
    devices = n_rows * n_cols
    vector = ((width,), F32)
    modulation_grad, final_grad, table_grad, clock_grad, time_grad, modulation_b, final_b, clock_b, time_b = call(
        functools.partial(condition_kernel, shape, ni),
        [((width, 6 * width), F32), ((width, 2 * width), F32), (class_table.shape, F32), ((width, width), F32),
         (time_weight.shape, F32), ((6 * width,), F32), ((2 * width,), F32), vector, vector],
        [*blocks_items, tl, feat, time_pre, condition, cond_act, modulation_weight, final_modulation, clock_weight],
        [((8, devices, ni, width), F32), ((8, width), F32)],
        us=8, room=40, near_in=range(2),
    )
    blocks = [block] + [
        call(copy_kernel, [(a.shape, BF16)], [a], near_in=(0,), near_out=(0,), after=[time_b])[0] for a in plane_block
    ]
    blocks += [send(b, *shape, flip_col=1) for b in blocks]
    (return_grad, hidden_grad, output_grad, readout_grad, return_b, hidden_b, output_b, readout_b, attention_grad, patch_grad,
     patch_b, query_b, value_b) = call(
        functools.partial(weights_kernel, shape),
        [((hidden, width), F32), ((width, hidden), F32), ((width, width), F32), ((16, width), F32), vector,
         ((hidden,), F32), vector, ((16,), F32), ((width, 3 * width), F32), ((16, width), F32), vector, vector, vector],
        blocks,
        [((devices, share_1, width), F32), ((4 * n_rows, share_2, width), F32)],
        us=4, room=36, near_in=range(len(blocks)), after=[time_b],
    )
    return (
        velocity, latent_grad, patch_grad, patch_b, time_grad, time_b, clock_grad, clock_b, table_grad, modulation_grad,
        modulation_b, attention_grad, query_b, value_b, output_grad, output_b, hidden_grad, hidden_b, return_grad,
        return_b, final_grad, final_b, readout_grad.T, readout_b,
    )


def solution(mesh):
    canvas, grid = P(None, "row", "col"), P("row", "col")
    return jax.shard_map(
        local,
        mesh=mesh,
        in_specs=(canvas, canvas, grid, canvas, grid) + (P(),) * 24,
        out_specs=(canvas, canvas) + (P(),) * 22,
        check_vma=False,
    )
```
